32 devices in a mesh: dp: 16 (over z, y, x), chan: 2 (over core).
Axes of the slice: x: 2, y: 2, z: 4, core: 2. Of those that a mesh axis runs over, the one named last changes fastest.
Arguments:
- features: bfloat16 [24576, 2048], P('dp', 'chan'), may hold values from -6 to 6
- boxes: int32 [48, 2, 4], P('dp'), may hold values from 0 to 22, as said below
- w_branch: bfloat16 [4, 2048, 512], P(None, 'chan'), may hold values from -0.125 to 0.125
- gain_branch: float32 [4, 512], P(None, 'chan'), may hold values from 0.5 to 1.5
- bias_branch: float32 [4, 512], P(None, 'chan'), may hold values from -3 to 3
- w_fx: bfloat16 [9, 2048, 512], P(None, 'chan'), may hold values from -0.03125 to 0.03125
- w_fb: bfloat16 [9, 4, 512, 512], P(None, None, 'chan'), may hold values from -0.03125 to 0.03125
- gain_join: float32 [512], replicated, may hold values from 0.5 to 1.5
- bias_join: float32 [512], replicated, may hold values from -3 to 3
- w_cls: bfloat16 [512, 150], replicated, may hold values from -0.25 to 0.25
- b_cls: float32 [150], replicated, may hold values from -4 to 4
- grad_logits: bfloat16 [24576, 150], P('dp'), may hold values from -6 to 6
Outputs:
- logits: bfloat16 [24576, 150], P('dp')
- grad_features: bfloat16 [24576, 2048], P('dp', 'chan')
- grad_w_branch: float32 [4, 2048, 512], P(None, 'chan', 'dp')
- grad_gain_branch: float32 [4, 512], P(None, 'chan')
- grad_bias_branch: float32 [4, 512], P(None, 'chan')
- grad_w_fx: float32 [9, 2048, 512], P(None, 'chan', 'dp')
- grad_w_fb: float32 [9, 4, 512, 512], P(None, None, 'chan', 'dp')
- grad_gain_join: float32 [512], replicated
- grad_bias_join: float32 [512], replicated
- grad_w_cls: float32 [512, 150], replicated
- grad_b_cls: float32 [150], replicated
The draws below stay inside these ranges and needn't reach their ends.
Inputs may be any that keep to these rules, and one draw needn't show every extreme that they name: Each canvas holds 2 disjoint boxes (top, left, height, width) inside the 16 x 32 canvas, side by side; heights at least 8, widths at least 10; the rest is padding.
All inputs are finite; a program needn't handle non-finite values.
Results may differ from the reference program's by a relative error of at most 0.017.
Values may be sent and summed in bfloat16 or wider, within the bound.
A program may use at most 320 MiB of HBM per device.

```python
import jax
import jax.numpy as jnp
from jax import lax

CIN = 2048
BR = 512
MID = 512
NCLS = 150
CH = 16
CW = 32
CANVASES = 48
PIX = 24576


def draw_boxes(key, part):
    key = jax.random.fold_in(key, 5)
    key_width, key_height, key_top, key_pick = jax.random.split(key, 4)
    widths = jax.random.randint(key_width, (CANVASES,), 10, CW - 9)
    chosen = jax.random.randint(key_pick, (), 0, CANVASES)
    widths = widths.at[chosen].set(10)
    heights = jax.random.randint(key_height, (CANVASES, 2), 8, CH + 1)
    tops = jax.random.randint(key_top, (CANVASES, 2), 0, CH - heights + 1)
    zeros_col = jnp.zeros((CANVASES,), jnp.int32)
    first = jnp.stack([tops[:, 0], zeros_col, heights[:, 0], widths], -1)
    second = jnp.stack([tops[:, 1], widths, heights[:, 1], CW - widths], -1)
    return jnp.stack([first, second], 1).astype(jnp.int32)


def block_levels(stream_key, shape, cuts, low, top_value):
    loudness = 1.0
    for axis_at, shards_of in cuts:
        steps = jax.random.uniform(jax.random.fold_in(jax.random.fold_in(stream_key, 6), axis_at), (shards_of,), jnp.float32, low / len(cuts), top_value / len(cuts))
        loudness = loudness * jnp.repeat(jnp.exp(steps), shape[axis_at] // shards_of).reshape((-1,) + (1,) * (len(shape) - 1 - axis_at))
    return loudness


def scatter_about(own_key, dims, scale, reach, shards=(), kind=jnp.bfloat16):
    factor_of = block_levels(own_key, dims, shards, -0.22, 0.18) if shards else 1.0
    array = jax.random.normal(own_key, dims, jnp.float32) * scale * factor_of
    return jnp.minimum(jnp.maximum(array, -reach), reach).astype(kind)


def setup_inputs(seed: int = 0) -> dict:
    splits = jax.random.split(jax.random.key(seed), 13)
    return {
        "features": scatter_about(splits[0], (PIX, CIN), 1.0, 6.0, ((0, 16), (1, 2))),
        "boxes": draw_boxes(jax.random.fold_in(splits[12], 71), 0),
        "w_branch": scatter_about(splits[2], (4, CIN, BR), CIN ** -0.5, 0.125, ((1, 2),)),
        "gain_branch": jnp.clip(0.5 + 1.0 * jax.random.uniform(splits[3], (4, BR), jnp.float32) ** block_levels(splits[3], (4, BR), ((1, 2),), -0.2, 0.2), 0.5, 1.5),
        "bias_branch": scatter_about(splits[4], (4, BR), 0.5, 3.0, ((1, 2),), jnp.float32),
        "w_fx": scatter_about(splits[5], (9, CIN, MID), (9 * (CIN + 4 * BR)) ** -0.5, 0.03125, ((1, 2),)),
        "w_fb": scatter_about(splits[6], (9, 4, BR, MID), (9 * (CIN + 4 * BR)) ** -0.5, 0.03125, ((2, 2),)),
        "gain_join": jnp.clip(jax.random.uniform(splits[7], (MID,), jnp.float32, 0.5, 1.5), 0.5, 1.5),
        "bias_join": scatter_about(splits[8], (MID,), 0.5, 3.0, (), jnp.float32),
        "w_cls": scatter_about(splits[9], (MID, NCLS), MID ** -0.5, 0.25),
        "b_cls": scatter_about(splits[10], (NCLS,), 1.0, 4.0, (), jnp.float32),
        "grad_logits": scatter_about(splits[11], (PIX, NCLS), 1.0, 6.0, ((0, 16),)),
    }


EPS = 1e-05
BINS = (1, 2, 3, 6)
HIGH = lax.Precision.HIGHEST

@jax.custom_vjp
def low(v):
    return lax.optimization_barrier(v.astype(jnp.bfloat16)).astype(jnp.float32)

@jax.custom_vjp
def low_back(v):
    return v

def low_keep(v):
    return (low(v), None)

def low_pass(kept, grad):
    return (grad,)

def back_keep(v):
    return (v, None)

def back_low(kept, grad):
    return (low(grad),)
low.defvjp(low_keep, low_pass)
low_back.defvjp(back_keep, back_low)

def box_tables(boxes):
    canv_count = boxes.shape[0]
    box_count = boxes.shape[1]
    places = jnp.arange(CH * CW, dtype=jnp.int32)
    place_y = places // CW
    place_x = places % CW
    top_edge = boxes[:, :, 0][:, :, None]
    left_edge = boxes[:, :, 1][:, :, None]
    height = boxes[:, :, 2][:, :, None]
    width = boxes[:, :, 3][:, :, None]
    rel_y = place_y[None, None, :] - top_edge
    rel_x = place_x[None, None, :] - left_edge
    inside = (rel_y >= 0) & (rel_y < height) & (rel_x >= 0) & (rel_x < width)
    box_ids = jnp.arange(box_count, dtype=jnp.int32)[None, :, None]
    labels = lax.optimization_barrier(jnp.max(jnp.where(inside, box_ids, -1), axis=1))
    pools, counts, lifts = ([], [], [])
    for grid_size in BINS:
        cell_ids = jnp.arange(grid_size, dtype=jnp.int32)

        def member(relative, extent):
            start = cell_ids[None, None, :] * extent // grid_size
            stop = ((cell_ids[None, None, :] + 1) * extent + grid_size - 1) // grid_size
            inbin = (relative[:, :, None, :] >= start[..., None]) & (relative[:, :, None, :] < stop[..., None])
            return (inbin, stop - start)

        def weights(relative, extent):
            numer = jnp.clip(relative, 0, extent - 1) * (grid_size - 1)
            denom = extent - 1
            low_cell = numer // denom
            frac = (numer - low_cell * denom).astype(jnp.float32) / denom.astype(jnp.float32)
            high_cell = jnp.minimum(low_cell + 1, grid_size - 1)
            first = (cell_ids == low_cell[..., None]).astype(jnp.float32) * (1.0 - frac)[..., None]
            second = (cell_ids == high_cell[..., None]).astype(jnp.float32) * frac[..., None]
            return first + second
        in_rows, len_rows = member(rel_y, height)
        in_cols, len_cols = member(rel_x, width)
        select = inside[:, :, None, None, :] & in_rows[:, :, :, None, :] & in_cols[:, :, None, :, :]
        pools.append(select.reshape(canv_count, box_count * grid_size * grid_size, CH * CW).astype(jnp.float32))
        counts.append((len_rows[:, :, :, None] * len_cols[:, :, None, :]).reshape(canv_count, -1).astype(jnp.float32))
        row_wts = weights(rel_y, height)
        col_wts = weights(rel_x, width)
        lifted = inside.astype(jnp.float32)[..., None, None] * row_wts[..., :, None] * col_wts[..., None, :]
        lifted = jnp.transpose(lifted, (0, 2, 1, 3, 4)).reshape(canv_count, CH * CW, box_count * grid_size * grid_size)
        lifts.append(lifted)
    return (labels, pools, counts, lifts)

def near_masks(labels):
    canv_count = labels.shape[0]
    label_grid = labels.reshape(canv_count, CH, CW)
    padded = jnp.pad(label_grid, ((0, 0), (1, 1), (1, 1)), constant_values=-2)
    result = []
    for offset in range(9):
        row_off, col_off = (offset // 3, offset % 3)
        nearby = padded[:, row_off:row_off + CH, col_off:col_off + CW]
        result.append(((nearby == label_grid) & (label_grid >= 0)).reshape(canv_count, CH * CW))
    return jnp.stack(result, -1).astype(jnp.float32)

def shift_in(values, offset, canv_count):
    depth = values.shape[-1]
    grid = values.reshape(canv_count, CH, CW, depth)
    padded = jnp.pad(grid, ((0, 0), (1, 1), (1, 1), (0, 0)))
    row_off, col_off = (offset // 3, offset % 3)
    return padded[:, row_off:row_off + CH, col_off:col_off + CW, :].reshape(canv_count * CH * CW, depth)

def join_canvas(masked_one, mask_one, wfx, terms_one, lifts_one):
    total = jnp.zeros((CH * CW, wfx.shape[-1]), jnp.float32)
    for offset in range(9):
        gate = mask_one[:, offset:offset + 1]
        moved = shift_in(masked_one, offset, 1) * gate
        branch_pix = jnp.zeros((CH * CW, wfx.shape[-1]), jnp.float32)
        for level in range(4):
            branch_pix = branch_pix + jnp.dot(lifts_one[level], terms_one[level][offset], precision=HIGH, preferred_element_type=jnp.float32)
        total = total + jnp.dot(moved, wfx[offset], precision=HIGH, preferred_element_type=jnp.float32)
        total = total + shift_in(branch_pix, offset, 1) * gate
    return total

def reference(features, boxes, w_branch, gain_branch, bias_branch, w_fx, w_fb, gain_join, bias_join, w_cls, b_cls, grad_logits):
    labels, pools, counts, lifts = box_tables(boxes)
    valid = (labels >= 0).astype(jnp.float32)
    masks = near_masks(labels)
    canv_count = boxes.shape[0]
    checked = jax.checkpoint(join_canvas)

    def forward(feats, wbranch, gbranch, bbranch, wfx, wfb, gfuse, bfuse, wcls, bcls):
        grid = feats.reshape(canv_count, CH * CW, CIN)
        terms = []
        for level in range(4):
            pooled = low(jnp.einsum('ncp,npd->ncd', pools[level], grid, precision=HIGH) / counts[level][..., None])
            branch = low_back(jnp.einsum('ncd,de->nce', pooled, wbranch[level], precision=HIGH))
            average = lax.optimization_barrier(jnp.mean(branch, axis=(0, 1)))
            variance = lax.optimization_barrier(jnp.mean((branch - average) ** 2, axis=(0, 1)))
            activ = gbranch[level] * (branch - average) * lax.rsqrt(variance + EPS) + bbranch[level]
            spread = low(jax.nn.silu(activ))
            terms.append(low_back(jnp.einsum('ncb,dbm->ndcm', spread, wfb[:, level], precision=HIGH)))
        masked = grid * valid[..., None]
        joined = lax.map(lambda ins: checked(ins[0], ins[1], wfx, ins[2], ins[3]), (masked, masks, tuple(terms), tuple(lifts)))
        joined = low_back(joined)
        count_valid = jnp.sum(valid)
        average = lax.optimization_barrier(jnp.sum(joined * valid[..., None], axis=(0, 1))) / count_valid
        variance = lax.optimization_barrier(jnp.sum(valid[..., None] * (joined - average) ** 2, axis=(0, 1))) / count_valid
        normed = (joined - average) * lax.rsqrt(variance + EPS)
        hidden = low(jax.nn.silu(gfuse * normed + bfuse) * valid[..., None])
        scores = jnp.einsum('npm,mk->npk', hidden, wcls, precision=HIGH) + bcls
        return scores.reshape(canv_count * CH * CW, NCLS)
    primals = tuple((arr.astype(jnp.float32) for arr in (features, w_branch, gain_branch, bias_branch, w_fx, w_fb, gain_join, bias_join, w_cls, b_cls)))
    scores, pullback = jax.vjp(forward, *primals)
    grads = pullback(grad_logits.astype(jnp.float32))
    return (scores.astype(jnp.bfloat16), grads[0].astype(jnp.bfloat16), grads[1], grads[2], grads[3], grads[4], grads[5], grads[6], grads[7], grads[8], grads[9])
```

```python
import functools

import jax
import jax.numpy as jnp
import numpy as np
from jax import lax
from jax.experimental import pallas as pl
from jax.experimental.pallas import tpu as pltpu
from jax.sharding import PartitionSpec as P

CH = 16
CW = 32
PX = CH * CW
EPS = 1e-05
BINS = (1, 2, 3, 6)
CELLS = 128
PLANE = 4
F32 = jnp.float32
BF16 = jnp.bfloat16
MESH = pl.DeviceIdType.MESH
VMEM_SPEC = pl.BlockSpec(memory_space=pltpu.VMEM)
SMEM_SPEC = pl.BlockSpec(memory_space=pltpu.SMEM)
ANY_SPEC = pl.BlockSpec(memory_space=pl.ANY)
NT = (((1,), (1,)), ((), ()))
TN = (((0,), (0,)), ((), ()))


COST_UNIT = 1_000_000_000
COSTS = {
    "pool": 12, "branch_sums": 2, "branch_act": 2, "join": 42, "join_sums": 4, "head": 5, "join_grad": 5,
    "branch_back": 16, "branch_dz": 2, "lifts": 10, "wgrad_fb": 15, "wgrad_fx0": 24, "wgrad_fx1": 24, "wgrad_br": 6,
    "dx": 33, "grad_x": 9,
}


def params(**extra):
    return pltpu.CompilerParams(vmem_limit_bytes=56 * 2**20, **extra)


def dot(a, b):
    return jnp.dot(a, b, preferred_element_type=F32)


def dot_nt(a, b):
    return lax.dot_general(a, b, NT, preferred_element_type=F32)


def dot_tn(a, b):
    return lax.dot_general(a, b, TN, preferred_element_type=F32)


def cell_table(box_count):
    table = np.zeros((8, CELLS), np.float32)
    table[1] = 1.0
    table[4] = 9.0
    at = 0
    for level, bins in enumerate(BINS):
        for box in range(box_count):
            for i in range(bins):
                for j in range(bins):
                    table[:6, at] = (box, bins, i, j, level, 1.0)
                    at += 1
    return table


def box_at(boxes_ref, canvas, box, box_count):
    base = (canvas * box_count + box) * 4
    return [boxes_ref[base + part] for part in range(4)]


def by_box(boxes_ref, canvas, which, box_count):
    sides = None
    for box in range(box_count):
        mine = [side.astype(F32) for side in box_at(boxes_ref, canvas, box, box_count)]
        if sides is None:
            sides = [jnp.full(which.shape, side, F32) for side in mine]
        else:
            sides = [jnp.where(which == box, new, old) for new, old in zip(mine, sides)]
    return sides


def within(relative, extent):
    return (relative >= 0) & (relative < extent)


def pixel_gates(boxes_ref, canvas, box_count, shape, axis):
    place = lax.broadcasted_iota(jnp.int32, shape, axis)
    row = place >> 5
    col = place & (CW - 1)
    rel = []
    for box in range(box_count):
        top, left, height, width = box_at(boxes_ref, canvas, box, box_count)
        rel.append((row - top, col - left, height, width))

    def gate(dy, dx):
        total = None
        for y, x, height, width in rel:
            hit = within(y, height) & within(x, width)
            if dy:
                hit = hit & within(y + dy, height)
            if dx:
                hit = hit & within(x + dx, width)
            value = jnp.where(hit, 1.0, 0.0)
            total = value if total is None else total + value
        return total

    return gate


def wide(column_block, times):
    return jnp.concatenate([column_block] * times, axis=1)


def member_bounds(table_at, height, width):
    bins, i, j = table_at(1), table_at(2), table_at(3)

    def start(at, extent):
        return jnp.floor((at * extent + 0.5) / bins)

    def stop(at, extent):
        return jnp.floor(((at + 1) * extent + bins - 0.5) / bins)

    return start(i, height), stop(i, height), start(j, width), stop(j, width)


def members(boxes_ref, canvas, box_count, table_at, shape, axis):
    top, left, height, width = by_box(boxes_ref, canvas, table_at(0), box_count)
    r0, r1, c0, c1 = member_bounds(table_at, height, width)
    place = lax.broadcasted_iota(jnp.int32, shape, axis)
    row = (place >> 5).astype(F32) - top
    col = (place & (CW - 1)).astype(F32) - left
    hit = (row >= r0) & (row < r1) & (col >= c0) & (col < c1) & (table_at(5) > 0)
    return jnp.where(hit, 1.0, 0.0), (r1 - r0) * (c1 - c0)


def gated_lifts(boxes_ref, canvas, box_count, lanes_ref):
    def table_at(row):
        return lanes_ref[row : row + 1, :]

    top, left, height, width = by_box(boxes_ref, canvas, table_at(0), box_count)
    place = lax.broadcasted_iota(jnp.int32, (PX, CELLS), 0)
    row = (place >> 5).astype(F32) - top
    col = (place & (CW - 1)).astype(F32) - left

    def side(relative, extent, cell):
        scale = (table_at(1) - 1.0) / (extent - 1.0)
        own = within(relative, extent)
        found = []
        for step in (-1, 0, 1):
            moved = relative + step
            weight = jnp.maximum(0.0, 1.0 - jnp.abs(moved * scale - cell))
            found.append(jnp.where(own & within(moved, extent), weight, 0.0))
        return found

    rows = [found * table_at(5) for found in side(row, height, table_at(2))]
    cols = side(col, width, table_at(3))
    return [rows[d // 3] * cols[d % 3] for d in range(9)]


def pltranspose(block):
    return jnp.transpose(block, (1, 0))


def lifts_kernel(box_count, boxes_ref, lanes_ref, out_ref):
    lifts = gated_lifts(boxes_ref, pl.program_id(0), box_count, lanes_ref)
    for d in range(9):
        out_ref[0, :, d * CELLS : (d + 1) * CELLS] = lifts[d].astype(BF16)


def pool_kernel(canv, box_count, boxes_ref, lanes_ref, cells_ref, x_ref, w_ref, pooled_ref, lift_ref, own_ref, send_ref, first_ref, last_ref, kept, zs):
    n = pl.program_id(0)
    span = first_ref.shape[1]
    first_ref[...] = x_ref[:, :span]
    last_ref[...] = x_ref[:, span:]

    def table_at(row):
        return cells_ref[:, row : row + 1]

    select, count = members(boxes_ref, n, box_count, table_at, (CELLS, PX), 1)
    pooled = (dot(select.astype(BF16), x_ref[...]) / count).astype(BF16)
    pooled_ref[...] = pooled
    kept[pl.ds(pl.multiple_of(n * CELLS, CELLS), CELLS), :] = pooled
    lifts = gated_lifts(boxes_ref, n, box_count, lanes_ref)
    for d in range(9):
        lift_ref[0, :, d * CELLS : (d + 1) * CELLS] = lifts[d].astype(BF16)

    @pl.when(n == canv - 1)
    def _():
        half = own_ref.shape[1]
        for level in range(4):
            part = dot(kept[...], w_ref[level])
            for m in range(canv):
                rows = slice(m * CELLS, (m + 1) * CELLS)
                mine = jnp.where(table_at(4) == level, part[rows], 0.0)
                zs[rows, :] = mine if level == 0 else zs[rows, :] + mine
        chan = lax.axis_index("chan")
        own_ref[...] = zs[:, pl.ds(pl.multiple_of(chan * half, half), half)]
        send_ref[...] = zs[:, pl.ds(pl.multiple_of((1 - chan) * half, half), half)].astype(BF16)


def branch_sums_kernel(canv, cells_ref, own_ref, got_ref, z_ref, part_ref):
    z = own_ref[...] + got_ref[...].astype(F32)
    z_ref[...] = z
    for level in range(4):
        first = second = 0.0
        for n in range(canv):
            mine = jnp.where(cells_ref[:, 4:5] == level, z[n * CELLS : (n + 1) * CELLS], 0.0)
            first = first + jnp.sum(mine, 0, keepdims=True)
            second = second + jnp.sum(mine * mine, 0, keepdims=True)
        part_ref[level : level + 1, :] = first
        part_ref[4 + level : 5 + level, :] = second


def exchange_kernel(total, own_ref, out_ref, slots, send_sem, recv_sem):
    me = lax.axis_index("dp")
    chan = lax.axis_index("chan")
    barrier = pltpu.get_barrier_semaphore()

    def signal(step, carry):
        pl.semaphore_signal(barrier, inc=1, device_id=(lax.rem(me + step, total), chan), device_id_type=MESH)
        return carry

    lax.fori_loop(1, total, signal, 0)
    slots[me] = own_ref[...]
    pl.semaphore_wait(barrier, total - 1)

    def copy_to(step):
        return pltpu.make_async_remote_copy(
            src_ref=own_ref,
            dst_ref=slots.at[me],
            send_sem=send_sem.at[step],
            recv_sem=recv_sem.at[me],
            device_id=(lax.rem(me + step, total), chan),
            device_id_type=MESH,
        )

    def copy_from(step):
        other = lax.rem(me + total - step, total)
        return pltpu.make_async_remote_copy(
            src_ref=own_ref,
            dst_ref=slots.at[other],
            send_sem=send_sem.at[step],
            recv_sem=recv_sem.at[other],
            device_id=(other, chan),
            device_id_type=MESH,
        )

    def start(step, carry):
        copy_to(step).start()
        return carry

    def finish(step, carry):
        copy_from(step).wait_recv()
        return carry

    def sent(step, carry):
        copy_to(step).wait_send()
        return carry

    lax.fori_loop(1, total, start, 0)
    lax.fori_loop(1, total, finish, 0)
    lax.fori_loop(1, total, sent, 0)
    value = slots[0]
    for other in range(1, total):
        value = value + slots[other]
    out_ref[...] = value


def dp_sum(part, total, number, after=()):
    return launch(
        functools.partial(exchange_kernel, total),
        after=after,
        out_shape=jax.ShapeDtypeStruct(part.shape, F32),
        in_specs=[VMEM_SPEC],
        out_specs=VMEM_SPEC,
        scratch_shapes=[
            pltpu.VMEM((total,) + part.shape, F32),
            pltpu.SemaphoreType.DMA((total,)),
            pltpu.SemaphoreType.DMA((total,)),
        ],
        compiler_params=pltpu.CompilerParams(collective_id=number, has_side_effects=True),
        name="dp_sum%d" % number,
    )(part)


def branch_stat(total_ref, level, rows_all):
    mean = total_ref[level : level + 1, :] / rows_all
    var = total_ref[4 + level : 5 + level, :] / rows_all - mean * mean
    return mean, lax.rsqrt(var + EPS)


def branch_act_kernel(canv, rows_all, cells_ref, z_ref, total_ref, gain_ref, bias_ref, y_ref, norm_ref, act_ref):
    for n in range(canv):
        rows = slice(n * CELLS, (n + 1) * CELLS)
        z = z_ref[rows]
        norm = act = 0.0
        for level in range(4):
            mean, rstd = branch_stat(total_ref, level, rows_all[level])
            here = jnp.where(cells_ref[:, 4:5] == level, 1.0, 0.0)
            mine = (z - mean) * rstd
            norm = norm + here * mine
            act = act + here * (gain_ref[level : level + 1, :] * mine + bias_ref[level : level + 1, :])
        norm_ref[rows] = norm
        act_ref[rows] = act
        y_ref[rows] = (act * jax.nn.sigmoid(act)).astype(BF16)

def expand(y, cells_ref, keep):
    width = y.shape[1]
    for n in range(y.shape[0] // CELLS):
        rows = slice(n * CELLS, (n + 1) * CELLS)
        block = y[rows].astype(F32)
        for level in range(4):
            mine = jnp.where(cells_ref[:, 4:5] == level, block, 0.0)
            keep[rows, level * width : (level + 1) * width] = mine.astype(BF16)


def join_kernel(canv, box_count, boxes_ref, cells_ref, x_ref, y_ref, lift_ref, wfx_ref, wfb_ref, own_ref, send_ref, q, gy, zp, ye):
    d = pl.program_id(0)
    dy = d // 3
    dx = d % 3
    mid = wfx_ref.shape[2]
    reps = mid // CELLS

    @pl.when(d == 0)
    def _():
        q[...] = jnp.zeros_like(q)
        zp[...] = jnp.zeros_like(zp)
        expand(y_ref[...], cells_ref, ye)
        for n in range(canv):
            gate = pixel_gates(boxes_ref, n, box_count, (PX, CELLS), 0)
            for step in range(3):
                gy[step, n] = gate(step - 1, 0)

    wfb = wfb_ref[0].reshape(ye.shape[1], mid)
    terms = dot(ye[...], wfb).astype(BF16)
    for n in range(canv):
        zp[n, CW : CW + PX] = dot(x_ref[n * PX : (n + 1) * PX], wfx_ref[0])
        q[1, n] += dot(lift_ref[n], terms[n * CELLS : (n + 1) * CELLS])
    for n in range(canv):
        moved = zp[n, pl.ds(pl.multiple_of(dy * CW, CW), PX)]
        q[dx, n] += wide(gy[dy, n], reps) * moved

    @pl.when(d == 8)
    def _():
        half = own_ref.shape[1]
        chan = lax.axis_index("chan")
        for n in range(canv):
            gate = pixel_gates(boxes_ref, n, box_count, (PX, CELLS), 0)
            f = q[1, n] + wide(gate(0, -1), reps) * pltpu.roll(q[0, n], 1, 0)
            f = f + wide(gate(0, 1), reps) * pltpu.roll(q[2, n], PX - 1, 0)
            zp[n, CW : CW + PX] = f
            rows = slice(n * PX, (n + 1) * PX)
            own_ref[rows] = zp[n, CW : CW + PX, pl.ds(pl.multiple_of(chan * half, half), half)]
            send_ref[rows] = zp[n, CW : CW + PX, pl.ds(pl.multiple_of((1 - chan) * half, half), half)].astype(BF16)


def join_sums_kernel(canv, box_count, boxes_ref, own_ref, got_ref, f_ref, part_ref):
    n = pl.program_id(0)
    f = own_ref[...] + got_ref[...].astype(F32)
    f_ref[...] = f

    @pl.when(n == 0)
    def _():
        part_ref[...] = jnp.zeros_like(part_ref)

    area = 0
    for box in range(box_count):
        side = box_at(boxes_ref, n, box, box_count)
        area = area + side[2] * side[3]
    part_ref[0:1, :] += jnp.sum(f, 0, keepdims=True)
    part_ref[1:2, :] += jnp.sum(f * f, 0, keepdims=True)
    part_ref[2:3, :] += jnp.full((1, f.shape[1]), area.astype(F32), F32)


def join_stat(total_ref):
    count = total_ref[2:3, :]
    mean = total_ref[0:1, :] / count
    var = total_ref[1:2, :] / count - mean * mean
    return mean, lax.rsqrt(var + EPS), count


def head_kernel(box_count, boxes_ref, f_ref, total_ref, gain_ref, bias_ref, w_ref, g_ref, score_ref, db_ref, part_ref, dw_ref):
    n = pl.program_id(0)
    half = f_ref.shape[1]
    chan = lax.axis_index("chan")
    w = w_ref[pl.ds(pl.multiple_of(chan * half, half), half), :]
    own = pl.ds(pl.multiple_of(chan * half, half), half)
    valid = wide(pixel_gates(boxes_ref, n, box_count, (PX, CELLS), 0)(0, 0), half // CELLS)
    mean, rstd, _ = join_stat(total_ref)
    norm = (f_ref[...] - mean) * rstd
    act = gain_ref[:, own] * norm + bias_ref[:, own]
    sig = jax.nn.sigmoid(act)
    hidden = (act * sig * valid).astype(BF16)
    g = g_ref[...]
    score_ref[...] = dot(hidden, w).astype(BF16)
    db = dot_nt(g, w) * valid * sig * (1.0 + act * (1.0 - sig))
    db_ref[...] = db

    @pl.when(n == 0)
    def _():
        part_ref[...] = jnp.zeros_like(part_ref)
        dw_ref[...] = jnp.zeros_like(dw_ref)

    part_ref[0:1, :] += jnp.sum(db * norm, 0, keepdims=True)
    part_ref[1:2, :] += jnp.sum(db, 0, keepdims=True)
    part_ref[2:3, : g.shape[1]] += jnp.sum(g.astype(F32), 0, keepdims=True)
    dw_ref[...] += dot_tn(hidden, g)


def split_rows(rows, groups, each, own_a, send_a, own_b, send_b, send_d=None):
    me = lax.axis_index("dp")
    x_bit = me % 2
    y_bit = (me // 2) % 2

    def piece(group, y, x):
        return rows[pl.ds(pl.multiple_of(((group * 2 + y) * 2 + x) * each, each), each), :].astype(BF16)

    for group in range(groups):
        for bit in range(2):
            at = (bit * groups + group) * each
            own_a[at : at + each] = piece(group, bit, x_bit)
            send_a[at : at + each] = piece(group, bit, 1 - x_bit)
            own_b[at : at + each] = piece(group, y_bit, bit)
            send_b[at : at + each] = piece(group, 1 - y_bit, bit)
        if send_d is not None:
            send_d[group * each : (group + 1) * each] = piece(group, 1 - y_bit, 1 - x_bit)


def join_grad_kernel(box_count, each, boxes_ref, f_ref, db_ref, total_ref, sums_ref, gain_ref, df_ref, pack_ref, send_a, send_b, send_d, flip):
    n = pl.program_id(0)
    half = f_ref.shape[1]
    own = pl.ds(pl.multiple_of(lax.axis_index("chan") * half, half), half)
    valid = wide(pixel_gates(boxes_ref, n, box_count, (PX, CELLS), 0)(0, 0), half // CELLS)
    mean, rstd, count = join_stat(total_ref)
    norm = (f_ref[...] - mean) * rstd
    df = gain_ref[:, own] * rstd * (db_ref[...] - sums_ref[1:2, :] / count - norm * (sums_ref[0:1, :] / count)) * valid
    df_ref[...] = df.astype(BF16)
    flip[...] = pltranspose(df)
    pack_ref[0:half] = flip[...].astype(BF16)
    own_a = pack_ref.at[half : half + half // 2]
    own_b = pack_ref.at[half + half // 2 : 2 * half]
    split_rows(flip, half // (4 * each), each, own_a, send_a, own_b, send_b, send_d)


def dx_kernel(canv, box_count, boxes_ref, own_ref, got_ref, w_ref, out_ref, acc, gy, e3):
    d = pl.program_id(0)
    dy = d // 3
    dx = d % 3
    half = own_ref.shape[1]
    reps = half // CELLS
    chan = lax.axis_index("chan")

    @pl.when(d == 0)
    def _():
        e3[...] = jnp.zeros_like(e3)
        for n in range(canv):
            gate = pixel_gates(boxes_ref, n, box_count, (PX, CELLS), 0)
            for step in range(3):
                gy[step, n] = gate(1 - step, 0).astype(BF16)
            rows = slice(n * PX, (n + 1) * PX)
            for side, ref in enumerate((own_ref, got_ref)):
                df = ref[rows].astype(F32)
                e3[side, 1, n, CW : CW + PX] = df.astype(BF16)
                e3[side, 0, n, CW : CW + PX] = (wide(gate(0, 1), reps) * pltpu.roll(df, PX - 1, 0)).astype(BF16)
                e3[side, 2, n, CW : CW + PX] = (wide(gate(0, -1), reps) * pltpu.roll(df, 1, 0)).astype(BF16)

    for n in range(canv):
        total = None
        for side, which in ((0, chan), (1, 1 - chan)):
            e = e3[side, dx, n, pl.ds(pl.multiple_of((2 - dy) * CW, CW), PX)] * wide(gy[dy, n], reps)
            w = w_ref[0, :, pl.ds(pl.multiple_of(which * half, half), half)]
            part = dot_nt(e, w)
            total = part if total is None else total + part

        @pl.when(d == 0)
        def _():
            acc[n] = total

        @pl.when(d > 0)
        def _():
            acc[n] += total

    @pl.when(d == 8)
    def _():
        for n in range(canv):
            out_ref[n * PX : (n + 1) * PX] = acc[n].astype(BF16)


def branch_back_kernel(canv, boxes_unused, cells_ref, lanes_ref, own_ref, got_ref, lift_ref, w_ref, norm_ref, act_ref, da_ref, part_ref, acc):
    d = pl.program_id(0)
    half = own_ref.shape[0]
    chan = lax.axis_index("chan")

    @pl.when(d == 0)
    def _():
        acc[...] = jnp.zeros_like(acc)

    for ref, which in ((own_ref, chan), (got_ref, 1 - chan)):
        cells = [dot(ref[:, n * PX : (n + 1) * PX], lift_ref[n]).astype(BF16) for n in range(canv)]
        w = w_ref[0, :, :, pl.ds(pl.multiple_of(which * half, half), half)].reshape(acc.shape[0], half)
        acc[...] += dot(w, jnp.concatenate(cells, axis=1))

    @pl.when(d == 8)
    def _():
        width = norm_ref.shape[1]
        levels = jnp.concatenate([lanes_ref[4:5, :]] * canv, axis=1)
        dy = 0.0
        for level in range(4):
            dy = dy + jnp.where(levels == level, acc[level * width : (level + 1) * width], 0.0)
        dy = pltranspose(dy)
        act = act_ref[...]
        sig = jax.nn.sigmoid(act)
        da = dy * sig * (1.0 + act * (1.0 - sig))
        da_ref[...] = da
        for level in range(4):
            gain = bias = 0.0
            for n in range(canv):
                rows = slice(n * CELLS, (n + 1) * CELLS)
                mine = jnp.where(cells_ref[:, 4:5] == level, da[rows], 0.0)
                gain = gain + jnp.sum(mine * norm_ref[rows], 0, keepdims=True)
                bias = bias + jnp.sum(mine, 0, keepdims=True)
            part_ref[level : level + 1, :] = gain
            part_ref[4 + level : 5 + level, :] = bias


def branch_dz_kernel(canv, rows_all, each, cells_ref, da_ref, norm_ref, total_ref, sums_ref, gain_ref, dz_ref, pack_ref, send_a, send_b, flip):
    for n in range(canv):
        rows = slice(n * CELLS, (n + 1) * CELLS)
        dz = 0.0
        for level in range(4):
            _, rstd = branch_stat(total_ref, level, rows_all[level])
            here = jnp.where(cells_ref[:, 4:5] == level, 1.0, 0.0)
            mean_gain = sums_ref[level : level + 1, :] / rows_all[level]
            mean_bias = sums_ref[4 + level : 5 + level, :] / rows_all[level]
            mine = gain_ref[level : level + 1, :] * rstd * (da_ref[rows] - mean_bias - norm_ref[rows] * mean_gain)
            dz = dz + here * mine
        dz_ref[rows] = dz.astype(BF16)
        flip[:, rows] = pltranspose(dz)
    half = flip.shape[0]
    split_rows(flip, half // (4 * each), each, pack_ref.at[0 : half // 2], send_a, pack_ref.at[half // 2 : half], send_b)


def grad_x_kernel(canv, box_count, boxes_ref, lanes_ref, cells_ref, own_ref, got_ref, w_ref, dx_ref, out_ref, kept):
    n = pl.program_id(0)
    half = own_ref.shape[1]
    chan = lax.axis_index("chan")

    @pl.when(n == 0)
    def _():
        total = 0.0
        for level in range(4):
            for ref, which in ((own_ref, chan), (got_ref, 1 - chan)):
                mine = [
                    jnp.where(cells_ref[:, 4:5] == level, ref[m * CELLS : (m + 1) * CELLS].astype(F32), 0.0).astype(BF16)
                    for m in range(canv)
                ]
                w = w_ref[level, :, pl.ds(pl.multiple_of(which * half, half), half)]
                total = total + dot_nt(jnp.concatenate(mine, axis=0), w)
        for m in range(canv):
            top, left, height, width = by_box(boxes_ref, m, cells_ref[:, 0:1], box_count)
            r0, r1, c0, c1 = member_bounds(lambda row: cells_ref[:, row : row + 1], height, width)
            kept[m] = (total[m * CELLS : (m + 1) * CELLS] / ((r1 - r0) * (c1 - c0))).astype(BF16)

    select, _ = members(boxes_ref, n, box_count, lambda row: lanes_ref[row : row + 1, :], (PX, CELLS), 0)
    out_ref[...] = (dx_ref[...].astype(F32) + dot(select.astype(BF16), kept[n])).astype(BF16)


def put_rows(out, index, own_ref, other_ref, scale=None):
    chan = lax.axis_index("chan")
    size = own_ref.shape[0]
    for ref, which in ((own_ref, chan), (other_ref, 1 - chan)):
        value = ref[...] if scale is None else (ref[...].astype(F32) * scale).astype(BF16)
        out[index, pl.ds(pl.multiple_of(which * size, size), size), :] = value


def wgrad_kernel(
    canv, box_count, bit_of, boxes0, boxes1, cells_ref, own0, other0, own1, other1, x0, x1, keep_ref, send_ref, pooled_ref, acc, lhs, xd
):
    pixels = x0.shape[0]
    reps = x0.shape[1] // CELLS
    for source, (boxes_ref, own_ref, other_ref, x_ref) in enumerate(((boxes0, own0, other0, x0), (boxes1, own1, other1, x1))):
        down = []
        for n in range(canv):
            rows = slice(n * PX, (n + 1) * PX)
            into = slice(CW + n * PX, CW + (n + 1) * PX)
            gate = pixel_gates(boxes_ref, n, box_count, (PX, CELLS), 0)
            x = x_ref[rows].astype(F32)
            xd[0, into] = (wide(gate(0, -1), reps) * pltpu.roll(x, 1, 0)).astype(BF16)
            xd[1, into] = x_ref[rows]
            xd[2, into] = (wide(gate(0, 1), reps) * pltpu.roll(x, PX - 1, 0)).astype(BF16)
            across = pixel_gates(boxes_ref, n, box_count, (8, PX), 1)
            down.append([across(step, 0)[0:1, :] for step in (-1, 0, 1)])
        if source == 0:
            for step in range(3):
                xd[step, 0:CW] = jnp.zeros((CW, x0.shape[1]), BF16)
                xd[step, CW + pixels : 2 * CW + pixels] = jnp.zeros((CW, x0.shape[1]), BF16)
        else:
            for n in range(canv):
                select, count = members(
                    boxes_ref, n, box_count, lambda row: cells_ref[:, row : row + 1], (CELLS, PX), 1
                )
                sums = dot(select.astype(BF16), x_ref[n * PX : (n + 1) * PX])
                pooled_ref[n * CELLS : (n + 1) * CELLS] = (sums / count).astype(BF16)
        for step in range(3):
            put_rows(lhs, step, own_ref, other_ref, jnp.concatenate([found[step] for found in down], axis=1))

        def offset(d, carry):
            dy = d // 3
            part = dot(lhs[dy], xd[d % 3, pl.ds(pl.multiple_of(dy * CW, CW), pixels), :])
            if source == 0:
                acc[d] = part
            else:
                acc[d] += part
            return carry

        lax.fori_loop(0, 9, offset, 0)
    split_out(9, bit_of, acc, keep_ref, send_ref)


def split_out(count, bit_of, acc, keep_ref, send_ref):
    bit = (lax.axis_index("dp") // bit_of) % 2
    size = keep_ref.shape[2]

    def one(d, carry):
        for half in range(2):
            for ref, which in ((keep_ref, bit), (send_ref, 1 - bit)):
                ref[d, half] = acc[d, pl.ds(pl.multiple_of((half * 2 + which) * size, size), size), :].astype(BF16)
        return carry

    lax.fori_loop(0, count, one, 0)


def wgrad_fb_kernel(
    canv, cells_ref, own0, oth0, own1, oth1, own2, oth2, own3, oth3, lift0_ref, lift1_ref, y_ref, out_ref, ye, lhs
):
    d = pl.program_id(0)

    @pl.when(d == 0)
    def _():
        expand(y_ref[...], cells_ref, ye)
        me = lax.axis_index("dp")
        x_bit, y_bit = me % 2, (me // 2) % 2
        size = own3.shape[0]
        sources = ((own0, oth0, y_bit), (own1, oth1, y_bit), (own2, oth2, x_bit), (own3, oth3, 0))
        for source, (own_ref, oth_ref, bit) in enumerate(sources):
            mine = pl.ds(pl.multiple_of(bit * size, size), size)
            put_rows(lhs, source, own_ref.at[mine], oth_ref.at[mine])

    cells = []
    for n in range(PLANE * canv):
        lift = lift0_ref[n] if n < canv else lift1_ref[n - canv]
        grads = lhs[n // canv, :, (n % canv) * PX : (n % canv + 1) * PX]
        cells.append(dot(grads, lift).astype(BF16))
    result = dot(jnp.concatenate(cells, axis=1), ye[...])
    parts, _, each, _ = out_ref.shape
    for part in range(parts):
        out_ref[part, 0] = result[part * each : (part + 1) * each].astype(BF16)


def wgrad_br_kernel(canv, lanes_ref, own_ref, oth_ref, owna, otha, ownb, othb, pooled_ref, poola, poolb, keepa, senda, keepb, sendb, acc, lhs):
    levels = jnp.concatenate([lanes_ref[4:5, :]] * canv, axis=1)
    size = owna.shape[0]
    wide_by = poola.shape[1]
    sides = ((0, owna, otha, poola, keepa, senda, 2), (1, ownb, othb, poolb, keepb, sendb, 1))
    for side, own1, oth1, pool1, keep_ref, send_ref, bit_of in sides:
        mine = slice(side * size, (side + 1) * size)
        put_rows(lhs, 0, own_ref.at[mine], oth_ref.at[mine])
        put_rows(lhs, 1, own1, oth1)
        pool0 = pooled_ref[:, side * wide_by : (side + 1) * wide_by]
        for level in range(4):
            left = [jnp.where(levels == level, lhs[source].astype(F32), 0.0).astype(BF16) for source in range(2)]
            acc[level] = dot(left[0], pool0) + dot(left[1], pool1[...])
        split_out(4, bit_of, acc, keep_ref, send_ref)


def launch(kernel, in_specs, after=(), **rest):
    used = len(in_specs)
    extra = len(after)

    def body(*refs):
        kernel(*refs[:used], *refs[used + extra :])

    cost = pl.CostEstimate(flops=COST_UNIT * COSTS.get(rest["name"], 10), bytes_accessed=0, transcendentals=0)
    call = pl.pallas_call(body, cost_estimate=cost, in_specs=list(in_specs) + [ANY_SPEC] * extra, **rest)
    return lambda *operands: call(*operands, *after)


def whole(shape):
    return pl.BlockSpec(shape, lambda i: (0,) * len(shape))


def shaped(shape, kind):
    return jax.ShapeDtypeStruct(shape, kind)


def per_device(features, boxes, w_branch, gain_branch, bias_branch, w_fx, w_fb, gain_join, bias_join, w_cls, b_cls, grad_logits):
    canv, box_count = boxes.shape[:2]
    pixels, cin = features.shape
    mid = gain_join.shape[0]
    half = mid // lax.axis_size("chan")
    bw = gain_branch.shape[1]
    br = w_branch.shape[2]
    ncls = w_cls.shape[1]
    dp = lax.axis_size("dp")
    parts = dp // PLANE
    each = mid // dp
    cols = parts * each
    rows = canv * CELLS
    chan = lax.axis_index("chan")
    me = lax.axis_index("dp")
    rows_all = [float(canv * dp * box_count * s * s) for s in BINS]
    lanes_np = cell_table(box_count)
    lanes = jnp.asarray(lanes_np)
    cells = jnp.asarray(np.concatenate([lanes_np.T, np.zeros((CELLS, CELLS - 8), np.float32)], 1))

    def to_mate(array, mate):
        return lax.ppermute(array, "dp", [(i, i ^ mate) for i in range(dp)])

    def swap(array):
        return lax.ppermute(array, "chan", [(0, 1), (1, 0)])

    def to_part(array, step):
        return lax.ppermute(array, "dp", [(i, ((i // PLANE + step) % parts) * PLANE + i % PLANE) for i in range(dp)])

    flat = boxes.reshape(-1)
    flat_of = [flat] + [to_mate(flat, m) for m in (1, 2, 3)]
    flat_mates = jnp.concatenate(flat_of[1:])

    pooled, lifts, z_own, z_send, x_first, x_last = launch(
        functools.partial(pool_kernel, canv, box_count),
        grid=(canv,),
        in_specs=[
            SMEM_SPEC,
            whole(lanes.shape),
            whole(cells.shape),
            pl.BlockSpec((PX, cin), lambda i: (i, 0)),
            whole(w_branch.shape),
        ],
        out_specs=[
            pl.BlockSpec((CELLS, cin), lambda i: (i, 0)),
            pl.BlockSpec((1, PX, 9 * CELLS), lambda i: (i, 0, 0)),
            whole((rows, bw)),
            whole((rows, bw)),
            pl.BlockSpec((PX, cin // 2), lambda i: (i, 0)),
            pl.BlockSpec((PX, cin // 2), lambda i: (i, 0)),
        ],
        out_shape=[
            shaped((rows, cin), BF16),
            shaped((canv, PX, 9 * CELLS), BF16),
            shaped((rows, bw), F32),
            shaped((rows, bw), BF16),
            shaped((pixels, cin // 2), BF16),
            shaped((pixels, cin // 2), BF16),
        ],
        scratch_shapes=[pltpu.VMEM((rows, cin), BF16), pltpu.VMEM((rows, br), F32)],
        compiler_params=params(),
        name="pool",
    )(flat, lanes, cells, features, w_branch)
    z_got = swap(z_send)
    z, z_part = launch(
        functools.partial(branch_sums_kernel, canv),
        in_specs=[VMEM_SPEC] * 3,
        out_specs=[VMEM_SPEC] * 2,
        out_shape=[shaped((rows, bw), F32), shaped((8, bw), F32)],
        compiler_params=params(),
        name="branch_sums",
    )(cells, z_own, z_got)
    z_total = dp_sum(z_part, dp, 0)
    y, z_norm, z_act = launch(
        functools.partial(branch_act_kernel, canv, rows_all),
        in_specs=[VMEM_SPEC] * 5,
        out_specs=[VMEM_SPEC] * 3,
        out_shape=[shaped((rows, bw), BF16), shaped((rows, bw), F32), shaped((rows, bw), F32)],
        compiler_params=params(),
        name="branch_act",
    )(cells, z, z_total, gain_branch, bias_branch)
    x_mate = to_mate(x_first, 1)
    y_mate = to_mate(x_last, 2)
    y_all = jnp.concatenate([y] + [to_mate(y, m) for m in (1, 2, 3)], 0)

    f_own, f_send = launch(
        functools.partial(join_kernel, canv, box_count),
        grid=(9,),
        in_specs=[
            SMEM_SPEC,
            whole(cells.shape),
            whole((pixels, cin)),
            whole((rows, bw)),
            pl.BlockSpec((canv, PX, CELLS), lambda i: (0, 0, i)),
            pl.BlockSpec((1, cin, mid), lambda i: (i, 0, 0)),
            pl.BlockSpec((1, 4, bw, mid), lambda i: (i, 0, 0, 0)),
        ],
        out_specs=[whole((pixels, half)), whole((pixels, half))],
        out_shape=[shaped((pixels, half), F32), shaped((pixels, half), BF16)],
        scratch_shapes=[
            pltpu.VMEM((3, canv, PX, mid), F32),
            pltpu.VMEM((3, canv, PX, CELLS), F32),
            pltpu.VMEM((canv, PX + 2 * CW, mid), F32),
            pltpu.VMEM((rows, 4 * bw), BF16),
        ],
        compiler_params=params(),
        name="join",
    )(flat, cells, features, y, lifts, w_fx, w_fb)
    f_got = swap(f_send)
    by_canvas = pl.BlockSpec((PX, half), lambda i: (i, 0))
    f, f_part = launch(
        functools.partial(join_sums_kernel, canv, box_count),
        grid=(canv,),
        in_specs=[SMEM_SPEC, by_canvas, by_canvas],
        out_specs=[by_canvas, whole((8, half))],
        out_shape=[shaped((pixels, half), F32), shaped((8, half), F32)],
        compiler_params=params(),
        name="join_sums",
        after=(x_mate, y_mate, y_all),
    )(flat, f_own, f_got)
    f_total = dp_sum(f_part, dp, 1)
    gain_row = gain_join.reshape(1, mid)
    bias_row = bias_join.reshape(1, mid)
    score, db, db_part, dw_cls = launch(
        functools.partial(head_kernel, box_count),
        grid=(canv,),
        in_specs=[
            SMEM_SPEC,
            by_canvas,
            whole((8, half)),
            whole((1, mid)),
            whole((1, mid)),
            whole((mid, ncls)),
            pl.BlockSpec((PX, ncls), lambda i: (i, 0)),
        ],
        out_specs=[pl.BlockSpec((PX, ncls), lambda i: (i, 0)), by_canvas, whole((8, half)), whole((half, ncls))],
        out_shape=[
            shaped((pixels, ncls), BF16),
            shaped((pixels, half), F32),
            shaped((8, half), F32),
            shaped((half, ncls), F32),
        ],
        compiler_params=params(),
        name="head",
    )(flat, f, f_total, gain_row, bias_row, w_cls, grad_logits)
    db_total = dp_sum(db_part, dp, 2)
    logits = (score.astype(F32) + swap(score).astype(F32) + b_cls).astype(BF16)
    quarter = half // 2
    df, pack, send_a, send_b, send_d = launch(
        functools.partial(join_grad_kernel, box_count, each),
        grid=(canv,),
        in_specs=[SMEM_SPEC, by_canvas, by_canvas, whole((8, half)), whole((8, half)), whole((1, mid))],
        out_specs=[by_canvas]
        + [pl.BlockSpec((size, PX), lambda i: (0, i)) for size in (2 * half, quarter, quarter, quarter // 2)],
        out_shape=[shaped((pixels, half), BF16)]
        + [shaped((size, pixels), BF16) for size in (2 * half, quarter, quarter, quarter // 2)],
        scratch_shapes=[pltpu.VMEM((half, PX), F32)],
        compiler_params=params(),
        name="join_grad",
    )(flat, f, db, f_total, db_total, gain_row)
    got_a, got_b, got_d = to_mate(send_a, 1), to_mate(send_b, 2), to_mate(send_d, 3)
    pack_other = swap(pack)
    df_got = swap(df)
    other_a, other_b, other_d = swap(got_a), swap(got_b), swap(got_d)
    half_rows = pl.BlockSpec((half, pixels), lambda i: (0, 0))

    da, da_part = launch(
        functools.partial(branch_back_kernel, canv),
        grid=(9,),
        in_specs=[
            SMEM_SPEC,
            whole(cells.shape),
            whole(lanes.shape),
            half_rows,
            half_rows,
            pl.BlockSpec((canv, PX, CELLS), lambda i: (0, 0, i)),
            pl.BlockSpec((1, 4, bw, mid), lambda i: (i, 0, 0, 0)),
            whole((rows, bw)),
            whole((rows, bw)),
        ],
        out_specs=[whole((rows, bw)), whole((8, bw))],
        out_shape=[shaped((rows, bw), F32), shaped((8, bw), F32)],
        scratch_shapes=[pltpu.VMEM((4 * bw, rows), F32)],
        compiler_params=params(),
        name="branch_back",
    )(flat, cells, lanes, pack, pack_other, lifts, w_fb, z_norm, z_act)
    da_total = dp_sum(da_part, dp, 3, (other_a, other_b, other_d))
    dz, zpack, zsend_a, zsend_b = launch(
        functools.partial(branch_dz_kernel, canv, rows_all, each),
        in_specs=[VMEM_SPEC] * 6,
        out_specs=[VMEM_SPEC] * 4,
        out_shape=[
            shaped((rows, bw), BF16),
            shaped((bw, rows), BF16),
            shaped((quarter, rows), BF16),
            shaped((quarter, rows), BF16),
        ],
        scratch_shapes=[pltpu.VMEM((bw, rows), F32)],
        compiler_params=params(),
        name="branch_dz",
    )(cells, da, z_norm, z_total, da_total, gain_branch)
    zgot_a, zgot_b = to_mate(zsend_a, 1), to_mate(zsend_b, 2)
    dz_got, zpack_other, zother_a, zother_b = swap(dz), swap(zpack), swap(zgot_a), swap(zgot_b)

    steps = PLANE * canv
    lifts_mates = launch(
        functools.partial(lifts_kernel, box_count),
        grid=(steps - canv,),
        in_specs=[SMEM_SPEC, whole(lanes.shape)],
        out_specs=pl.BlockSpec((1, PX, 9 * CELLS), lambda i: (i, 0, 0)),
        out_shape=shaped((steps - canv, PX, 9 * CELLS), BF16),
        compiler_params=params(),
        name="lifts",
    )(flat_mates, lanes)
    quarter_at = [pl.BlockSpec((quarter, pixels), lambda i, at=at: (at, 0)) for at in (2, 0, 0)]
    fb_parts = launch(
        functools.partial(wgrad_fb_kernel, canv),
        grid=(9,),
        in_specs=[
            whole(cells.shape),
            quarter_at[0],
            quarter_at[0],
            quarter_at[1],
            quarter_at[1],
            quarter_at[2],
            quarter_at[2],
            whole((quarter // 2, pixels)),
            whole((quarter // 2, pixels)),
            pl.BlockSpec((canv, PX, CELLS), lambda i: (0, 0, i)),
            pl.BlockSpec((steps - canv, PX, CELLS), lambda i: (0, 0, i)),
            whole((steps * CELLS, bw)),
        ],
        out_specs=pl.BlockSpec((parts, 1, each, 4 * bw), lambda i: (0, i, 0, 0)),
        out_shape=shaped((parts, 9, each, 4 * bw), BF16),
        scratch_shapes=[pltpu.VMEM((steps * CELLS, 4 * bw), BF16), pltpu.VMEM((PLANE, cols, pixels), BF16)],
        compiler_params=params(),
        name="wgrad_fb",
        after=(da_total,),
    )(cells, pack, pack_other, got_a, other_a, got_b, other_b, got_d, other_d, lifts, lifts_mates, y_all)

    span = cin // 2

    def wgrad(side, bit_of, boxes_mate, got, other, x_got, after):
        own = pl.BlockSpec((quarter, pixels), lambda i: (2 + side, 0))
        return launch(
            functools.partial(wgrad_kernel, canv, box_count, bit_of),
            grid=(1,),
            in_specs=[
                SMEM_SPEC,
                SMEM_SPEC,
                whole(cells.shape),
                own,
                own,
                whole((quarter, pixels)),
                whole((quarter, pixels)),
                pl.BlockSpec((pixels, span), lambda i: (0, side)),
                whole((pixels, span)),
            ],
            out_specs=[whole((9, 2, quarter // 2, span))] * 2 + [whole((rows, span))],
            out_shape=[shaped((9, 2, quarter // 2, span), BF16)] * 2 + [shaped((rows, span), BF16)],
            scratch_shapes=[
                pltpu.VMEM((9, half, span), F32),
                pltpu.VMEM((3, half, pixels), BF16),
                pltpu.VMEM((3, pixels + 2 * CW, span), BF16),
            ],
            compiler_params=params(),
            name="wgrad_fx%d" % side,
            after=after,
        )(flat, boxes_mate, cells, pack, pack_other, got, other, features, x_got)

    keep_fa, send_fa, pool_a = wgrad(0, 2, flat_of[1], got_a, other_a, x_mate, (fb_parts,))
    keep_fb, send_fb, pool_b = wgrad(1, 1, flat_of[2], got_b, other_b, y_mate, (send_fa,))
    quarter_shape = (4, 2, quarter // 2, span)
    keep_ba, send_ba, keep_bb, send_bb = launch(
        functools.partial(wgrad_br_kernel, canv),
        in_specs=[VMEM_SPEC] * 10,
        out_specs=[VMEM_SPEC] * 4,
        out_shape=[shaped(quarter_shape, BF16)] * 4,
        scratch_shapes=[pltpu.VMEM((4, half, span), F32), pltpu.VMEM((2, half, rows), BF16)],
        compiler_params=params(),
        name="wgrad_br",
    )(lanes, zpack, zpack_other, zgot_a, zother_a, zgot_b, zother_b, pooled, pool_a, pool_b)

    def across_groups(pick):
        group = me // PLANE
        total = pick(group)
        for step in range(1, parts):
            total = total + to_part(pick((group + step) % parts).astype(BF16), step).astype(F32)
        return total

    def through_mate(keep, send, mate):
        got = to_mate(send, mate)
        shape = (keep.shape[0], parts, each, span)

        def pick(part):
            mine = [lax.dynamic_index_in_dim(a.reshape(shape), part, 1, keepdims=False) for a in (keep, got)]
            return mine[0].astype(F32) + mine[1].astype(F32)

        return across_groups(pick)

    sum_fb = across_groups(lambda part: lax.dynamic_index_in_dim(fb_parts, part, 0, keepdims=False).astype(F32))
    out_fb = jnp.transpose(sum_fb.reshape(9, each, 4, bw), (0, 2, 3, 1))
    out_fx = [through_mate(keep_fa, send_fa, 2), through_mate(keep_fb, send_fb, 1)]
    out_fx = jnp.transpose(jnp.concatenate(out_fx, 2), (0, 2, 1))
    out_br = [through_mate(keep_ba, send_ba, 2), through_mate(keep_bb, send_bb, 1)]
    out_br = jnp.transpose(jnp.concatenate(out_br, 2), (0, 2, 1))

    dx = launch(
        functools.partial(dx_kernel, canv, box_count),
        grid=(9,),
        in_specs=[
            SMEM_SPEC,
            whole((pixels, half)),
            whole((pixels, half)),
            pl.BlockSpec((1, cin, mid), lambda i: (i, 0, 0)),
        ],
        out_specs=whole((pixels, cin)),
        out_shape=shaped((pixels, cin), BF16),
        scratch_shapes=[
            pltpu.VMEM((canv, PX, cin), F32),
            pltpu.VMEM((3, canv, PX, CELLS), BF16),
            pltpu.VMEM((2, 3, canv, PX + 2 * CW, half), BF16),
        ],
        compiler_params=params(),
        name="dx",
        after=(send_bb,),
    )(flat, df, df_got, w_fx)
    grad_features = launch(
        functools.partial(grad_x_kernel, canv, box_count),
        grid=(canv,),
        in_specs=[
            SMEM_SPEC,
            whole(lanes.shape),
            whole(cells.shape),
            whole((rows, bw)),
            whole((rows, bw)),
            whole(w_branch.shape),
            pl.BlockSpec((PX, cin), lambda i: (i, 0)),
        ],
        out_specs=pl.BlockSpec((PX, cin), lambda i: (i, 0)),
        out_shape=shaped((pixels, cin), BF16),
        scratch_shapes=[pltpu.VMEM((canv, CELLS, cin), BF16)],
        compiler_params=params(),
        name="grad_x",
    )(flat, lanes, cells, dz, dz_got, w_branch, dx)

    small = db_total[:2]
    small_got = swap(small)
    small_all = jnp.concatenate([jnp.where(chan == 0, small, small_got), jnp.where(chan == 0, small_got, small)], 1)
    placed = jnp.zeros((mid, ncls), F32)
    grad_w_cls = lax.psum(lax.dynamic_update_slice_in_dim(placed, dw_cls, chan * half, 0), ("dp", "chan"))
    return (
        logits,
        grad_features,
        out_br,
        da_total[:4],
        da_total[4:],
        out_fx,
        out_fb,
        small_all[0],
        small_all[1],
        grad_w_cls,
        db_total[2, :ncls],
    )


def solution(mesh):
    return jax.shard_map(
        per_device,
        mesh=mesh,
        in_specs=(
            P("dp", "chan"),
            P("dp", None, None),
            P(None, "chan", None),
            P(None, "chan"),
            P(None, "chan"),
            P(None, "chan", None),
            P(None, None, "chan", None),
            P(),
            P(),
            P(),
            P(),
            P("dp", None),
        ),
        out_specs=(
            P("dp", None),
            P("dp", "chan"),
            P(None, "chan", "dp"),
            P(None, "chan"),
            P(None, "chan"),
            P(None, "chan", "dp"),
            P(None, None, "chan", "dp"),
            P(),
            P(),
            P(),
            P(),
        ),
        check_vma=False,
    )
```

```python
import functools

import jax
import jax.numpy as jnp
import numpy as np
from jax import lax
from jax.experimental import pallas as pl
from jax.experimental.pallas import tpu as pltpu
from jax.sharding import PartitionSpec as P

CH = 16
CW = 32
PX = CH * CW
EPS = 1e-05
BINS = (1, 2, 3, 6)
CELLS = 128
PLANE = 4
F32 = jnp.float32
BF16 = jnp.bfloat16
MESH = pl.DeviceIdType.MESH
VMEM_SPEC = pl.BlockSpec(memory_space=pltpu.VMEM)
SMEM_SPEC = pl.BlockSpec(memory_space=pltpu.SMEM)
ANY_SPEC = pl.BlockSpec(memory_space=pl.ANY)
NT = (((1,), (1,)), ((), ()))
TN = (((0,), (0,)), ((), ()))


COST_UNIT = 1_000_000_000
COSTS = {
    "pool": 12, "branch_sums": 2, "branch_act": 2, "join": 42, "join_sums": 4, "head": 5, "join_grad": 5,
    "branch_back": 16, "branch_dz": 2, "lifts": 10, "wgrad_fb": 15, "wgrad_fx0": 24, "wgrad_fx1": 24, "wgrad_br": 6,
    "dx": 33, "grad_x": 9,
}


def params(**extra):
    return pltpu.CompilerParams(vmem_limit_bytes=56 * 2**20, **extra)


def dot(a, b):
    return jnp.dot(a, b, preferred_element_type=F32)


def dot_nt(a, b):
    return lax.dot_general(a, b, NT, preferred_element_type=F32)


def dot_tn(a, b):
    return lax.dot_general(a, b, TN, preferred_element_type=F32)


def cell_table(box_count):
    table = np.zeros((8, CELLS), np.float32)
    table[1] = 1.0
    table[4] = 9.0
    at = 0
    for level, bins in enumerate(BINS):
        for box in range(box_count):
            for i in range(bins):
                for j in range(bins):
                    table[:6, at] = (box, bins, i, j, level, 1.0)
                    at += 1
    return table


def box_at(boxes_ref, canvas, box, box_count):
    base = (canvas * box_count + box) * 4
    return [boxes_ref[base + part] for part in range(4)]


def by_box(boxes_ref, canvas, which, box_count):
    sides = None
    for box in range(box_count):
        mine = [side.astype(F32) for side in box_at(boxes_ref, canvas, box, box_count)]
        if sides is None:
            sides = [jnp.full(which.shape, side, F32) for side in mine]
        else:
            sides = [jnp.where(which == box, new, old) for new, old in zip(mine, sides)]
    return sides


def within(relative, extent):
    return (relative >= 0) & (relative < extent)


def pixel_gates(boxes_ref, canvas, box_count, shape, axis):
    place = lax.broadcasted_iota(jnp.int32, shape, axis)
    row = place >> 5
    col = place & (CW - 1)
    rel = []
    for box in range(box_count):
        top, left, height, width = box_at(boxes_ref, canvas, box, box_count)
        rel.append((row - top, col - left, height, width))

    def gate(dy, dx):
        total = None
        for y, x, height, width in rel:
            hit = within(y, height) & within(x, width)
            if not isinstance(dy, int) or dy:
                hit = hit & within(y + dy, height)
            if not isinstance(dx, int) or dx:
                hit = hit & within(x + dx, width)
            value = jnp.where(hit, 1.0, 0.0)
            total = value if total is None else total + value
        return total

    return gate


def wide(column_block, times):
    return jnp.concatenate([column_block] * times, axis=1)


def rows_down(boxes_ref, canvas, box_count, x_ref, xs, at):
    gate = pixel_gates(boxes_ref, canvas, box_count, (PX, CELLS), 0)
    reps = xs.shape[2] // CELLS
    blank = jnp.zeros((CW, xs.shape[2]), BF16)
    up = wide(gate(-1, 0).astype(BF16), reps)
    down = wide(gate(1, 0).astype(BF16), reps)
    xs[0, at : at + CW] = blank
    xs[0, at + CW : at + PX] = x_ref[at : at + PX - CW] * up[CW:]
    xs[1, at : at + PX] = x_ref[at : at + PX] * wide(gate(0, 0).astype(BF16), reps)
    xs[2, at : at + PX - CW] = x_ref[at + CW : at + PX] * down[: PX - CW]
    xs[2, at + PX - CW : at + PX] = blank


def member_bounds(table_at, height, width):
    bins, i, j = table_at(1), table_at(2), table_at(3)

    def start(at, extent):
        return jnp.floor((at * extent + 0.5) / bins)

    def stop(at, extent):
        return jnp.floor(((at + 1) * extent + bins - 0.5) / bins)

    return start(i, height), stop(i, height), start(j, width), stop(j, width)


def members(boxes_ref, canvas, box_count, table_at, shape, axis):
    top, left, height, width = by_box(boxes_ref, canvas, table_at(0), box_count)
    r0, r1, c0, c1 = member_bounds(table_at, height, width)
    place = lax.broadcasted_iota(jnp.int32, shape, axis)
    row = (place >> 5).astype(F32) - top
    col = (place & (CW - 1)).astype(F32) - left
    hit = (row >= r0) & (row < r1) & (col >= c0) & (col < c1) & (table_at(5) > 0)
    return jnp.where(hit, 1.0, 0.0), (r1 - r0) * (c1 - c0)


def gated_lifts(boxes_ref, canvas, box_count, lanes_ref, store):
    def table_at(row):
        return lanes_ref[row : row + 1, :]

    top, left, height, width = by_box(boxes_ref, canvas, table_at(0), box_count)

    def side(size, edge, extent, cell):
        relative = lax.broadcasted_iota(jnp.int32, (size, CELLS), 0).astype(F32) - edge
        scale = (table_at(1) - 1.0) / (extent - 1.0)
        own = within(relative, extent)
        found = []
        for step in (-1, 0, 1):
            moved = relative + step
            weight = jnp.maximum(0.0, 1.0 - jnp.abs(moved * scale - cell))
            found.append(jnp.where(own & within(moved, extent), weight, 0.0))
        return found

    rows = [found * table_at(5) for found in side(CH, top, height, table_at(2))]
    cols = side(CW, left, width, table_at(3))
    for d in range(9):
        for y in range(CH):
            store(d, y, (rows[d // 3][y : y + 1] * cols[d % 3]).astype(BF16))


def pltranspose(block):
    return jnp.transpose(block, (1, 0))


def pool_kernel(canv, box_count, boxes_ref, lanes_ref, cells_ref, x_ref, w_ref, pooled_ref, lift_ref, own_ref, send_ref, first_ref, last_ref, kept, zs):
    n = pl.program_id(0)
    span = first_ref.shape[1]
    first_ref[...] = x_ref[:, :span]
    last_ref[...] = x_ref[:, span:]

    def table_at(row):
        return cells_ref[:, row : row + 1]

    select, count = members(boxes_ref, n, box_count, table_at, (CELLS, PX), 1)
    pooled = (dot(select.astype(BF16), x_ref[...]) / count).astype(BF16)
    pooled_ref[...] = pooled
    kept[pl.ds(pl.multiple_of(n * CELLS, CELLS), CELLS), :] = pooled

    def store(d, y, block):
        lift_ref[0, y * CW : (y + 1) * CW, d * CELLS : (d + 1) * CELLS] = block

    gated_lifts(boxes_ref, n, box_count, lanes_ref, store)

    @pl.when(n == canv - 1)
    def _():
        half = own_ref.shape[1]
        for level in range(4):
            part = dot(kept[...], w_ref[level])
            for m in range(canv):
                rows = slice(m * CELLS, (m + 1) * CELLS)
                mine = jnp.where(table_at(4) == level, part[rows], 0.0)
                zs[rows, :] = mine if level == 0 else zs[rows, :] + mine
        chan = lax.axis_index("chan")
        own_ref[...] = zs[:, pl.ds(pl.multiple_of(chan * half, half), half)]
        send_ref[...] = zs[:, pl.ds(pl.multiple_of((1 - chan) * half, half), half)].astype(BF16)


def branch_sums_kernel(canv, cells_ref, own_ref, got_ref, z_ref, part_ref):
    z = own_ref[...] + got_ref[...].astype(F32)
    z_ref[...] = z
    for level in range(4):
        first = second = 0.0
        for n in range(canv):
            mine = jnp.where(cells_ref[:, 4:5] == level, z[n * CELLS : (n + 1) * CELLS], 0.0)
            first = first + jnp.sum(mine, 0, keepdims=True)
            second = second + jnp.sum(mine * mine, 0, keepdims=True)
        part_ref[level : level + 1, :] = first
        part_ref[4 + level : 5 + level, :] = second


def exchange_kernel(total, own_ref, out_ref, slots, send_sem, recv_sem):
    me = lax.axis_index("dp")
    chan = lax.axis_index("chan")
    barrier = pltpu.get_barrier_semaphore()

    def signal(step, carry):
        pl.semaphore_signal(barrier, inc=1, device_id=(lax.rem(me + step, total), chan), device_id_type=MESH)
        return carry

    lax.fori_loop(1, total, signal, 0)
    slots[me] = own_ref[...]
    pl.semaphore_wait(barrier, total - 1)

    def copy_to(step):
        return pltpu.make_async_remote_copy(
            src_ref=own_ref,
            dst_ref=slots.at[me],
            send_sem=send_sem.at[step],
            recv_sem=recv_sem.at[me],
            device_id=(lax.rem(me + step, total), chan),
            device_id_type=MESH,
        )

    def copy_from(step):
        other = lax.rem(me + total - step, total)
        return pltpu.make_async_remote_copy(
            src_ref=own_ref,
            dst_ref=slots.at[other],
            send_sem=send_sem.at[step],
            recv_sem=recv_sem.at[other],
            device_id=(other, chan),
            device_id_type=MESH,
        )

    def start(step, carry):
        copy_to(step).start()
        return carry

    def finish(step, carry):
        copy_from(step).wait_recv()
        return carry

    def sent(step, carry):
        copy_to(step).wait_send()
        return carry

    lax.fori_loop(1, total, start, 0)
    lax.fori_loop(1, total, finish, 0)
    lax.fori_loop(1, total, sent, 0)
    value = slots[0]
    for other in range(1, total):
        value = value + slots[other]
    out_ref[...] = value


def dp_sum(part, total, number, after=()):
    return launch(
        functools.partial(exchange_kernel, total),
        after=after,
        out_shape=jax.ShapeDtypeStruct(part.shape, F32),
        in_specs=[VMEM_SPEC],
        out_specs=VMEM_SPEC,
        scratch_shapes=[
            pltpu.VMEM((total,) + part.shape, F32),
            pltpu.SemaphoreType.DMA((total,)),
            pltpu.SemaphoreType.DMA((total,)),
        ],
        compiler_params=pltpu.CompilerParams(collective_id=number, has_side_effects=True),
        name="dp_sum%d" % number,
    )(part)


def branch_stat(total_ref, level, rows_all):
    mean = total_ref[level : level + 1, :] / rows_all
    var = total_ref[4 + level : 5 + level, :] / rows_all - mean * mean
    return mean, lax.rsqrt(var + EPS)


def branch_act_kernel(canv, rows_all, cells_ref, z_ref, total_ref, gain_ref, bias_ref, y_ref, norm_ref, act_ref):
    for n in range(canv):
        rows = slice(n * CELLS, (n + 1) * CELLS)
        z = z_ref[rows]
        norm = act = 0.0
        for level in range(4):
            mean, rstd = branch_stat(total_ref, level, rows_all[level])
            here = jnp.where(cells_ref[:, 4:5] == level, 1.0, 0.0)
            mine = (z - mean) * rstd
            norm = norm + here * mine
            act = act + here * (gain_ref[level : level + 1, :] * mine + bias_ref[level : level + 1, :])
        norm_ref[rows] = norm
        act_ref[rows] = act
        y_ref[rows] = (act * jax.nn.sigmoid(act)).astype(BF16)

def expand(y, cells_ref, keep):
    width = y.shape[1]
    for n in range(y.shape[0] // CELLS):
        rows = slice(n * CELLS, (n + 1) * CELLS)
        block = y[rows].astype(F32)
        for level in range(4):
            mine = jnp.where(cells_ref[:, 4:5] == level, block, 0.0)
            keep[rows, level * width : (level + 1) * width] = mine.astype(BF16)


def join_kernel(canv, box_count, boxes_ref, cells_ref, x_ref, y_ref, lift_ref, wfx_ref, wfb_ref, own_ref, send_ref, xs, ye, terms, f):
    t = pl.program_id(0)
    mid = wfx_ref.shape[3]
    reps = mid // CELLS

    @pl.when(t == 0)
    def _():
        expand(y_ref[...], cells_ref, ye)
        for n in range(canv):
            rows_down(boxes_ref, n, box_count, x_ref, xs, n * PX)

    for n in range(canv):
        rows = slice(n * PX, (n + 1) * PX)
        q = dot(xs[0, rows], wfx_ref[0, 0]) + dot(xs[1, rows], wfx_ref[1, 0]) + dot(xs[2, rows], wfx_ref[2, 0])
        gate = wide(pixel_gates(boxes_ref, n, box_count, (PX, CELLS), 0)(0, t - 1), reps)
        q = gate * pltpu.roll(q, (PX + 1 - t) % PX, 0)

        @pl.when(t == 0)
        def _():
            f[n] = q

        @pl.when(t > 0)
        def _():
            f[n] += q

    for dy in range(3):
        term = dot(ye[...], wfb_ref[dy, 0].reshape(ye.shape[1], mid)).astype(BF16)
        for n in range(canv):
            terms[n, pl.ds(pl.multiple_of((dy * 3 + t) * CELLS, CELLS), CELLS)] = term[n * CELLS : (n + 1) * CELLS]

    @pl.when(t == 2)
    def _():
        half = own_ref.shape[1]
        chan = lax.axis_index("chan")
        for n in range(canv):
            f[n] += dot(lift_ref[n], terms[n])
            rows = slice(n * PX, (n + 1) * PX)
            own_ref[rows] = f[n, :, pl.ds(pl.multiple_of(chan * half, half), half)]
            send_ref[rows] = f[n, :, pl.ds(pl.multiple_of((1 - chan) * half, half), half)].astype(BF16)


def join_sums_kernel(canv, box_count, boxes_ref, own_ref, got_ref, f_ref, part_ref):
    n = pl.program_id(0)
    f = own_ref[...] + got_ref[...].astype(F32)
    f_ref[...] = f

    @pl.when(n == 0)
    def _():
        part_ref[...] = jnp.zeros_like(part_ref)

    area = 0
    for box in range(box_count):
        side = box_at(boxes_ref, n, box, box_count)
        area = area + side[2] * side[3]
    part_ref[0:1, :] += jnp.sum(f, 0, keepdims=True)
    part_ref[1:2, :] += jnp.sum(f * f, 0, keepdims=True)
    part_ref[2:3, :] += jnp.full((1, f.shape[1]), area.astype(F32), F32)


def join_stat(total_ref):
    count = total_ref[2:3, :]
    mean = total_ref[0:1, :] / count
    var = total_ref[1:2, :] / count - mean * mean
    return mean, lax.rsqrt(var + EPS), count


def head_kernel(box_count, boxes_ref, f_ref, total_ref, gain_ref, bias_ref, w_ref, g_ref, score_ref, db_ref, part_ref, dw_ref):
    n = pl.program_id(0)
    half = f_ref.shape[1]
    chan = lax.axis_index("chan")
    w = w_ref[pl.ds(pl.multiple_of(chan * half, half), half), :]
    own = pl.ds(pl.multiple_of(chan * half, half), half)
    valid = wide(pixel_gates(boxes_ref, n, box_count, (PX, CELLS), 0)(0, 0), half // CELLS)
    mean, rstd, _ = join_stat(total_ref)
    norm = (f_ref[...] - mean) * rstd
    act = gain_ref[:, own] * norm + bias_ref[:, own]
    sig = jax.nn.sigmoid(act)
    hidden = (act * sig * valid).astype(BF16)
    g = g_ref[...]
    score_ref[...] = dot(hidden, w).astype(BF16)
    db = dot_nt(g, w) * valid * sig * (1.0 + act * (1.0 - sig))
    db_ref[...] = db

    @pl.when(n == 0)
    def _():
        part_ref[...] = jnp.zeros_like(part_ref)
        dw_ref[...] = jnp.zeros_like(dw_ref)

    part_ref[0:1, :] += jnp.sum(db * norm, 0, keepdims=True)
    part_ref[1:2, :] += jnp.sum(db, 0, keepdims=True)
    part_ref[2:3, : g.shape[1]] += jnp.sum(g.astype(F32), 0, keepdims=True)
    dw_ref[...] += dot_tn(hidden, g)


def split_rows(rows, groups, each, own_a, send_a, own_b, send_b, send_d=None):
    me = lax.axis_index("dp")
    x_bit = me % 2
    y_bit = (me // 2) % 2

    def piece(group, y, x):
        return rows[pl.ds(pl.multiple_of(((group * 2 + y) * 2 + x) * each, each), each), :].astype(BF16)

    for group in range(groups):
        for bit in range(2):
            at = (bit * groups + group) * each
            own_a[at : at + each] = piece(group, bit, x_bit)
            send_a[at : at + each] = piece(group, bit, 1 - x_bit)
            own_b[at : at + each] = piece(group, y_bit, bit)
            send_b[at : at + each] = piece(group, 1 - y_bit, bit)
        if send_d is not None:
            send_d[group * each : (group + 1) * each] = piece(group, 1 - y_bit, 1 - x_bit)


def join_grad_kernel(box_count, each, boxes_ref, f_ref, db_ref, total_ref, sums_ref, gain_ref, df_ref, pack_ref, send_a, send_b, send_d, flip):
    n = pl.program_id(0)
    half = f_ref.shape[1]
    own = pl.ds(pl.multiple_of(lax.axis_index("chan") * half, half), half)
    valid = wide(pixel_gates(boxes_ref, n, box_count, (PX, CELLS), 0)(0, 0), half // CELLS)
    mean, rstd, count = join_stat(total_ref)
    norm = (f_ref[...] - mean) * rstd
    df = gain_ref[:, own] * rstd * (db_ref[...] - sums_ref[1:2, :] / count - norm * (sums_ref[0:1, :] / count)) * valid
    df_ref[...] = df.astype(BF16)
    flip[...] = pltranspose(df)
    pack_ref[0:half] = flip[...].astype(BF16)
    own_a = pack_ref.at[half : half + half // 2]
    own_b = pack_ref.at[half + half // 2 : 2 * half]
    split_rows(flip, half // (4 * each), each, own_a, send_a, own_b, send_b, send_d)


def branch_back_kernel(canv, cells_ref, lanes_ref, own_ref, got_ref, lift_ref, w_ref, norm_ref, act_ref, da_ref, part_ref, acc, grads):
    d = pl.program_id(0)
    half = own_ref.shape[0]
    chan = lax.axis_index("chan")

    @pl.when(d == 0)
    def _():
        for ref, which in ((own_ref, chan), (got_ref, 1 - chan)):
            for n in range(canv):
                found = dot(ref[:, n * PX : (n + 1) * PX], lift_ref[n]).astype(BF16)
                for e in range(9):
                    into = pl.ds(pl.multiple_of(which * half, half), half)
                    grads[e, into, n * CELLS : (n + 1) * CELLS] = found[:, e * CELLS : (e + 1) * CELLS]

    part = dot(w_ref[0].reshape(acc.shape[0], 2 * half), grads[d])

    @pl.when(d == 0)
    def _():
        acc[...] = part

    @pl.when(d > 0)
    def _():
        acc[...] += part

    @pl.when(d == 8)
    def _():
        width = norm_ref.shape[1]
        levels = jnp.concatenate([lanes_ref[4:5, :]] * canv, axis=1)
        dy = 0.0
        for level in range(4):
            dy = dy + jnp.where(levels == level, acc[level * width : (level + 1) * width], 0.0)
        dy = pltranspose(dy)
        act = act_ref[...]
        sig = jax.nn.sigmoid(act)
        da = dy * sig * (1.0 + act * (1.0 - sig))
        da_ref[...] = da
        for level in range(4):
            gain = bias = 0.0
            for n in range(canv):
                rows = slice(n * CELLS, (n + 1) * CELLS)
                mine = jnp.where(cells_ref[:, 4:5] == level, da[rows], 0.0)
                gain = gain + jnp.sum(mine * norm_ref[rows], 0, keepdims=True)
                bias = bias + jnp.sum(mine, 0, keepdims=True)
            part_ref[level : level + 1, :] = gain
            part_ref[4 + level : 5 + level, :] = bias


def branch_dz_kernel(canv, rows_all, each, cells_ref, da_ref, norm_ref, total_ref, sums_ref, gain_ref, dz_ref, pack_ref, send_a, send_b, flip):
    for n in range(canv):
        rows = slice(n * CELLS, (n + 1) * CELLS)
        dz = 0.0
        for level in range(4):
            _, rstd = branch_stat(total_ref, level, rows_all[level])
            here = jnp.where(cells_ref[:, 4:5] == level, 1.0, 0.0)
            mean_gain = sums_ref[level : level + 1, :] / rows_all[level]
            mean_bias = sums_ref[4 + level : 5 + level, :] / rows_all[level]
            mine = gain_ref[level : level + 1, :] * rstd * (da_ref[rows] - mean_bias - norm_ref[rows] * mean_gain)
            dz = dz + here * mine
        dz_ref[rows] = dz.astype(BF16)
        flip[:, rows] = pltranspose(dz)
    half = flip.shape[0]
    split_rows(flip, half // (4 * each), each, pack_ref.at[0 : half // 2], send_a, pack_ref.at[half // 2 : half], send_b)


def put_rows(out, index, own_ref, other_ref):
    chan = lax.axis_index("chan")
    size = own_ref.shape[0]
    width = own_ref.shape[1]
    for ref, which in ((own_ref, chan), (other_ref, 1 - chan)):
        out[index, pl.ds(pl.multiple_of(which * size, size), size), :width] = ref[...]


def cols_across(boxes_ref, canvas, at, box_count, own_ref, other_ref, lhs):
    chan = lax.axis_index("chan")
    size = own_ref.shape[0]
    span = slice(at * PX, (at + 1) * PX)
    gate = pixel_gates(boxes_ref, canvas, box_count, (8, PX), 1)
    for ref, which in ((own_ref, chan), (other_ref, 1 - chan)):
        into = pl.ds(pl.multiple_of(which * size, size), size)
        value = ref[:, span].astype(F32)
        lhs[0, into, span] = (pltpu.roll(value, PX - 1, 1) * gate(0, 1)[0:1]).astype(BF16)
        lhs[1, into, span] = ref[:, span]
        lhs[2, into, span] = (pltpu.roll(value, 1, 1) * gate(0, -1)[0:1]).astype(BF16)


def split_out(count, bit, acc, keep, send):
    parts, _, each, _ = keep.shape
    groups = parts // 2
    block = groups * each

    def one(d, carry):
        for half in range(2):
            for ref, which in ((keep, bit), (send, 1 - bit)):
                for group in range(groups):
                    at = (half * 2 + which) * block + group * each
                    ref[half * groups + group, d] = acc[d, pl.ds(pl.multiple_of(at, each), each), :].astype(BF16)
        return carry

    lax.fori_loop(0, count, one, 0)


def tail_kernel(
    canv, box_count,
    boxes_ref, lanes_ref, cells_ref, qa0, qa1, qb0, qb1, ga0, ga1, gb0, gb1, gd0, gd1, y_ref, pooled_ref,
    za0, za1, zb0, zb1, zga0, zga1, zgb0, zgb1, dz0, dz1, df0, df1, x_any, xm_any, ym_any, wfx_any, wbr_any,
    gx_ref, out_fx, out_fb, out_br,
    lhs4, lift, grads, xbuf, wbuf, xd, lhs, acc, pool_mate, kept,
    fb_send, fb_recv, keep_a, send_a, recv_a, zrecv_a, keep_b, send_b, recv_b, zrecv_b,
    bkeep_a, bsend_a, brecv_a, bzrecv_a, bkeep_b, bsend_b, brecv_b, bzrecv_b,
    load_sem, w_sem, mate_send, mate_recv, part_send, part_recv,
):
    me = lax.axis_index("dp")
    chan = lax.axis_index("chan")
    parts = fb_send.shape[0]
    pixels = df0.shape[0]
    half = df0.shape[1]
    span = xbuf.shape[2]
    group, place = me // PLANE, me % PLANE
    x_bit, y_bit = me % 2, (me // 2) % 2
    x_mate = me + 1 - 2 * x_bit
    y_mate = me + 2 - 4 * y_bit

    def peer(step):
        return lax.rem(group + step, parts) * PLANE + place

    barrier = pltpu.get_barrier_semaphore()
    for other in [x_mate, y_mate] + [peer(step) for step in range(1, parts)]:
        pl.semaphore_signal(barrier, inc=1, device_id=(other, chan), device_id_type=MESH)

    def load(source, slot, which):
        return pltpu.make_async_copy(source, xbuf.at[slot], load_sem.at[which])

    loads = [
        load(x_any.at[:, pl.ds(0, span)], 0, 0),
        load(xm_any, 1, 1),
        load(x_any.at[:, pl.ds(span, span)], 0, 2),
        load(ym_any, 1, 3),
    ]
    loads[0].start()
    loads[1].start()

    def tile_load(tile):
        width = wbuf.shape[1]
        return pltpu.make_async_copy(
            wfx_any.at[:, pl.ds(pl.multiple_of(tile * width, width), width), :],
            wbuf.at[pl.ds(pl.multiple_of(lax.rem(tile, 2) * 9, 9), 9)],
            w_sem.at[lax.rem(tile, 2)],
        )

    tile_load(0).start()

    def mate_copy(number, source, target, mate):
        return pltpu.make_async_remote_copy(
            src_ref=source, dst_ref=target, send_sem=mate_send.at[number], recv_sem=mate_recv.at[number],
            device_id=(mate, chan), device_id_type=MESH,
        )

    def part_copy(number, step, source, target):
        return pltpu.make_async_remote_copy(
            src_ref=source.at[lax.rem(group + step, parts)], dst_ref=target.at[step - 1],
            send_sem=part_send.at[number * (parts - 1) + step - 1], recv_sem=part_recv.at[number * (parts - 1) + step - 1],
            device_id=(peer(step), chan), device_id_type=MESH,
        )

    ye = gx_ref
    expand(y_ref[...], cells_ref, ye)
    size = gd0.shape[0]
    for source, (own_ref, oth_ref, bit) in enumerate(((qa0, qa1, y_bit), (ga0, ga1, y_bit), (gb0, gb1, x_bit), (gd0, gd1, 0))):
        mine = pl.ds(pl.multiple_of(bit * size, size), size)
        put_rows(lhs4, source, own_ref.at[mine], oth_ref.at[mine])

    def canvas(n, carry):
        def store(d, y, block):
            lift[y * CW : (y + 1) * CW, d * CELLS : (d + 1) * CELLS] = block

        gated_lifts(boxes_ref, n, box_count, lanes_ref, store)
        rows = lhs4[n // canv, :, pl.ds(pl.multiple_of((n % canv) * PX, PX), PX)]
        found = dot(rows, lift[...]).astype(BF16)
        for d in range(9):
            grads[d, :, pl.ds(pl.multiple_of(n * CELLS, CELLS), CELLS)] = found[:, d * CELLS : (d + 1) * CELLS]
        return carry

    lax.fori_loop(0, PLANE * canv, canvas, 0)
    each = fb_send.shape[2]
    for d in range(9):
        result = dot(grads[d], ye[...])
        for part in range(parts):
            fb_send[part, d] = result[part * each : (part + 1) * each].astype(BF16)
    pl.semaphore_wait(barrier, parts + 1)
    fb_copies = [part_copy(0, step, fb_send, fb_recv) for step in range(1, parts)]
    for copy in fb_copies:
        copy.start()

    mate_copies = []
    sides = (
        (0, ((0, qa0, qa1, 0), (1, ga0, ga1, 1)), y_bit, keep_a, send_a, recv_a, y_mate),
        (1, ((0, qb0, qb1, 0), (2, gb0, gb1, 1)), x_bit, keep_b, send_b, recv_b, x_mate),
    )
    for side, sources, bit, keep, send, recv, mate in sides:
        for number, (device, own_ref, oth_ref, slot) in enumerate(sources):
            loads[2 * side + slot].wait()
            for n in range(canv):
                rows_down(boxes_ref, device * canv + n, box_count, xbuf.at[slot], xd, n * PX)
                cols_across(boxes_ref, device * canv + n, n, box_count, own_ref, oth_ref, lhs)
                if number:
                    select, count = members(
                        boxes_ref, device * canv + n, box_count, lambda row: cells_ref[:, row : row + 1], (CELLS, PX), 1
                    )
                    sums = dot(select.astype(BF16), xbuf[slot, n * PX : (n + 1) * PX])
                    pool_mate[side, n * CELLS : (n + 1) * CELLS] = (sums / count).astype(BF16)
            if side == 0:
                loads[2 + slot].start()
            for d in range(9):
                part = dot(lhs[d % 3], xd[d // 3])
                acc[d] = part if number == 0 else acc[d] + part
        split_out(9, bit, acc, keep, send)
        mate_copies.append(mate_copy(side, send, recv, mate))
        mate_copies[-1].start()

    levels = jnp.concatenate([lanes_ref[4:5, :]] * canv, axis=1)
    rows = canv * CELLS
    sides = (
        (0, za0, za1, zga0, zga1, y_bit, bkeep_a, bsend_a, brecv_a, y_mate),
        (1, zb0, zb1, zgb0, zgb1, x_bit, bkeep_b, bsend_b, brecv_b, x_mate),
    )
    for side, own0, oth0, own1, oth1, bit, keep, send, recv, mate in sides:
        put_rows(lhs, 0, own0, oth0)
        put_rows(lhs, 1, own1, oth1)
        for level in range(4):
            left = [jnp.where(levels == level, lhs[k, :, :rows].astype(F32), 0.0).astype(BF16) for k in range(2)]
            acc[level] = dot(left[0], pooled_ref[:, side * span : (side + 1) * span]) + dot(left[1], pool_mate[side])
        split_out(4, bit, acc, keep, send)
        mate_copies.append(mate_copy(2 + side, send, recv, mate))
        mate_copies[-1].start()

    part_copies = []

    def pass_on(number, keep, recv, target):
        mate_copies[number].wait_recv()

        def add(d, carry):
            for part in range(parts):
                keep[part, d] = (keep[part, d].astype(F32) + recv[part, d].astype(F32)).astype(BF16)
            return carry

        lax.fori_loop(0, keep.shape[1], add, 0)
        for step in range(1, parts):
            part_copies.append(part_copy(1 + number, step, keep, target))
            part_copies[-1].start()

    for n in range(canv):
        gate = pixel_gates(boxes_ref, n, box_count, (PX, CELLS), 0)
        at = slice(n * PX, (n + 1) * PX)
        for which, ref in ((chan, df0), (1 - chan, df1)):
            into = pl.ds(pl.multiple_of(which * half, half), half)
            df = ref[at].astype(F32)
            xd[1, at, into] = ref[at]
            xd[0, at, into] = (wide(gate(0, 1), half // CELLS) * pltpu.roll(df, PX - 1, 0)).astype(BF16)
            xd[2, at, into] = (wide(gate(0, -1), half // CELLS) * pltpu.roll(df, 1, 0)).astype(BF16)

    width = wbuf.shape[1]
    tiles = wfx_any.shape[1] // width

    def tile(t, carry):
        tile_load(t).wait()

        @pl.when(t + 1 < tiles)
        def _():
            tile_load(t + 1).start()

        first = lax.rem(t, 2) * 9
        for n in range(canv):
            at = slice(n * PX, (n + 1) * PX)
            gate = pixel_gates(boxes_ref, n, box_count, (PX, CELLS), 0)
            total = None
            for dy in range(3):
                part = dot_nt(xd[0, at], wbuf[first + dy * 3])
                for dx in range(1, 3):
                    part = part + dot_nt(xd[dx, at], wbuf[first + dy * 3 + dx])
                if dy != 1:
                    part = wide(gate(1 - dy, 0), width // CELLS) * pltpu.roll(part, ((dy - 1) * CW) % PX, 0)
                total = part if total is None else total + part
            gx_ref[at, pl.ds(pl.multiple_of(t * width, width), width)] = total.astype(BF16)
        return carry

    lax.fori_loop(0, 1, tile, 0)
    pass_on(0, keep_a, recv_a, zrecv_a)
    lax.fori_loop(1, 3, tile, 0)
    pass_on(1, keep_b, recv_b, zrecv_b)
    lax.fori_loop(3, tiles, tile, 0)

    wbr_load = pltpu.make_async_copy(wbr_any, wbuf.at[pl.ds(0, wbr_any.shape[0])], load_sem.at[4])
    wbr_load.start()
    wbr_load.wait()
    per_level = wbr_any.shape[0] // 4
    total = 0.0
    for level in range(4):
        w = wbuf[level * per_level : (level + 1) * per_level].reshape(per_level * width, 2 * half)
        mine = []
        for which, ref in ((0, dz0), (1, dz1)):
            blocks = [
                jnp.where(cells_ref[:, 4:5] == level, ref[m * CELLS : (m + 1) * CELLS].astype(F32), 0.0).astype(BF16)
                for m in range(canv)
            ]
            mine.append(jnp.concatenate(blocks, axis=0))
        first = jnp.where(chan == 0, mine[0].astype(F32), mine[1].astype(F32)).astype(BF16)
        last = jnp.where(chan == 0, mine[1].astype(F32), mine[0].astype(F32)).astype(BF16)
        total = total + dot_nt(jnp.concatenate([first, last], axis=1), w)
    for m in range(canv):
        _, _, high, across = by_box(boxes_ref, m, cells_ref[:, 0:1], box_count)
        r0, r1, c0, c1 = member_bounds(lambda row: cells_ref[:, row : row + 1], high, across)
        kept[m] = (total[m * CELLS : (m + 1) * CELLS] / ((r1 - r0) * (c1 - c0))).astype(BF16)
    for n in range(canv):
        at = slice(n * PX, (n + 1) * PX)
        select, _ = members(boxes_ref, n, box_count, lambda row: lanes_ref[row : row + 1, :], (PX, CELLS), 0)
        gx_ref[at] = (gx_ref[at].astype(F32) + dot(select.astype(BF16), kept[n])).astype(BF16)

    pass_on(2, bkeep_a, brecv_a, bzrecv_a)
    pass_on(3, bkeep_b, brecv_b, bzrecv_b)

    def finish(copies, keep, recv, out, spot):
        for copy in copies:
            copy.wait_recv()

        def add(d, carry):
            total = keep[group, d].astype(F32)
            for step in range(parts - 1):
                total = total + recv[step, d].astype(F32)
            out[d, :, spot] = total
            return carry

        lax.fori_loop(0, out.shape[0], add, 0)

    first, last = slice(0, span), slice(span, 2 * span)
    steps = parts - 1
    finish(fb_copies, fb_send, fb_recv, out_fb, slice(0, out_fb.shape[2]))
    finish(part_copies[:steps], keep_a, zrecv_a, out_fx, first)
    finish(part_copies[steps : 2 * steps], keep_b, zrecv_b, out_fx, last)
    finish(part_copies[2 * steps : 3 * steps], bkeep_a, bzrecv_a, out_br, first)
    finish(part_copies[3 * steps :], bkeep_b, bzrecv_b, out_br, last)
    for copy in fb_copies + mate_copies + part_copies:
        copy.wait_send()


def launch(kernel, in_specs, after=(), through=(), **rest):
    used = len(in_specs)
    extra = len(after) + len(through)
    if through:
        outs = len(rest["out_specs"])
        rest["out_specs"] = list(rest["out_specs"]) + [ANY_SPEC] * len(through)
        rest["out_shape"] = list(rest["out_shape"]) + [jax.ShapeDtypeStruct(a.shape, a.dtype) for a in through]
        rest["input_output_aliases"] = {used + len(after) + i: outs + i for i in range(len(through))}
        after = tuple(after) + tuple(through)
    else:
        outs = 0

    def body(*refs):
        refs = refs[:used] + refs[used + extra :]
        kernel(*(refs[: used + outs] + refs[used + outs + len(through) :] if through else refs))

    cost = pl.CostEstimate(flops=COST_UNIT * COSTS.get(rest["name"], 10), bytes_accessed=0, transcendentals=0)
    call = pl.pallas_call(body, cost_estimate=cost, in_specs=list(in_specs) + [ANY_SPEC] * extra, **rest)
    return lambda *operands: call(*operands, *after)


def whole(shape):
    return pl.BlockSpec(shape, lambda i: (0,) * len(shape))


def shaped(shape, kind):
    return jax.ShapeDtypeStruct(shape, kind)


def per_device(features, boxes, w_branch, gain_branch, bias_branch, w_fx, w_fb, gain_join, bias_join, w_cls, b_cls, grad_logits):
    canv, box_count = boxes.shape[:2]
    pixels, cin = features.shape
    mid = gain_join.shape[0]
    half = mid // lax.axis_size("chan")
    bw = gain_branch.shape[1]
    br = w_branch.shape[2]
    ncls = w_cls.shape[1]
    dp = lax.axis_size("dp")
    parts = dp // PLANE
    each = mid // dp
    cols = parts * each
    rows = canv * CELLS
    chan = lax.axis_index("chan")
    me = lax.axis_index("dp")
    rows_all = [float(canv * dp * box_count * s * s) for s in BINS]
    lanes_np = cell_table(box_count)
    lanes = jnp.asarray(lanes_np)
    cells = jnp.asarray(np.concatenate([lanes_np.T, np.zeros((CELLS, CELLS - 8), np.float32)], 1))

    def to_mate(array, mate):
        return lax.ppermute(array, "dp", [(i, i ^ mate) for i in range(dp)])

    def swap(array):
        return lax.ppermute(array, "chan", [(0, 1), (1, 0)])

    flat = boxes.reshape(-1)
    flat_of = [flat] + [to_mate(flat, m) for m in (1, 2, 3)]
    flat_all = jnp.concatenate(flat_of)

    pooled, lifts, z_own, z_send, x_first, x_last = launch(
        functools.partial(pool_kernel, canv, box_count),
        grid=(canv,),
        in_specs=[
            SMEM_SPEC,
            whole(lanes.shape),
            whole(cells.shape),
            pl.BlockSpec((PX, cin), lambda i: (i, 0)),
            whole(w_branch.shape),
        ],
        out_specs=[
            pl.BlockSpec((CELLS, cin), lambda i: (i, 0)),
            pl.BlockSpec((1, PX, 9 * CELLS), lambda i: (i, 0, 0)),
            whole((rows, bw)),
            whole((rows, bw)),
            pl.BlockSpec((PX, cin // 2), lambda i: (i, 0)),
            pl.BlockSpec((PX, cin // 2), lambda i: (i, 0)),
        ],
        out_shape=[
            shaped((rows, cin), BF16),
            shaped((canv, PX, 9 * CELLS), BF16),
            shaped((rows, bw), F32),
            shaped((rows, bw), BF16),
            shaped((pixels, cin // 2), BF16),
            shaped((pixels, cin // 2), BF16),
        ],
        scratch_shapes=[pltpu.VMEM((rows, cin), BF16), pltpu.VMEM((rows, br), F32)],
        compiler_params=params(),
        name="pool",
    )(flat, lanes, cells, features, w_branch)
    z_got = swap(z_send)
    z, z_part = launch(
        functools.partial(branch_sums_kernel, canv),
        in_specs=[VMEM_SPEC] * 3,
        out_specs=[VMEM_SPEC] * 2,
        out_shape=[shaped((rows, bw), F32), shaped((8, bw), F32)],
        compiler_params=params(),
        name="branch_sums",
    )(cells, z_own, z_got)
    z_total = dp_sum(z_part, dp, 0)
    y, z_norm, z_act, x_first, x_last = launch(
        functools.partial(branch_act_kernel, canv, rows_all),
        through=(x_first, x_last),
        in_specs=[VMEM_SPEC] * 5,
        out_specs=[VMEM_SPEC] * 3,
        out_shape=[shaped((rows, bw), BF16), shaped((rows, bw), F32), shaped((rows, bw), F32)],
        compiler_params=params(),
        name="branch_act",
    )(cells, z, z_total, gain_branch, bias_branch)
    x_mate = to_mate(x_first, 1)
    y_mate = to_mate(x_last, 2)
    y_all = jnp.concatenate([y] + [to_mate(y, m) for m in (1, 2, 3)], 0)

    f_own, f_send = launch(
        functools.partial(join_kernel, canv, box_count),
        grid=(3,),
        in_specs=[
            SMEM_SPEC,
            whole(cells.shape),
            whole((pixels, cin)),
            whole((rows, bw)),
            whole((canv, PX, 9 * CELLS)),
            pl.BlockSpec((3, 1, cin, mid), lambda i: (0, i, 0, 0)),
            pl.BlockSpec((3, 1, 4, bw, mid), lambda i: (0, i, 0, 0, 0)),
        ],
        out_specs=[whole((pixels, half)), whole((pixels, half))],
        out_shape=[shaped((pixels, half), F32), shaped((pixels, half), BF16)],
        scratch_shapes=[
            pltpu.VMEM((3, pixels, cin), BF16),
            pltpu.VMEM((rows, 4 * bw), BF16),
            pltpu.VMEM((canv, 9 * CELLS, mid), BF16),
            pltpu.VMEM((canv, PX, mid), F32),
        ],
        compiler_params=params(),
        name="join",
    )(flat, cells, features, y, lifts, w_fx.reshape(3, 3, cin, mid), w_fb.reshape(3, 3, 4, bw, mid))
    f_got = swap(f_send)
    by_canvas = pl.BlockSpec((PX, half), lambda i: (i, 0))
    f, f_part = launch(
        functools.partial(join_sums_kernel, canv, box_count),
        grid=(canv,),
        in_specs=[SMEM_SPEC, by_canvas, by_canvas],
        out_specs=[by_canvas, whole((8, half))],
        out_shape=[shaped((pixels, half), F32), shaped((8, half), F32)],
        compiler_params=params(),
        name="join_sums",
        after=(x_mate, y_mate, y_all),
    )(flat, f_own, f_got)
    f_total = dp_sum(f_part, dp, 1)
    gain_row = gain_join.reshape(1, mid)
    bias_row = bias_join.reshape(1, mid)
    score, db, db_part, dw_cls = launch(
        functools.partial(head_kernel, box_count),
        grid=(canv,),
        in_specs=[
            SMEM_SPEC,
            by_canvas,
            whole((8, half)),
            whole((1, mid)),
            whole((1, mid)),
            whole((mid, ncls)),
            pl.BlockSpec((PX, ncls), lambda i: (i, 0)),
        ],
        out_specs=[pl.BlockSpec((PX, ncls), lambda i: (i, 0)), by_canvas, whole((8, half)), whole((half, ncls))],
        out_shape=[
            shaped((pixels, ncls), BF16),
            shaped((pixels, half), F32),
            shaped((8, half), F32),
            shaped((half, ncls), F32),
        ],
        compiler_params=params(),
        name="head",
    )(flat, f, f_total, gain_row, bias_row, w_cls, grad_logits)
    db_total = dp_sum(db_part, dp, 2)
    logits = (score.astype(F32) + swap(score).astype(F32) + b_cls).astype(BF16)
    quarter = half // 2
    df, pack, send_a, send_b, send_d = launch(
        functools.partial(join_grad_kernel, box_count, each),
        grid=(canv,),
        in_specs=[SMEM_SPEC, by_canvas, by_canvas, whole((8, half)), whole((8, half)), whole((1, mid))],
        out_specs=[by_canvas]
        + [pl.BlockSpec((size, PX), lambda i: (0, i)) for size in (2 * half, quarter, quarter, quarter // 2)],
        out_shape=[shaped((pixels, half), BF16)]
        + [shaped((size, pixels), BF16) for size in (2 * half, quarter, quarter, quarter // 2)],
        scratch_shapes=[pltpu.VMEM((half, PX), F32)],
        compiler_params=params(),
        name="join_grad",
    )(flat, f, db, f_total, db_total, gain_row)
    got_a, got_b, got_d = to_mate(send_a, 1), to_mate(send_b, 2), to_mate(send_d, 3)
    pack_other = swap(pack)
    df_got = swap(df)
    other_a, other_b, other_d = swap(got_a), swap(got_b), swap(got_d)
    half_rows = pl.BlockSpec((half, pixels), lambda i: (0, 0))

    da, da_part = launch(
        functools.partial(branch_back_kernel, canv),
        grid=(9,),
        in_specs=[
            whole(cells.shape),
            whole(lanes.shape),
            half_rows,
            half_rows,
            whole((canv, PX, 9 * CELLS)),
            pl.BlockSpec((1, 4, bw, mid), lambda i: (i, 0, 0, 0)),
            whole((rows, bw)),
            whole((rows, bw)),
        ],
        out_specs=[whole((rows, bw)), whole((8, bw))],
        out_shape=[shaped((rows, bw), F32), shaped((8, bw), F32)],
        scratch_shapes=[pltpu.VMEM((4 * bw, rows), F32), pltpu.VMEM((9, mid, rows), BF16)],
        compiler_params=params(),
        name="branch_back",
    )(cells, lanes, pack, pack_other, lifts, w_fb, z_norm, z_act)
    da_total = dp_sum(da_part, dp, 3, (other_a, other_b, other_d))
    dz, zpack, zsend_a, zsend_b = launch(
        functools.partial(branch_dz_kernel, canv, rows_all, each),
        in_specs=[VMEM_SPEC] * 6,
        out_specs=[VMEM_SPEC] * 4,
        out_shape=[
            shaped((rows, bw), BF16),
            shaped((bw, rows), BF16),
            shaped((quarter, rows), BF16),
            shaped((quarter, rows), BF16),
        ],
        scratch_shapes=[pltpu.VMEM((bw, rows), F32)],
        compiler_params=params(),
        name="branch_dz",
    )(cells, da, z_norm, z_total, da_total, gain_branch)
    zgot_a, zgot_b = to_mate(zsend_a, 1), to_mate(zsend_b, 2)
    dz_got, zpack_other, zother_a, zother_b = swap(dz), swap(zpack), swap(zgot_a), swap(zgot_b)

    span = cin // 2
    bundle = quarter // 2
    tile = cin // 4

    def quarter_at(at):
        return pl.BlockSpec((quarter, pixels), lambda i: (at, 0))

    def zquarter_at(at):
        return pl.BlockSpec((quarter, rows), lambda i: (at, 0))

    def buffers(count, width):
        return [
            pltpu.VMEM((parts, count, each, width), BF16),
            pltpu.VMEM((parts, count, each, width), BF16),
            pltpu.VMEM((parts, count, each, width), BF16),
            pltpu.VMEM((parts - 1, count, each, width), BF16),
        ]

    grad_features, sum_fx, sum_fb, sum_br = launch(
        functools.partial(tail_kernel, canv, box_count),
        grid=(1,),
        in_specs=[
            SMEM_SPEC,
            whole(lanes.shape),
            whole(cells.shape),
            quarter_at(2),
            quarter_at(2),
            quarter_at(3),
            quarter_at(3),
        ]
        + [whole((quarter, pixels))] * 4
        + [whole((bundle, pixels))] * 2
        + [whole((PLANE * rows, bw)), whole((rows, cin))]
        + [zquarter_at(0), zquarter_at(0), zquarter_at(1), zquarter_at(1)]
        + [whole((quarter, rows))] * 4
        + [whole((rows, bw))] * 2
        + [whole((pixels, half))] * 2
        + [ANY_SPEC] * 5,
        out_specs=[
            whole((pixels, cin)),
            whole((9, each, cin)),
            whole((9, each, 4 * bw)),
            whole((4, each, cin)),
        ],
        out_shape=[
            shaped((pixels, cin), BF16),
            shaped((9, each, cin), F32),
            shaped((9, each, 4 * bw), F32),
            shaped((4, each, cin), F32),
        ],
        scratch_shapes=[
            pltpu.VMEM((PLANE, cols, pixels), BF16),
            pltpu.VMEM((PX, 9 * CELLS), BF16),
            pltpu.VMEM((9, cols, PLANE * rows), BF16),
            pltpu.VMEM((2, pixels, span), BF16),
            pltpu.VMEM((18, tile, mid), BF16),
            pltpu.VMEM((3, pixels, mid), BF16),
            pltpu.VMEM((3, half, pixels), BF16),
            pltpu.VMEM((9, half, span), F32),
            pltpu.VMEM((2, rows, span), BF16),
            pltpu.VMEM((canv, CELLS, cin), BF16),
            pltpu.VMEM((parts, 9, each, 4 * bw), BF16),
            pltpu.VMEM((parts - 1, 9, each, 4 * bw), BF16),
        ]
        + buffers(9, span)
        + buffers(9, span)
        + buffers(4, span)
        + buffers(4, span)
        + [
            pltpu.SemaphoreType.DMA((5,)),
            pltpu.SemaphoreType.DMA((2,)),
            pltpu.SemaphoreType.DMA((4,)),
            pltpu.SemaphoreType.DMA((4,)),
            pltpu.SemaphoreType.DMA((5 * (parts - 1),)),
            pltpu.SemaphoreType.DMA((5 * (parts - 1),)),
        ],
        compiler_params=pltpu.CompilerParams(vmem_limit_bytes=62 * 2**20, collective_id=4, has_side_effects=True),
        name="tail",
    )(
        flat_all, lanes, cells, pack, pack_other, pack, pack_other, got_a, other_a, got_b, other_b, got_d, other_d,
        y_all, pooled, zpack, zpack_other, zpack, zpack_other, zgot_a, zother_a, zgot_b, zother_b, dz, dz_got, df, df_got,
        features, x_mate, y_mate, w_fx, w_branch.reshape(16, tile, br),
    )
    out_fx = jnp.transpose(sum_fx, (0, 2, 1))
    out_fb = jnp.transpose(sum_fb.reshape(9, each, 4, bw), (0, 2, 3, 1))
    out_br = jnp.transpose(sum_br, (0, 2, 1))

    small = db_total[:2]
    small_got = swap(small)
    small_all = jnp.concatenate([jnp.where(chan == 0, small, small_got), jnp.where(chan == 0, small_got, small)], 1)
    placed = jnp.zeros((mid, ncls), F32)
    grad_w_cls = lax.psum(lax.dynamic_update_slice_in_dim(placed, dw_cls, chan * half, 0), ("dp", "chan"))
    return (
        logits,
        grad_features,
        out_br,
        da_total[:4],
        da_total[4:],
        out_fx,
        out_fb,
        small_all[0],
        small_all[1],
        grad_w_cls,
        db_total[2, :ncls],
    )


def solution(mesh):
    return jax.shard_map(
        per_device,
        mesh=mesh,
        in_specs=(
            P("dp", "chan"),
            P("dp", None, None),
            P(None, "chan", None),
            P(None, "chan"),
            P(None, "chan"),
            P(None, "chan", None),
            P(None, None, "chan", None),
            P(),
            P(),
            P(),
            P(),
            P("dp", None),
        ),
        out_specs=(
            P("dp", None),
            P("dp", "chan"),
            P(None, "chan", "dp"),
            P(None, "chan"),
            P(None, "chan"),
            P(None, "chan", "dp"),
            P(None, None, "chan", "dp"),
            P(),
            P(),
            P(),
            P(),
        ),
        check_vma=False,
    )
```

```python
import functools

import jax
import jax.numpy as jnp
import numpy as np
from jax import lax
from jax.experimental import pallas as pl
from jax.experimental.pallas import tpu as pltpu
from jax.sharding import PartitionSpec as P

CH = 16
CW = 32
PX = CH * CW
EPS = 1e-05
BINS = (1, 2, 3, 6)
CELLS = 128
PLANE = 4
F32 = jnp.float32
BF16 = jnp.bfloat16
MESH = pl.DeviceIdType.MESH
VMEM_SPEC = pl.BlockSpec(memory_space=pltpu.VMEM)
SMEM_SPEC = pl.BlockSpec(memory_space=pltpu.SMEM)
ANY_SPEC = pl.BlockSpec(memory_space=pl.ANY)
NT = (((1,), (1,)), ((), ()))
TN = (((0,), (0,)), ((), ()))


COST_UNIT = 1_000_000_000
COSTS = {
    "pool": 12, "branch_sums": 2, "branch_act": 2, "join": 42, "join_sums": 4, "head": 5, "join_grad": 5,
    "branch_back": 16, "branch_dz": 2, "lifts": 10, "wgrad_fb": 15, "wgrad_fx0": 24, "wgrad_fx1": 24, "wgrad_br": 6,
    "dx": 33, "grad_x": 9,
}


def params(**extra):
    return pltpu.CompilerParams(vmem_limit_bytes=56 * 2**20, **extra)


def dot(a, b):
    return jnp.dot(a, b, preferred_element_type=F32)


def dot_nt(a, b):
    return lax.dot_general(a, b, NT, preferred_element_type=F32)


def dot_tn(a, b):
    return lax.dot_general(a, b, TN, preferred_element_type=F32)


def cell_table(box_count):
    table = np.zeros((8, CELLS), np.float32)
    table[1] = 1.0
    table[4] = 9.0
    at = 0
    for level, bins in enumerate(BINS):
        for box in range(box_count):
            for i in range(bins):
                for j in range(bins):
                    table[:6, at] = (box, bins, i, j, level, 1.0)
                    at += 1
    return table


def box_at(boxes_ref, canvas, box, box_count):
    base = (canvas * box_count + box) * 4
    return [boxes_ref[base + part] for part in range(4)]


def by_box(boxes_ref, canvas, which, box_count):
    sides = None
    for box in range(box_count):
        mine = [side.astype(F32) for side in box_at(boxes_ref, canvas, box, box_count)]
        if sides is None:
            sides = [jnp.full(which.shape, side, F32) for side in mine]
        else:
            sides = [jnp.where(which == box, new, old) for new, old in zip(mine, sides)]
    return sides


def within(relative, extent):
    return (relative >= 0) & (relative < extent)


def pixel_gates(boxes_ref, canvas, box_count, shape, axis):
    place = lax.broadcasted_iota(jnp.int32, shape, axis)
    row = place >> 5
    col = place & (CW - 1)
    rel = []
    for box in range(box_count):
        top, left, height, width = box_at(boxes_ref, canvas, box, box_count)
        rel.append((row - top, col - left, height, width))

    def gate(dy, dx):
        total = None
        for y, x, height, width in rel:
            hit = within(y, height) & within(x, width)
            if not isinstance(dy, int) or dy:
                hit = hit & within(y + dy, height)
            if not isinstance(dx, int) or dx:
                hit = hit & within(x + dx, width)
            value = jnp.where(hit, 1.0, 0.0)
            total = value if total is None else total + value
        return total

    return gate


def wide(column_block, times):
    return jnp.concatenate([column_block] * times, axis=1)


def rows_down(boxes_ref, canvas, box_count, x_ref, xs, n):
    gate = pixel_gates(boxes_ref, canvas, box_count, (PX, CELLS), 0)
    canv = xs.shape[0] // 3
    reps = xs.shape[2] // CELLS
    blank = jnp.zeros((CW, xs.shape[2]), BF16)
    up = wide(gate(-1, 0).astype(BF16), reps)
    down = wide(gate(1, 0).astype(BF16), reps)
    at = n * PX
    xs[n, 0:CW] = blank
    xs[n, CW:PX] = x_ref[at : at + PX - CW] * up[CW:]
    xs[canv + n] = x_ref[at : at + PX] * wide(gate(0, 0).astype(BF16), reps)
    xs[2 * canv + n, 0 : PX - CW] = x_ref[at + CW : at + PX] * down[: PX - CW]
    xs[2 * canv + n, PX - CW : PX] = blank


def member_bounds(table_at, height, width):
    bins, i, j = table_at(1), table_at(2), table_at(3)

    def start(at, extent):
        return jnp.floor((at * extent + 0.5) / bins)

    def stop(at, extent):
        return jnp.floor(((at + 1) * extent + bins - 0.5) / bins)

    return start(i, height), stop(i, height), start(j, width), stop(j, width)


def members(boxes_ref, canvas, box_count, table_at, shape, axis):
    top, left, height, width = by_box(boxes_ref, canvas, table_at(0), box_count)
    r0, r1, c0, c1 = member_bounds(table_at, height, width)
    place = lax.broadcasted_iota(jnp.int32, shape, axis)
    row = (place >> 5).astype(F32) - top
    col = (place & (CW - 1)).astype(F32) - left
    hit = (row >= r0) & (row < r1) & (col >= c0) & (col < c1) & (table_at(5) > 0)
    return jnp.where(hit, 1.0, 0.0), (r1 - r0) * (c1 - c0)


def gated_lifts(boxes_ref, canvas, box_count, lanes_ref, store):
    def table_at(row):
        return lanes_ref[row : row + 1, :]

    top, left, height, width = by_box(boxes_ref, canvas, table_at(0), box_count)

    def side(size, edge, extent, cell):
        relative = lax.broadcasted_iota(jnp.int32, (size, CELLS), 0).astype(F32) - edge
        scale = (table_at(1) - 1.0) / (extent - 1.0)
        own = within(relative, extent)
        found = []
        for step in (-1, 0, 1):
            moved = relative + step
            weight = jnp.maximum(0.0, 1.0 - jnp.abs(moved * scale - cell))
            found.append(jnp.where(own & within(moved, extent), weight, 0.0))
        return found

    rows = [found * table_at(5) for found in side(CH, top, height, table_at(2))]
    cols = side(CW, left, width, table_at(3))
    for d in range(9):
        for y in range(CH):
            store(d, y, (rows[d // 3][y : y + 1] * cols[d % 3]).astype(BF16))


def pltranspose(block):
    return jnp.transpose(block, (1, 0))


def pool_kernel(canv, box_count, boxes_ref, lanes_ref, cells_ref, x_ref, w_ref, pooled_ref, lift_ref, own_ref, send_ref, first_ref, last_ref, kept, zs):
    n = pl.program_id(0)
    span = first_ref.shape[1]
    first_ref[...] = x_ref[:, :span]
    last_ref[...] = x_ref[:, span:]

    def table_at(row):
        return cells_ref[:, row : row + 1]

    select, count = members(boxes_ref, n, box_count, table_at, (CELLS, PX), 1)
    pooled = (dot(select.astype(BF16), x_ref[...]) / count).astype(BF16)
    pooled_ref[...] = pooled
    kept[pl.ds(pl.multiple_of(n * CELLS, CELLS), CELLS), :] = pooled

    def store(d, y, block):
        lift_ref[0, y * CW : (y + 1) * CW, d * CELLS : (d + 1) * CELLS] = block

    gated_lifts(boxes_ref, n, box_count, lanes_ref, store)

    @pl.when(n == canv - 1)
    def _():
        half = own_ref.shape[1]
        for level in range(4):
            part = dot(kept[...], w_ref[level])
            for m in range(canv):
                rows = slice(m * CELLS, (m + 1) * CELLS)
                mine = jnp.where(table_at(4) == level, part[rows], 0.0)
                zs[rows, :] = mine if level == 0 else zs[rows, :] + mine
        chan = lax.axis_index("chan")
        own_ref[...] = zs[:, pl.ds(pl.multiple_of(chan * half, half), half)]
        send_ref[...] = zs[:, pl.ds(pl.multiple_of((1 - chan) * half, half), half)].astype(BF16)


def branch_sums_kernel(canv, cells_ref, own_ref, got_ref, z_ref, part_ref):
    z = own_ref[...] + got_ref[...].astype(F32)
    z_ref[...] = z
    for level in range(4):
        first = second = 0.0
        for n in range(canv):
            mine = jnp.where(cells_ref[:, 4:5] == level, z[n * CELLS : (n + 1) * CELLS], 0.0)
            first = first + jnp.sum(mine, 0, keepdims=True)
            second = second + jnp.sum(mine * mine, 0, keepdims=True)
        part_ref[level : level + 1, :] = first
        part_ref[4 + level : 5 + level, :] = second


def signal_all(total, chan_too=False):
    me = lax.axis_index("dp")
    chan = lax.axis_index("chan")
    barrier = pltpu.get_barrier_semaphore()

    def signal(step, carry):
        pl.semaphore_signal(barrier, inc=1, device_id=(lax.rem(me + step, total), chan), device_id_type=MESH)
        return carry

    lax.fori_loop(1, total, signal, 0)
    if chan_too:
        pl.semaphore_signal(barrier, inc=1, device_id=(me, 1 - chan), device_id_type=MESH)
    return total if chan_too else total - 1


class Exchange:
    def __init__(self, total, own, slots, send_sem, recv_sem, parted=False):
        self.total, self.own, self.slots, self.send_sem, self.recv_sem = total, own, slots, send_sem, recv_sem
        self.me = lax.axis_index("dp")
        self.parted = parted

    def block(self, device):
        return self.own.at[device] if self.parted else self.own

    def copy_to(self, step):
        return pltpu.make_async_remote_copy(
            src_ref=self.block(lax.rem(self.me + step, self.total)),
            dst_ref=self.slots.at[self.me],
            send_sem=self.send_sem.at[step],
            recv_sem=self.recv_sem.at[self.me],
            device_id=(lax.rem(self.me + step, self.total), lax.axis_index("chan")),
            device_id_type=MESH,
        )

    def copy_from(self, step):
        other = lax.rem(self.me + self.total - step, self.total)
        return pltpu.make_async_remote_copy(
            src_ref=self.block(other),
            dst_ref=self.slots.at[other],
            send_sem=self.send_sem.at[step],
            recv_sem=self.recv_sem.at[other],
            device_id=(other, lax.axis_index("chan")),
            device_id_type=MESH,
        )

    def start(self):
        self.slots[self.me] = self.block(self.me)[...]

        def one(step, carry):
            self.copy_to(step).start()
            return carry

        lax.fori_loop(1, self.total, one, 0)

    def arrive(self):
        def one(step, carry):
            self.copy_from(step).wait_recv()
            return carry

        def sent(step, carry):
            self.copy_to(step).wait_send()
            return carry

        lax.fori_loop(1, self.total, one, 0)
        lax.fori_loop(1, self.total, sent, 0)

    def finish(self):
        self.arrive()
        value = self.slots[0]
        for other in range(1, self.total):
            value = value + self.slots[other]
        return value


def exchange_kernel(total, own_ref, out_ref, slots, send_sem, recv_sem):
    expected = signal_all(total)
    pl.semaphore_wait(pltpu.get_barrier_semaphore(), expected)
    exchange = Exchange(total, own_ref, slots, send_sem, recv_sem)
    exchange.start()
    out_ref[...] = exchange.finish()


def exchange_scratch(total, width, times):
    return [
        pltpu.VMEM((times, 8, width), F32),
        pltpu.VMEM((times, total, 8, width), F32),
        pltpu.SemaphoreType.DMA((times, total)),
        pltpu.SemaphoreType.DMA((times, total)),
    ]


def core_copy(source, target, send_sem, recv_sem):
    return pltpu.make_async_remote_copy(
        src_ref=source,
        dst_ref=target,
        send_sem=send_sem,
        recv_sem=recv_sem,
        device_id=(lax.axis_index("dp"), 1 - lax.axis_index("chan")),
        device_id_type=MESH,
    )


def dp_sum(part, total, number, after=()):
    return launch(
        functools.partial(exchange_kernel, total),
        after=after,
        out_shape=jax.ShapeDtypeStruct(part.shape, F32),
        in_specs=[VMEM_SPEC],
        out_specs=VMEM_SPEC,
        scratch_shapes=[
            pltpu.VMEM((total,) + part.shape, F32),
            pltpu.SemaphoreType.DMA((total,)),
            pltpu.SemaphoreType.DMA((total,)),
        ],
        compiler_params=pltpu.CompilerParams(collective_id=number, has_side_effects=True),
        name="dp_sum%d" % number,
    )(part)


def branch_stat(total_ref, level, rows_all):
    mean = total_ref[level : level + 1, :] / rows_all
    var = total_ref[4 + level : 5 + level, :] / rows_all - mean * mean
    return mean, lax.rsqrt(var + EPS)


def branch_act_kernel(canv, rows_all, cells_ref, z_ref, total_ref, gain_ref, bias_ref, y_ref, norm_ref, act_ref):
    for n in range(canv):
        rows = slice(n * CELLS, (n + 1) * CELLS)
        z = z_ref[rows]
        norm = act = 0.0
        for level in range(4):
            mean, rstd = branch_stat(total_ref, level, rows_all[level])
            here = jnp.where(cells_ref[:, 4:5] == level, 1.0, 0.0)
            mine = (z - mean) * rstd
            norm = norm + here * mine
            act = act + here * (gain_ref[level : level + 1, :] * mine + bias_ref[level : level + 1, :])
        norm_ref[rows] = norm
        act_ref[rows] = act
        y_ref[rows] = (act * jax.nn.sigmoid(act)).astype(BF16)

def expand(y, cells_ref, keep):
    width = y.shape[1]
    for n in range(y.shape[0] // CELLS):
        rows = slice(n * CELLS, (n + 1) * CELLS)
        block = y[rows].astype(F32)
        for level in range(4):
            mine = jnp.where(cells_ref[:, 4:5] == level, block, 0.0)
            keep[rows, level * width : (level + 1) * width] = mine.astype(BF16)


def join_kernel(canv, box_count, boxes_ref, cells_ref, x_ref, y_ref, lift_ref, wfx_ref, wfb_ref, own_ref, send_ref, xs, ye, terms, f):
    t = pl.program_id(0)
    mid = wfx_ref.shape[3]
    reps = mid // CELLS

    @pl.when(t == 0)
    def _():
        expand(y_ref[...], cells_ref, ye)
        for n in range(canv):
            rows_down(boxes_ref, n, box_count, x_ref, xs, n)

    for n in range(canv):
        q = dot(xs[n], wfx_ref[0, 0]) + dot(xs[canv + n], wfx_ref[1, 0]) + dot(xs[2 * canv + n], wfx_ref[2, 0])
        gate = pixel_gates(boxes_ref, n, box_count, (PX, CELLS), 0)

        @pl.when(t == 0)
        def _():
            f[n] = wide(gate(0, -1), reps) * pltpu.roll(q, 1, 0)

        @pl.when(t == 1)
        def _():
            f[n] += q

        @pl.when(t == 2)
        def _():
            f[n] += wide(gate(0, 1), reps) * pltpu.roll(q, PX - 1, 0)

    for dy in range(3):
        term = dot(ye[...], wfb_ref[dy, 0].reshape(ye.shape[1], mid)).astype(BF16)
        for n in range(canv):
            terms[n, pl.ds(pl.multiple_of((dy * 3 + t) * CELLS, CELLS), CELLS)] = term[n * CELLS : (n + 1) * CELLS]

    @pl.when(t == 2)
    def _():
        half = own_ref.shape[1]
        chan = lax.axis_index("chan")
        for n in range(canv):
            f[n] += dot(lift_ref[n], terms[n])
            rows = slice(n * PX, (n + 1) * PX)
            own_ref[rows] = f[n, :, pl.ds(pl.multiple_of(chan * half, half), half)]
            send_ref[rows] = f[n, :, pl.ds(pl.multiple_of((1 - chan) * half, half), half)].astype(BF16)


def head_kernel(
    canv, box_count, total, each,
    boxes_ref, own_ref, send_ref, gain_ref, bias_ref, w_ref, bcls_ref, g_ref,
    logits_ref, df_ref, pack_ref, send_a, send_b, send_d, dw_ref, sums_ref,
    dw, got, f, db, score, score_got, flip, part, slots, send_sem, recv_sem, core_send, core_recv,
):
    half = own_ref.shape[1]
    ncls = g_ref.shape[1]
    chan = lax.axis_index("chan")
    own = pl.ds(pl.multiple_of(chan * half, half), half)
    expected = signal_all(total, True)
    pl.semaphore_wait(pltpu.get_barrier_semaphore(), expected)
    swap_f = core_copy(send_ref, got, core_send.at[0], core_recv.at[0])
    swap_f.start()
    part[...] = jnp.zeros_like(part)
    dw[...] = jnp.zeros_like(dw)
    area = 0
    for n in range(canv):
        for box in range(box_count):
            side = box_at(boxes_ref, n, box, box_count)
            area = area + side[2] * side[3]
    part[0, 2:3, :] = jnp.full((1, half), area.astype(F32), F32)
    swap_f.wait()
    for n in range(canv):
        rows = slice(n * PX, (n + 1) * PX)
        value = own_ref[rows] + got[rows].astype(F32)
        f[rows] = value
        part[0, 0:1, :] += jnp.sum(value, 0, keepdims=True)
        part[0, 1:2, :] += jnp.sum(value * value, 0, keepdims=True)
    first = Exchange(total, part.at[0], slots.at[0], send_sem.at[0], recv_sem.at[0])
    first.start()
    f_total = first.finish()
    count = f_total[2:3, :]
    mean = f_total[0:1, :] / count
    rstd = lax.rsqrt(f_total[1:2, :] / count - mean * mean + EPS)
    gain, bias, w = gain_ref[:, own], bias_ref[:, own], w_ref[own, :]
    valid = [wide(pixel_gates(boxes_ref, n, box_count, (PX, CELLS), 0)(0, 0), half // CELLS) for n in range(canv)]
    for n in range(canv):
        rows = slice(n * PX, (n + 1) * PX)
        norm = (f[rows] - mean) * rstd
        f[rows] = norm
        act = gain * norm + bias
        sig = jax.nn.sigmoid(act)
        hidden = (act * sig * valid[n]).astype(BF16)
        g = g_ref[rows]
        score[rows] = dot(hidden, w).astype(BF16)
        value = dot_nt(g, w) * valid[n] * sig * (1.0 + act * (1.0 - sig))
        db[rows] = value
        part[1, 0:1, :] += jnp.sum(value * norm, 0, keepdims=True)
        part[1, 1:2, :] += jnp.sum(value, 0, keepdims=True)
        part[1, 2:3, :ncls] += jnp.sum(g.astype(F32), 0, keepdims=True)
        dw[...] += dot_tn(hidden, g)
    second = Exchange(total, part.at[1], slots.at[1], send_sem.at[1], recv_sem.at[1])
    second.start()
    swap_score = core_copy(score, score_got, core_send.at[1], core_recv.at[1])
    swap_score.start()
    sums = second.finish()
    sums_ref[...] = sums
    scale = gain * rstd
    for n in range(canv):
        rows = slice(n * PX, (n + 1) * PX)
        df = scale * (db[rows] - sums[1:2, :] / count - f[rows] * (sums[0:1, :] / count)) * valid[n]
        df_ref[rows] = df.astype(BF16)
        flip[...] = pltranspose(df)
        span = pl.ds(n * PX, PX)
        pack_ref[0:half, span] = flip[...].astype(BF16)
        views = [pack_ref.at[half : half + half // 2, span], send_a.at[:, span]]
        views += [pack_ref.at[half + half // 2 : 2 * half, span], send_b.at[:, span], send_d.at[:, span]]
        split_rows(flip, half // (4 * each), each, *views)
    strip = dw_ref.shape[1]
    for device in range(total):
        dw_ref[device] = dw[device * strip : (device + 1) * strip]
    swap_score.wait()
    for n in range(canv):
        rows = slice(n * PX, (n + 1) * PX)
        both = score[rows].astype(F32) + score_got[rows].astype(F32)
        logits_ref[rows] = (both + bcls_ref[...]).astype(BF16)


def split_rows(rows, groups, each, own_a, send_a, own_b, send_b, send_d=None):
    me = lax.axis_index("dp")
    x_bit = me % 2
    y_bit = (me // 2) % 2

    def piece(group, y, x):
        return rows[pl.ds(pl.multiple_of(((group * 2 + y) * 2 + x) * each, each), each), :].astype(BF16)

    for group in range(groups):
        for bit in range(2):
            at = (bit * groups + group) * each
            own_a[at : at + each] = piece(group, bit, x_bit)
            send_a[at : at + each] = piece(group, bit, 1 - x_bit)
            own_b[at : at + each] = piece(group, y_bit, bit)
            send_b[at : at + each] = piece(group, 1 - y_bit, bit)
        if send_d is not None:
            send_d[group * each : (group + 1) * each] = piece(group, 1 - y_bit, 1 - x_bit)


def put_rows(out, index, own_ref, other_ref):
    chan = lax.axis_index("chan")
    size = own_ref.shape[0]
    width = own_ref.shape[1]
    for ref, which in ((own_ref, chan), (other_ref, 1 - chan)):
        into = pl.ds(pl.multiple_of(which * size, size), size)
        if index is None:
            out[into, :width] = ref[...]
        else:
            out[index, into, :width] = ref[...]


def cols_across(boxes_ref, canvas, at, box_count, own_ref, other_ref, lhs):
    chan = lax.axis_index("chan")
    size = own_ref.shape[0]
    span = slice(at * PX, (at + 1) * PX)
    gate = pixel_gates(boxes_ref, canvas, box_count, (8, PX), 1)
    for ref, which in ((own_ref, chan), (other_ref, 1 - chan)):
        into = pl.ds(pl.multiple_of(which * size, size), size)
        value = ref[:, span].astype(F32)
        lhs[0, into, span] = (pltpu.roll(value, PX - 1, 1) * gate(0, 1)[0:1]).astype(BF16)
        lhs[1, into, span] = ref[:, span]
        lhs[2, into, span] = (pltpu.roll(value, 1, 1) * gate(0, -1)[0:1]).astype(BF16)


def reversed_bits(number, bits):
    return sum(((number >> bit) & 1) << (bits - 1 - bit) for bit in range(bits))


def split_out(count, bit, acc, keep, send):
    parts, _, each, _ = keep.shape
    groups = parts // 2
    block = groups * each

    def one(d, carry):
        for half in range(2):
            for ref, which in ((keep, bit), (send, 1 - bit)):
                for group in range(groups):
                    at = (half * 2 + which) * block + group * each
                    ref[reversed_bits(half * groups + group, parts.bit_length() - 1), d] = acc[d, pl.ds(pl.multiple_of(at, each), each), :].astype(BF16)
        return carry

    lax.fori_loop(0, count, one, 0)


def tail_kernel(
    canv, box_count,
    total_dp, rows_all,
    boxes_ref, lanes_ref, cells_ref, pack0, sa, sb, sd, df0, y_ref, pooled_ref, norm_ref, act_ref, ztotal_ref, zgain_ref, dw_ref,
    x_any, xm_any, ym_any, wfx_any, wfb_any, wbr_any,
    gx_ref, out_fx, out_fb, out_br, sums_ref, dw_own, dw_other,
    dw_slots, dw_sum, dw_send, dw_recv, pack1, df1, ga0, ga1, gb0, gb1, gd0, gd1, zpack0, zpack1, zsa, zsb, zga0, zga1, zgb0, zgb1, dz0, dz1, da,
    part, slots, sum_send, sum_recv, core_send, core_recv, near_send, near_recv,
    lift, grads, xbuf, wbuf, xd, lhs, acc, pool_mate,
    fb_send, fb_recv, keep_a, send_a, recv_a, zrecv_a, keep_b, send_b, recv_b, zrecv_b,
    bkeep_a, bsend_a, brecv_a, bzrecv_a, bkeep_b, bsend_b, brecv_b, bzrecv_b,
    load_sem, store_sem, w_sem, fb_sem, mate_send, mate_recv, part_send, part_recv,
):
    me = lax.axis_index("dp")
    chan = lax.axis_index("chan")
    parts = fb_send.shape[0]
    pixels = df0.shape[0]
    half = df0.shape[1]
    span = xbuf.shape[2]
    group, place = me // PLANE, me % PLANE
    x_bit, y_bit = me % 2, (me // 2) % 2
    x_mate = me + 1 - 2 * x_bit
    y_mate = me + 2 - 4 * y_bit

    stages = parts.bit_length() - 1

    def group_bit(stage):
        return (group // 2**stage) % 2

    def group_mate(stage):
        return (group + 2**stage * (1 - 2 * group_bit(stage))) * PLANE + place

    d_mate = x_mate + y_mate - me
    expected = signal_all(total_dp, True)

    def load(source, slot, which):
        return pltpu.make_async_copy(source, xbuf.at[slot], load_sem.at[which])

    loads = [
        load(x_any.at[:, pl.ds(0, span)], 0, 0),
        load(xm_any, 1, 1),
        load(x_any.at[:, pl.ds(span, span)], 0, 2),
        load(ym_any, 1, 3),
    ]
    loads[0].start()
    loads[1].start()

    def tile_load(tile):
        width = wbuf.shape[1]
        return pltpu.make_async_copy(
            wfx_any.at[:, pl.ds(pl.multiple_of(tile * width, width), width), :],
            wbuf.at[pl.ds(pl.multiple_of(lax.rem(tile, 2) * 9, 9), 9)],
            w_sem.at[lax.rem(tile, 2)],
        )

    levels_at_once = wfb_any.shape[1]

    def fb_load(d):
        at = lax.rem(d, 4) * levels_at_once
        return pltpu.make_async_copy(wfb_any.at[d], wbuf.at[pl.ds(at, levels_at_once)], fb_sem.at[lax.rem(d, 4)])

    for d in range(3):
        fb_load(d).start()

    def mate_copy(number, source, target, mate):
        return pltpu.make_async_remote_copy(
            src_ref=source, dst_ref=target, send_sem=mate_send.at[number], recv_sem=mate_recv.at[number],
            device_id=(mate, chan), device_id_type=MESH,
        )

    class Halving:
        def __init__(self, number, keep, recv):
            self.number, self.keep, self.recv = number, keep, recv
            self.copies = []

        def kept(self, stage):
            at = 0
            for bit in range(stage):
                at = at + group_bit(bit) * (parts >> (bit + 1))
            return at

        def send(self):
            stage = len(self.copies)
            count = parts >> (stage + 1)
            from_at = self.kept(stage) + (1 - group_bit(stage)) * count
            number = self.number * stages + stage
            copy = pltpu.make_async_remote_copy(
                src_ref=self.keep.at[pl.ds(from_at, count)],
                dst_ref=self.recv.at[pl.ds(parts - 2 * count, count)],
                send_sem=part_send.at[number],
                recv_sem=part_recv.at[number],
                device_id=(group_mate(stage), chan),
                device_id_type=MESH,
            )
            copy.start()
            self.copies.append(copy)

        def receive(self):
            stage = len(self.copies)
            self.copies[-1].wait_recv()
            if stage == stages:
                return
            count = parts >> stage
            at = self.kept(stage)

            def add(d, carry):
                for part in range(count):
                    got = self.recv[parts - 2 * count + part, d].astype(F32)
                    self.keep[at + part, d] = (self.keep[at + part, d].astype(F32) + got).astype(BF16)
                return carry

            lax.fori_loop(0, self.keep.shape[1], add, 0)
            self.send()

    def near_copy(number, source, target, mate):
        return pltpu.make_async_remote_copy(
            src_ref=source, dst_ref=target, send_sem=near_send.at[number], recv_sem=near_recv.at[number],
            device_id=(mate, chan), device_id_type=MESH,
        )

    def swap_copy(number, source, target):
        return core_copy(source, target, core_send.at[number], core_recv.at[number])

    pl.semaphore_wait(pltpu.get_barrier_semaphore(), expected)
    swaps = [swap_copy(0, pack0, pack1), swap_copy(1, df0, df1)]
    near = [near_copy(0, sa, ga0, x_mate), near_copy(1, sb, gb0, y_mate), near_copy(2, sd, gd0, d_mate)]
    for copy in swaps + near:
        copy.start()
    dw_parts = Exchange(total_dp, dw_ref, dw_slots, dw_send.at[0], dw_recv.at[0], True)
    dw_parts.start()

    def lift_of(n):
        def store(d, y, block):
            lift[y * CW : (y + 1) * CW, d * CELLS : (d + 1) * CELLS] = block

        gated_lifts(boxes_ref, n, box_count, lanes_ref, store)

    rows = canv * CELLS
    for n in range(canv):
        lift_of(n)
        for ref, which in ((pack0, chan), (pack1, 1 - chan)):
            if n == 0 and ref is pack1:
                swaps[0].wait_recv()
            found = dot(ref[:half, n * PX : (n + 1) * PX], lift[...]).astype(BF16)
            into = pl.ds(pl.multiple_of(which * half, half), half)
            for e in range(9):
                xd[e, into, n * CELLS : (n + 1) * CELLS] = found[:, e * CELLS : (e + 1) * CELLS]

    def back(d, carry):
        fb_load(d).wait()

        @pl.when(d + 3 < 9)
        def _():
            fb_load(d + 3).start()

        for level in range(4):
            found = dot(wbuf[lax.rem(d, 4) * levels_at_once + level], xd[d, :, :rows])

            @pl.when(d == 0)
            def _():
                acc[level, :, :rows] = found

            @pl.when(d > 0)
            def _():
                acc[level, :, :rows] += found

        return carry

    lax.fori_loop(0, 9, back, 0)
    tile_load(0).start()
    levels = jnp.concatenate([lanes_ref[4:5, :]] * canv, axis=1)
    dy = 0.0
    for level in range(4):
        dy = dy + jnp.where(levels == level, acc[level, :, :rows], 0.0)
    dy = pltranspose(dy)
    sig = jax.nn.sigmoid(act_ref[...])
    da[...] = dy * sig * (1.0 + act_ref[...] * (1.0 - sig))
    for level in range(4):
        gain = bias = 0.0
        for n in range(canv):
            at = slice(n * CELLS, (n + 1) * CELLS)
            mine = jnp.where(cells_ref[:, 4:5] == level, da[at], 0.0)
            gain = gain + jnp.sum(mine * norm_ref[at], 0, keepdims=True)
            bias = bias + jnp.sum(mine, 0, keepdims=True)
        part[0, level : level + 1, :] = gain
        part[0, 4 + level : 5 + level, :] = bias
    exchange = Exchange(total_dp, part.at[0], slots.at[0], sum_send.at[0], sum_recv.at[0])
    exchange.start()
    dw_sum[...] = dw_parts.finish()
    dw_sums = Exchange(total_dp, dw_sum, dw_own, dw_send.at[1], dw_recv.at[1])
    dw_sums.start()
    for number, (source, target) in enumerate(((ga0, ga1), (gb0, gb1), (gd0, gd1))):
        near[number].wait_recv()
        swaps.append(swap_copy(2 + number, source, target))
        swaps[-1].start()
    for number in range(2, 5):
        swaps[number].wait_recv()

    half_a, half_b = half, half + half // 2
    qa0, qa1 = pack0.at[half_a:half_b], pack1.at[half_a:half_b]
    qb0, qb1 = pack0.at[half_b : 2 * half], pack1.at[half_b : 2 * half]
    ye = gx_ref
    expand(y_ref[...], cells_ref, ye)
    size = gd0.shape[0]
    cols = 2 * size
    for source, (own_ref, oth_ref, bit) in enumerate(((qa0, qa1, y_bit), (ga0, ga1, y_bit), (gb0, gb1, x_bit), (gd0, gd1, 0))):
        mine = pl.ds(pl.multiple_of(bit * size, size), size)
        put_rows(lhs.at[source // 2, source % 2 * cols : (source % 2 + 1) * cols], None, own_ref.at[mine], oth_ref.at[mine])

    def canvas(n, carry):
        lift_of(n)
        source = n // canv
        at = pl.ds(pl.multiple_of(lax.rem(source, 2) * cols, cols), cols)
        found = dot(lhs[source // 2, at, pl.ds(pl.multiple_of((n % canv) * PX, PX), PX)], lift[...]).astype(BF16)
        for d in range(9):
            grads[d, :, pl.ds(pl.multiple_of(n * CELLS, CELLS), CELLS)] = found[:, d * CELLS : (d + 1) * CELLS]
        return carry

    lax.fori_loop(0, PLANE * canv, canvas, 0)
    each = fb_send.shape[2]
    for d in range(9):
        result = dot(grads[d], ye[...])
        for part in range(parts):
            fb_send[reversed_bits(part, stages), d] = result[part * each : (part + 1) * each].astype(BF16)
    fb_way = Halving(0, fb_send, fb_recv)
    fb_way.send()

    sums = exchange.finish()
    sums_ref[...] = sums
    dw_sums.arrive()
    zflip = acc.at[4, :, 0:rows]
    for n in range(canv):
        at = slice(n * CELLS, (n + 1) * CELLS)
        dz = 0.0
        for level in range(4):
            _, rstd = branch_stat(ztotal_ref, level, rows_all[level])
            here = jnp.where(cells_ref[:, 4:5] == level, 1.0, 0.0)
            mean_gain = sums[level : level + 1, :] / rows_all[level]
            mean_bias = sums[4 + level : 5 + level, :] / rows_all[level]
            mine = zgain_ref[level : level + 1, :] * rstd * (da[at] - mean_bias - norm_ref[at] * mean_gain)
            dz = dz + here * mine
        dz0[at] = dz.astype(BF16)
        zflip[:, at] = pltranspose(dz)
    quarter = half // 2
    split_rows(zflip, half // (4 * each), each, zpack0.at[0:quarter], zsa, zpack0.at[quarter:half], zsb)
    swaps += [swap_copy(5, zpack0, zpack1), swap_copy(6, dz0, dz1)]
    dw_swap = swap_copy(9, dw_own, dw_other)
    dw_swap.start()
    near += [near_copy(3, zsa, zga0, x_mate), near_copy(4, zsb, zgb0, y_mate)]
    for copy in swaps[5:] + near[3:]:
        copy.start()

    mate_copies = []
    sides = (
        (0, ((0, qa0, qa1, 0), (1, ga0, ga1, 1)), y_bit, keep_a, send_a, recv_a, y_mate),
        (1, ((0, qb0, qb1, 0), (2, gb0, gb1, 1)), x_bit, keep_b, send_b, recv_b, x_mate),
    )
    for side, sources, bit, keep, send, recv, mate in sides:
        for number, (device, own_ref, oth_ref, slot) in enumerate(sources):
            loads[2 * side + slot].wait()
            for n in range(canv):
                rows_down(boxes_ref, device * canv + n, box_count, xbuf.at[slot], xd, n)
                cols_across(boxes_ref, device * canv + n, n, box_count, own_ref, oth_ref, lhs)
                if number:
                    select, count = members(
                        boxes_ref, device * canv + n, box_count, lambda row: cells_ref[:, row : row + 1], (CELLS, PX), 1
                    )
                    sums = dot(select.astype(BF16), xbuf[slot, n * PX : (n + 1) * PX])
                    pool_mate[side, n * CELLS : (n + 1) * CELLS] = (sums / count).astype(BF16)
            if side == 0:
                loads[2 + slot].start()
            for d in range(9):
                across = xd[d // 3 * canv : (d // 3 + 1) * canv].reshape(pixels, span)
                found = dot(lhs[d % 3], across)
                acc[d] = found if number == 0 else acc[d] + found
        split_out(9, bit, acc, keep, send)
        mate_copies.append(mate_copy(side, send, recv, mate))
        mate_copies[-1].start()
        if side == 0:
            for number, (source, target) in enumerate(((zga0, zga1), (zgb0, zgb1))):
                near[3 + number].wait_recv()
                swaps.append(swap_copy(7 + number, source, target))
                swaps[-1].start()

    for number in (5, 7, 8):
        swaps[number].wait_recv()
    za0, za1 = zpack0.at[0:quarter], zpack1.at[0:quarter]
    zb0, zb1 = zpack0.at[quarter:half], zpack1.at[quarter:half]
    sides = (
        (0, za0, za1, zga0, zga1, y_bit, bkeep_a, bsend_a, brecv_a, y_mate),
        (1, zb0, zb1, zgb0, zgb1, x_bit, bkeep_b, bsend_b, brecv_b, x_mate),
    )
    for side, own0, oth0, own1, oth1, bit, keep, send, recv, mate in sides:
        put_rows(lhs, 0, own0, oth0)
        put_rows(lhs, 1, own1, oth1)
        for level in range(4):
            left = [jnp.where(levels == level, lhs[k, :, :rows].astype(F32), 0.0).astype(BF16) for k in range(2)]
            acc[level] = dot(left[0], pooled_ref[:, side * span : (side + 1) * span]) + dot(left[1], pool_mate[side])
        split_out(4, bit, acc, keep, send)
        mate_copies.append(mate_copy(2 + side, send, recv, mate))
        mate_copies[-1].start()

    ways = [fb_way]

    def pass_on(number, keep, recv, target):
        mate_copies[number].wait_recv()

        def add(d, carry):
            for part in range(parts):
                keep[part, d] = (keep[part, d].astype(F32) + recv[part, d].astype(F32)).astype(BF16)
            return carry

        lax.fori_loop(0, keep.shape[1], add, 0)
        ways.append(Halving(1 + number, keep, target))
        ways[-1].send()

    fb_way.receive()

    swaps[1].wait_recv()
    swaps[6].wait_recv()
    for n in range(canv):
        gate = pixel_gates(boxes_ref, n, box_count, (PX, CELLS), 0)
        at = slice(n * PX, (n + 1) * PX)
        for which, ref in ((chan, df0), (1 - chan, df1)):
            into = pl.ds(pl.multiple_of(which * half, half), half)
            df = ref[at].astype(F32)
            xd[canv + n, :, into] = ref[at]
            xd[n, :, into] = (wide(gate(0, 1), half // CELLS) * pltpu.roll(df, PX - 1, 0)).astype(BF16)
            xd[2 * canv + n, :, into] = (wide(gate(0, -1), half // CELLS) * pltpu.roll(df, 1, 0)).astype(BF16)

    width = wbuf.shape[1]
    tiles = wfx_any.shape[1] // width

    def tile(t, carry):
        tile_load(t).wait()

        @pl.when(t + 1 < tiles)
        def _():
            tile_load(t + 1).start()

        first = lax.rem(t, 2) * 9
        for n in range(canv):
            at = slice(n * PX, (n + 1) * PX)
            gate = pixel_gates(boxes_ref, n, box_count, (PX, CELLS), 0)
            total = None
            for dy in range(3):
                found = dot_nt(xd[n], wbuf[first + dy * 3])
                for dx in range(1, 3):
                    found = found + dot_nt(xd[dx * canv + n], wbuf[first + dy * 3 + dx])
                if dy != 1:
                    found = wide(gate(1 - dy, 0), width // CELLS) * pltpu.roll(found, ((dy - 1) * CW) % PX, 0)
                total = found if total is None else total + found
            gx_ref[at, pl.ds(pl.multiple_of(t * width, width), width)] = total.astype(BF16)
        return carry

    lax.fori_loop(0, 2, tile, 0)
    pass_on(0, keep_a, recv_a, zrecv_a)
    lax.fori_loop(2, tiles, tile, 0)
    pass_on(1, keep_b, recv_b, zrecv_b)

    wbr_load = pltpu.make_async_copy(wbr_any, wbuf.at[pl.ds(0, wbr_any.shape[0])], load_sem.at[4])
    wbr_load.start()
    wbr_load.wait()
    per_level = wbr_any.shape[0] // 4
    total = 0.0
    for level in range(4):
        w = wbuf[level * per_level : (level + 1) * per_level].reshape(per_level * width, 2 * half)
        mine = []
        for which, ref in ((0, dz0), (1, dz1)):
            blocks = [
                jnp.where(cells_ref[:, 4:5] == level, ref[m * CELLS : (m + 1) * CELLS].astype(F32), 0.0).astype(BF16)
                for m in range(canv)
            ]
            mine.append(jnp.concatenate(blocks, axis=0))
        first = jnp.where(chan == 0, mine[0].astype(F32), mine[1].astype(F32)).astype(BF16)
        last = jnp.where(chan == 0, mine[1].astype(F32), mine[0].astype(F32)).astype(BF16)
        total = total + dot_nt(jnp.concatenate([first, last], axis=1), w)
    for m in range(canv):
        _, _, high, across = by_box(boxes_ref, m, cells_ref[:, 0:1], box_count)
        r0, r1, c0, c1 = member_bounds(lambda row: cells_ref[:, row : row + 1], high, across)
        mean = (total[m * CELLS : (m + 1) * CELLS] / ((r1 - r0) * (c1 - c0))).astype(BF16)
        for side in range(2):
            pool_mate[side, m * CELLS : (m + 1) * CELLS] = mean[:, side * span : (side + 1) * span]
    for n in range(canv):
        at = slice(n * PX, (n + 1) * PX)
        select, _ = members(boxes_ref, n, box_count, lambda row: lanes_ref[row : row + 1, :], (PX, CELLS), 0)
        for side in range(2):
            into = slice(side * span, (side + 1) * span)
            pooled = dot(select.astype(BF16), pool_mate[side, n * CELLS : (n + 1) * CELLS])
            gx_ref[at, into] = (gx_ref[at, into].astype(F32) + pooled).astype(BF16)

    pass_on(2, bkeep_a, brecv_a, bzrecv_a)
    pass_on(3, bkeep_b, brecv_b, bzrecv_b)
    for stage in range(1, stages):
        for way in ways:
            if len(way.copies) == stage:
                way.receive()

    stores = []

    def finish(way, out, at, sides):
        way.receive()
        keep, recv = way.keep, way.recv
        count = keep.shape[1]
        lanes_of = keep.shape[3] // len(sides)

        def add(d, carry):
            total = keep[way.kept(stages), d].astype(F32) + recv[parts - 2, d].astype(F32)
            for place_at, _ in enumerate(sides):
                row = at + place_at * each
                acc[d, row : row + each] = total[:, place_at * lanes_of : (place_at + 1) * lanes_of]
            return carry

        lax.fori_loop(0, count, add, 0)
        for place_at, side in enumerate(sides):
            source = acc.at[pl.ds(0, count), pl.ds(at + place_at * each, each), :]
            target = out.at[:, :, pl.ds(side * lanes_of, lanes_of)]
            stores.append(pltpu.make_async_copy(source, target, store_sem.at[len(stores)]))
            stores[-1].start()

    finish(ways[0], out_fb, 0, (0, 1))
    finish(ways[1], out_fx, 2 * each, (0,))
    finish(ways[2], out_fx, 3 * each, (1,))
    finish(ways[3], out_br, 4 * each, (0,))
    finish(ways[4], out_br, 5 * each, (1,))
    for copy in stores:
        copy.wait()
    dw_swap.wait()
    for copy in mate_copies + swaps + near + [copy for way in ways for copy in way.copies]:
        copy.wait_send()


def launch(kernel, in_specs, after=(), through=(), **rest):
    used = len(in_specs)
    extra = len(after) + len(through)
    if through:
        outs = len(rest["out_specs"])
        rest["out_specs"] = list(rest["out_specs"]) + [ANY_SPEC] * len(through)
        rest["out_shape"] = list(rest["out_shape"]) + [jax.ShapeDtypeStruct(a.shape, a.dtype) for a in through]
        rest["input_output_aliases"] = {used + len(after) + i: outs + i for i in range(len(through))}
        after = tuple(after) + tuple(through)
    else:
        outs = 0

    def body(*refs):
        refs = refs[:used] + refs[used + extra :]
        kernel(*(refs[: used + outs] + refs[used + outs + len(through) :] if through else refs))

    cost = pl.CostEstimate(flops=COST_UNIT * COSTS.get(rest["name"], 10), bytes_accessed=0, transcendentals=0)
    call = pl.pallas_call(body, cost_estimate=cost, in_specs=list(in_specs) + [ANY_SPEC] * extra, **rest)
    return lambda *operands: call(*operands, *after)


def whole(shape):
    return pl.BlockSpec(shape, lambda i: (0,) * len(shape))


def shaped(shape, kind):
    return jax.ShapeDtypeStruct(shape, kind)


def per_device(features, boxes, w_branch, gain_branch, bias_branch, w_fx, w_fb, gain_join, bias_join, w_cls, b_cls, grad_logits):
    canv, box_count = boxes.shape[:2]
    pixels, cin = features.shape
    mid = gain_join.shape[0]
    half = mid // lax.axis_size("chan")
    bw = gain_branch.shape[1]
    br = w_branch.shape[2]
    ncls = w_cls.shape[1]
    dp = lax.axis_size("dp")
    parts = dp // PLANE
    each = mid // dp
    cols = parts * each
    rows = canv * CELLS
    chan = lax.axis_index("chan")
    me = lax.axis_index("dp")
    rows_all = [float(canv * dp * box_count * s * s) for s in BINS]
    lanes_np = cell_table(box_count)
    lanes = jnp.asarray(lanes_np)
    cells = jnp.asarray(np.concatenate([lanes_np.T, np.zeros((CELLS, CELLS - 8), np.float32)], 1))

    def to_mate(array, mate):
        return lax.ppermute(array, "dp", [(i, i ^ mate) for i in range(dp)])

    def swap(array):
        return lax.ppermute(array, "chan", [(0, 1), (1, 0)])

    flat = boxes.reshape(-1)
    flat_of = [flat] + [to_mate(flat, m) for m in (1, 2, 3)]
    flat_all = jnp.concatenate(flat_of)

    pooled, lifts, z_own, z_send, x_first, x_last = launch(
        functools.partial(pool_kernel, canv, box_count),
        grid=(canv,),
        in_specs=[
            SMEM_SPEC,
            whole(lanes.shape),
            whole(cells.shape),
            pl.BlockSpec((PX, cin), lambda i: (i, 0)),
            whole(w_branch.shape),
        ],
        out_specs=[
            pl.BlockSpec((CELLS, cin), lambda i: (i, 0)),
            pl.BlockSpec((1, PX, 9 * CELLS), lambda i: (i, 0, 0)),
            whole((rows, bw)),
            whole((rows, bw)),
            pl.BlockSpec((PX, cin // 2), lambda i: (i, 0)),
            pl.BlockSpec((PX, cin // 2), lambda i: (i, 0)),
        ],
        out_shape=[
            shaped((rows, cin), BF16),
            shaped((canv, PX, 9 * CELLS), BF16),
            shaped((rows, bw), F32),
            shaped((rows, bw), BF16),
            shaped((pixels, cin // 2), BF16),
            shaped((pixels, cin // 2), BF16),
        ],
        scratch_shapes=[pltpu.VMEM((rows, cin), BF16), pltpu.VMEM((rows, br), F32)],
        compiler_params=params(),
        name="pool",
    )(flat, lanes, cells, features, w_branch)
    z_got = swap(z_send)
    z, z_part = launch(
        functools.partial(branch_sums_kernel, canv),
        in_specs=[VMEM_SPEC] * 3,
        out_specs=[VMEM_SPEC] * 2,
        out_shape=[shaped((rows, bw), F32), shaped((8, bw), F32)],
        compiler_params=params(),
        name="branch_sums",
    )(cells, z_own, z_got)
    z_total = dp_sum(z_part, dp, 0)
    y, z_norm, z_act, x_first, x_last = launch(
        functools.partial(branch_act_kernel, canv, rows_all),
        through=(x_first, x_last),
        in_specs=[VMEM_SPEC] * 5,
        out_specs=[VMEM_SPEC] * 3,
        out_shape=[shaped((rows, bw), BF16), shaped((rows, bw), F32), shaped((rows, bw), F32)],
        compiler_params=params(),
        name="branch_act",
    )(cells, z, z_total, gain_branch, bias_branch)
    x_mate = to_mate(x_first, 1)
    y_mate = to_mate(x_last, 2)
    y_all = jnp.concatenate([y] + [to_mate(y, m) for m in (1, 2, 3)], 0)

    f_own, f_send = launch(
        functools.partial(join_kernel, canv, box_count),
        grid=(3,),
        in_specs=[
            SMEM_SPEC,
            whole(cells.shape),
            whole((pixels, cin)),
            whole((rows, bw)),
            whole((canv, PX, 9 * CELLS)),
            pl.BlockSpec((3, 1, cin, mid), lambda i: (0, i, 0, 0)),
            pl.BlockSpec((3, 1, 4, bw, mid), lambda i: (0, i, 0, 0, 0)),
        ],
        out_specs=[whole((pixels, half)), whole((pixels, half))],
        out_shape=[shaped((pixels, half), F32), shaped((pixels, half), BF16)],
        scratch_shapes=[
            pltpu.VMEM((3 * canv, PX, cin), BF16),
            pltpu.VMEM((rows, 4 * bw), BF16),
            pltpu.VMEM((canv, 9 * CELLS, mid), BF16),
            pltpu.VMEM((canv, PX, mid), F32),
        ],
        compiler_params=params(),
        name="join",
    )(flat, cells, features, y, lifts, w_fx.reshape(3, 3, cin, mid), w_fb.reshape(3, 3, 4, bw, mid))
    quarter = half // 2
    bundle = quarter // 2
    logits, df, pack, send_a, send_b, send_d, dw_cls, db_total = launch(
        functools.partial(head_kernel, canv, box_count, dp, each),
        in_specs=[SMEM_SPEC] + [VMEM_SPEC] * 7,
        out_specs=[VMEM_SPEC] * 8,
        out_shape=[
            shaped((pixels, ncls), BF16),
            shaped((pixels, half), BF16),
            shaped((2 * half, pixels), BF16),
            shaped((quarter, pixels), BF16),
            shaped((quarter, pixels), BF16),
            shaped((bundle, pixels), BF16),
            shaped((dp, half // dp, ncls), F32),
            shaped((8, half), F32),
        ],
        scratch_shapes=[
            pltpu.VMEM((half, ncls), F32),
            pltpu.VMEM((pixels, half), BF16),
            pltpu.VMEM((pixels, half), F32),
            pltpu.VMEM((pixels, half), F32),
            pltpu.VMEM((pixels, ncls), BF16),
            pltpu.VMEM((pixels, ncls), BF16),
            pltpu.VMEM((half, PX), F32),
        ]
        + exchange_scratch(dp, half, 2)
        + [pltpu.SemaphoreType.DMA((2,)), pltpu.SemaphoreType.DMA((2,))],
        compiler_params=params(collective_id=1, has_side_effects=True),
        name="head",
        after=(x_mate, y_mate, y_all),
    )(flat, f_own, f_send, gain_join.reshape(1, mid), bias_join.reshape(1, mid), w_cls, b_cls.reshape(1, ncls), grad_logits)

    span = cin // 2
    tile = cin // 4
    stages = parts.bit_length() - 1

    def buffers(count, width):
        return [
            pltpu.VMEM((parts, count, each, width), BF16),
            pltpu.VMEM((parts, count, each, width), BF16),
            pltpu.VMEM((parts, count, each, width), BF16),
            pltpu.VMEM((parts - 1, count, each, width), BF16),
        ]

    def sems(*counts):
        return [pltpu.SemaphoreType.DMA((count,)) for count in counts]

    near_rows = [pltpu.VMEM((quarter, pixels), BF16)] * 4 + [pltpu.VMEM((bundle, pixels), BF16)] * 2
    near_cells = [pltpu.VMEM((quarter, rows), BF16)] * 6
    grad_features, sum_fx, sum_fb, sum_br, da_total, dw_own, dw_other = launch(
        functools.partial(tail_kernel, canv, box_count, dp, rows_all),
        in_specs=[SMEM_SPEC] + [VMEM_SPEC] * 3 + [ANY_SPEC] * 3 + [VMEM_SPEC] * 8 + [ANY_SPEC] * 6,
        out_specs=[VMEM_SPEC] + [ANY_SPEC] * 3 + [VMEM_SPEC] * 3,
        out_shape=[
            shaped((pixels, cin), BF16),
            shaped((9, each, cin), F32),
            shaped((9, each, 4 * bw), F32),
            shaped((4, each, cin), F32),
            shaped((8, bw), F32),
            shaped((dp, half // dp, ncls), F32),
            shaped((dp, half // dp, ncls), F32),
        ],
        scratch_shapes=[
            pltpu.VMEM((dp, half // dp, ncls), F32),
            pltpu.VMEM((half // dp, ncls), F32),
            pltpu.SemaphoreType.DMA((2, dp)),
            pltpu.SemaphoreType.DMA((2, dp)),
            pltpu.VMEM((2 * half, pixels), BF16),
            pltpu.VMEM((pixels, half), BF16),
        ]
        + near_rows
        + [pltpu.VMEM((bw, rows), BF16), pltpu.VMEM((bw, rows), BF16)]
        + near_cells
        + [pltpu.VMEM((rows, bw), BF16), pltpu.VMEM((rows, bw), BF16), pltpu.VMEM((rows, bw), F32)]
        + exchange_scratch(dp, bw, 1)
        + sems(10, 10, 5, 5)
        + [
            pltpu.VMEM((PX, 9 * CELLS), BF16),
            pltpu.VMEM((9, cols, PLANE * rows), BF16),
            pltpu.VMEM((2, pixels, span), BF16),
            pltpu.VMEM((18, tile, mid), BF16),
            pltpu.VMEM((3 * canv, PX, mid), BF16),
            pltpu.VMEM((3, half, pixels), BF16),
            pltpu.VMEM((9, half, span), F32),
            pltpu.VMEM((2, rows, span), BF16),
            pltpu.VMEM((parts, 9, each, 4 * bw), BF16),
            pltpu.VMEM((parts - 1, 9, each, 4 * bw), BF16),
        ]
        + buffers(9, span)
        + buffers(9, span)
        + buffers(4, span)
        + buffers(4, span)
        + sems(5, 6, 2, 4, 4, 4, 5 * stages, 5 * stages),
        compiler_params=pltpu.CompilerParams(vmem_limit_bytes=63 * 2**20, collective_id=4, has_side_effects=True),
        name="tail",
    )(
        flat_all, lanes, cells, pack, send_a, send_b, send_d, df, y_all, pooled, z_norm, z_act, z_total, gain_branch, dw_cls,
        features, x_mate, y_mate, w_fx, w_fb, w_branch.reshape(16, tile, br),
    )
    out_fx = jnp.transpose(sum_fx, (0, 2, 1))
    out_fb = jnp.transpose(sum_fb.reshape(9, each, 4, bw), (0, 2, 3, 1))
    out_br = jnp.transpose(sum_br, (0, 2, 1))

    small = db_total[:2]
    small_got = swap(small)
    small_all = jnp.concatenate([jnp.where(chan == 0, small, small_got), jnp.where(chan == 0, small_got, small)], 1)
    dw_halves = [jnp.where(chan == 0, dw_own, dw_other), jnp.where(chan == 0, dw_other, dw_own)]
    grad_w_cls = jnp.concatenate([a.reshape(half, ncls) for a in dw_halves], 0)
    return (
        logits,
        grad_features,
        out_br,
        da_total[:4],
        da_total[4:],
        out_fx,
        out_fb,
        small_all[0],
        small_all[1],
        grad_w_cls,
        db_total[2, :ncls],
    )


def solution(mesh):
    return jax.shard_map(
        per_device,
        mesh=mesh,
        in_specs=(
            P("dp", "chan"),
            P("dp", None, None),
            P(None, "chan", None),
            P(None, "chan"),
            P(None, "chan"),
            P(None, "chan", None),
            P(None, None, "chan", None),
            P(),
            P(),
            P(),
            P(),
            P("dp", None),
        ),
        out_specs=(
            P("dp", None),
            P("dp", "chan"),
            P(None, "chan", "dp"),
            P(None, "chan"),
            P(None, "chan"),
            P(None, "chan", "dp"),
            P(None, None, "chan", "dp"),
            P(),
            P(),
            P(),
            P(),
        ),
        check_vma=False,
    )
```

```python
import functools

import jax
import jax.numpy as jnp
import numpy as np
from jax import lax
from jax.experimental import pallas as pl
from jax.experimental.pallas import tpu as pltpu
from jax.sharding import PartitionSpec as P

CH = 16
CW = 32
PX = CH * CW
EPS = 1e-05
BINS = (1, 2, 3, 6)
CELLS = 128
PLANE = 4
F32 = jnp.float32
BF16 = jnp.bfloat16
MESH = pl.DeviceIdType.MESH
VMEM_SPEC = pl.BlockSpec(memory_space=pltpu.VMEM)
SMEM_SPEC = pl.BlockSpec(memory_space=pltpu.SMEM)
ANY_SPEC = pl.BlockSpec(memory_space=pl.ANY)
NT = (((1,), (1,)), ((), ()))
TN = (((0,), (0,)), ((), ()))


def dot(a, b):
    return jnp.dot(a, b, preferred_element_type=F32)


def dot_nt(a, b):
    return lax.dot_general(a, b, NT, preferred_element_type=F32)


def dot_tn(a, b):
    return lax.dot_general(a, b, TN, preferred_element_type=F32)


def cell_table(box_count):
    table = np.zeros((8, CELLS), np.float32)
    table[1] = 1.0
    table[4] = 9.0
    at = 0
    for level, bins in enumerate(BINS):
        for box in range(box_count):
            for i in range(bins):
                for j in range(bins):
                    table[:6, at] = (box, bins, i, j, level, 1.0)
                    at += 1
    return table


def box_at(boxes_ref, canvas, box, box_count):
    base = (canvas * box_count + box) * 4
    return [boxes_ref[base + part] for part in range(4)]


def by_box(boxes_ref, canvas, which, box_count):
    sides = None
    for box in range(box_count):
        mine = [side.astype(F32) for side in box_at(boxes_ref, canvas, box, box_count)]
        if sides is None:
            sides = [jnp.full(which.shape, side, F32) for side in mine]
        else:
            sides = [jnp.where(which == box, new, old) for new, old in zip(mine, sides)]
    return sides


def within(relative, extent):
    return (relative >= 0) & (relative < extent)


def pixel_gates(boxes_ref, canvas, box_count, shape, axis):
    place = lax.broadcasted_iota(jnp.int32, shape, axis)
    row = place >> 5
    col = place & (CW - 1)
    rel = []
    for box in range(box_count):
        top, left, height, width = box_at(boxes_ref, canvas, box, box_count)
        rel.append((row - top, col - left, height, width))

    def gate(dy, dx):
        total = None
        for y, x, height, width in rel:
            hit = within(y, height) & within(x, width)
            if not isinstance(dy, int) or dy:
                hit = hit & within(y + dy, height)
            if not isinstance(dx, int) or dx:
                hit = hit & within(x + dx, width)
            value = jnp.where(hit, 1.0, 0.0)
            total = value if total is None else total + value
        return total

    return gate


def wide(column_block, times):
    return jnp.concatenate([column_block] * times, axis=1)


def rows_down(boxes_ref, canvas, box_count, x, xs, n, below):
    gate = pixel_gates(boxes_ref, canvas, box_count, (PX, CELLS), 0)
    reps = xs.shape[2] // CELLS
    blank = jnp.zeros((CW, xs.shape[2]), BF16)
    xs[n, 0:CW] = blank
    xs[n, CW:PX] = x[0 : PX - CW] * wide(gate(-1, 0).astype(BF16), reps)[CW:]
    xs[below + n, 0 : PX - CW] = x[CW:PX] * wide(gate(1, 0).astype(BF16), reps)[: PX - CW]
    xs[below + n, PX - CW : PX] = blank


def member_bounds(table_at, height, width):
    bins, i, j = table_at(1), table_at(2), table_at(3)

    def start(at, extent):
        return jnp.floor((at * extent + 0.5) / bins)

    def stop(at, extent):
        return jnp.floor(((at + 1) * extent + bins - 0.5) / bins)

    return start(i, height), stop(i, height), start(j, width), stop(j, width)


def members(boxes_ref, canvas, box_count, table_at, shape, axis):
    top, left, height, width = by_box(boxes_ref, canvas, table_at(0), box_count)
    r0, r1, c0, c1 = member_bounds(table_at, height, width)
    place = lax.broadcasted_iota(jnp.int32, shape, axis)
    row = (place >> 5).astype(F32) - top
    col = (place & (CW - 1)).astype(F32) - left
    hit = (row >= r0) & (row < r1) & (col >= c0) & (col < c1) & (table_at(5) > 0)
    return jnp.where(hit, 1.0, 0.0), (r1 - r0) * (c1 - c0)


def gated_lifts(boxes_ref, canvas, box_count, lanes_ref, store):
    def table_at(row):
        return lanes_ref[row : row + 1, :]

    top, left, height, width = by_box(boxes_ref, canvas, table_at(0), box_count)

    def side(size, edge, extent, cell):
        relative = lax.broadcasted_iota(jnp.int32, (size, CELLS), 0).astype(F32) - edge
        scale = (table_at(1) - 1.0) / (extent - 1.0)
        own = within(relative, extent)
        found = []
        for step in (-1, 0, 1):
            moved = relative + step
            weight = jnp.maximum(0.0, 1.0 - jnp.abs(moved * scale - cell))
            found.append(jnp.where(own & within(moved, extent), weight, 0.0))
        return found

    rows = [found * table_at(5) for found in side(CH, top, height, table_at(2))]
    cols = side(CW, left, width, table_at(3))
    for d in range(9):
        for y in range(CH):
            store(d, y, (rows[d // 3][y : y + 1] * cols[d % 3]).astype(BF16))


def pltranspose(block):
    return jnp.transpose(block, (1, 0))


def signal_all(total, chan_too=False):
    me = lax.axis_index("dp")
    chan = lax.axis_index("chan")
    barrier = pltpu.get_barrier_semaphore()

    def signal(step, carry):
        pl.semaphore_signal(barrier, inc=1, device_id=(lax.rem(me + step, total), chan), device_id_type=MESH)
        return carry

    lax.fori_loop(1, total, signal, 0)
    if chan_too:
        pl.semaphore_signal(barrier, inc=1, device_id=(me, 1 - chan), device_id_type=MESH)
    return total if chan_too else total - 1


class Exchange:
    def __init__(self, total, own, slots, send_sem, recv_sem, parted=False):
        self.total, self.own, self.slots, self.send_sem, self.recv_sem = total, own, slots, send_sem, recv_sem
        self.me = lax.axis_index("dp")
        self.parted = parted

    def block(self, device):
        return self.own.at[device] if self.parted else self.own

    def copy_to(self, step):
        return pltpu.make_async_remote_copy(
            src_ref=self.block(lax.rem(self.me + step, self.total)),
            dst_ref=self.slots.at[self.me],
            send_sem=self.send_sem.at[step],
            recv_sem=self.recv_sem.at[self.me],
            device_id=(lax.rem(self.me + step, self.total), lax.axis_index("chan")),
            device_id_type=MESH,
        )

    def copy_from(self, step):
        other = lax.rem(self.me + self.total - step, self.total)
        return pltpu.make_async_remote_copy(
            src_ref=self.block(other),
            dst_ref=self.slots.at[other],
            send_sem=self.send_sem.at[step],
            recv_sem=self.recv_sem.at[other],
            device_id=(other, lax.axis_index("chan")),
            device_id_type=MESH,
        )

    def start(self):
        if self.parted:
            keep = pltpu.make_async_copy(self.block(self.me), self.slots.at[self.me], self.recv_sem.at[self.me])
            keep.start()
            keep.wait()
        else:
            self.slots[self.me] = self.own[...]

        def one(step, carry):
            self.copy_to(step).start()
            return carry

        lax.fori_loop(1, self.total, one, 0)

    def arrive(self):
        def one(step, carry):
            self.copy_from(step).wait_recv()
            return carry

        def sent(step, carry):
            self.copy_to(step).wait_send()
            return carry

        lax.fori_loop(1, self.total, one, 0)
        lax.fori_loop(1, self.total, sent, 0)

    def finish(self):
        self.arrive()
        value = self.slots[0]
        for other in range(1, self.total):
            value = value + self.slots[other]
        return value


def exchange_scratch(total, width, times):
    return [
        pltpu.VMEM((times, 8, width), F32),
        pltpu.VMEM((times, total, 8, width), F32),
        pltpu.SemaphoreType.DMA((times, total)),
        pltpu.SemaphoreType.DMA((times, total)),
    ]


def core_copy(source, target, send_sem, recv_sem):
    return pltpu.make_async_remote_copy(
        src_ref=source,
        dst_ref=target,
        send_sem=send_sem,
        recv_sem=recv_sem,
        device_id=(lax.axis_index("dp"), 1 - lax.axis_index("chan")),
        device_id_type=MESH,
    )


def branch_stat(total_ref, level, rows_all):
    mean = total_ref[level : level + 1, :] / rows_all
    var = total_ref[4 + level : 5 + level, :] / rows_all - mean * mean
    return mean, lax.rsqrt(var + EPS)


def expand(y, cells_ref, keep, at):
    width = y.shape[1]
    for n in range(y.shape[0] // CELLS):
        rows = slice(n * CELLS, (n + 1) * CELLS)
        block = y[rows].astype(F32)
        for level in range(4):
            mine = jnp.where(cells_ref[:, 4:5] == level, block, 0.0)
            keep[at + n * CELLS : at + (n + 1) * CELLS, level * width : (level + 1) * width] = mine.astype(BF16)


def front_kernel(
    canv, box_count, total, each, rows_all,
    boxes_ref, box_ref, lanes_ref, cells_ref, zgain_ref, zbias_ref, gain_ref, bias_ref, w_ref, bcls_ref, g_ref,
    x_any, wbr_any, wfx_any, wfb_any,
    pooled_ref, y_ref, norm_ref, act_ref, ztotal_ref, boxes_all, logits_ref, df_ref, pack_ref, send_a, send_b, send_d,
    dw_ref, sums_ref, xm_any, ym_any,
    x, xs, wbr, wbuf, lifts, terms, fjoin, ye, zs, zsend, zgot, dw, fsend, got, f, db, score, score_got, flip,
    part, slots, send_sem, recv_sem, core_send, core_recv, near_send, near_recv, load_sem,
):
    me = lax.axis_index("dp")
    chan = lax.axis_index("chan")
    x_mate = me + 1 - 2 * (me % 2)
    y_mate = me + 2 - 4 * ((me // 2) % 2)
    span = xm_any.shape[1]
    half = df_ref.shape[1]
    mid = 2 * half
    ncls = g_ref.shape[1]
    own = pl.ds(pl.multiple_of(chan * half, half), half)
    away = pl.ds(pl.multiple_of((1 - chan) * half, half), half)
    expected = signal_all(total, True)
    loads = [pltpu.make_async_copy(x_any.at[pl.ds(n * PX, PX)], x.at[n], load_sem.at[n]) for n in range(canv)]
    loads.append(pltpu.make_async_copy(wbr_any, wbr, load_sem.at[canv]))
    loads += [pltpu.make_async_copy(wfx_any.at[:, t], wbuf.at[t], load_sem.at[canv + 1 + t]) for t in range(3)]
    for copy in loads:
        copy.start()

    def near_copy(number, source, target, mate):
        return pltpu.make_async_remote_copy(
            src_ref=source, dst_ref=target, send_sem=near_send.at[number], recv_sem=near_recv.at[number],
            device_id=(mate, chan), device_id_type=MESH,
        )

    def share(number, first, last):
        at = pl.ds(first * PX, (last - first) * PX)
        copies = [
            near_copy(number, x_any.at[at, pl.ds(0, span)], xm_any.at[at], x_mate),
            near_copy(number + 1, x_any.at[at, pl.ds(span, span)], ym_any.at[at], y_mate),
        ]
        for copy in copies:
            copy.start()
        return copies

    def table_at(row):
        return cells_ref[:, row : row + 1]

    part[...] = jnp.zeros_like(part)
    near = []
    for n in range(canv):
        loads[n].wait()
        select, count = members(boxes_ref, n, box_count, table_at, (CELLS, PX), 1)
        pooled_ref[n * CELLS : (n + 1) * CELLS] = (dot(select.astype(BF16), x[n]) / count).astype(BF16)
        if n == 0:
            pl.semaphore_wait(pltpu.get_barrier_semaphore(), expected)
            near += share(0, 0, 1)
            boxes_all[0] = box_ref[...]
            for number, mate in ((1, x_mate), (2, y_mate), (3, x_mate + y_mate - me)):
                near.append(near_copy(3 + number, box_ref, boxes_all.at[number], mate))
                near[-1].start()
    loads[canv].wait()
    for level in range(4):
        found = dot(pooled_ref[...], wbr[level])
        for n in range(canv):
            rows = slice(n * CELLS, (n + 1) * CELLS)
            mine = jnp.where(table_at(4) == level, found[rows], 0.0)
            zs[rows, :] = mine if level == 0 else zs[rows, :] + mine
    zsend[...] = zs[:, away].astype(BF16)
    swap_z = core_copy(zsend, zgot, core_send.at[0], core_recv.at[0])
    swap_z.start()
    for n in range(canv):
        rows_down(boxes_ref, n, box_count, x.at[n], xs, n, canv)

        def store(d, y, block, n=n):
            lifts[n, y * CW : (y + 1) * CW, d * CELLS : (d + 1) * CELLS] = block

        gated_lifts(boxes_ref, n, box_count, lanes_ref, store)
    swap_z.wait()
    bw = y_ref.shape[1]
    for n in range(canv):
        rows = slice(n * CELLS, (n + 1) * CELLS)
        z = zs[rows, own] + zgot[rows].astype(F32)
        norm_ref[rows] = z
        for level in range(4):
            mine = jnp.where(table_at(4) == level, z, 0.0)
            part[0, level : level + 1, :] += jnp.sum(mine, 0, keepdims=True)
            part[0, 4 + level : 5 + level, :] += jnp.sum(mine * mine, 0, keepdims=True)
    z_sums = Exchange(total, part.at[0], slots.at[0], send_sem.at[0], recv_sem.at[0])
    z_sums.start()

    def features_part(t):
        loads[canv + 1 + t].wait()
        for n in range(canv):
            q = dot(xs[n], wbuf[t, 0]) + dot(x[n], wbuf[t, 1]) + dot(xs[canv + n], wbuf[t, 2])
            gate = pixel_gates(boxes_ref, n, box_count, (PX, CELLS), 0)
            if t == 0:
                fjoin[n] = wide(gate(0, -1), mid // CELLS) * pltpu.roll(q, 1, 0)
            elif t == 1:
                fjoin[n] += wide(gate(0, 0), mid // CELLS) * q
            else:
                fjoin[n] += wide(gate(0, 1), mid // CELLS) * pltpu.roll(q, PX - 1, 0)
        loads.append(pltpu.make_async_copy(wfb_any.at[:, t], wbuf.at[t], load_sem.at[canv + 4 + t]))
        loads[-1].start()

    features_part(0)
    z_total = z_sums.finish()
    ztotal_ref[...] = z_total
    near += share(2, 1, canv)
    for n in range(canv):
        rows = slice(n * CELLS, (n + 1) * CELLS)
        z = norm_ref[rows]
        norm = act = 0.0
        for level in range(4):
            mean, rstd = branch_stat(ztotal_ref, level, rows_all[level])
            here = jnp.where(table_at(4) == level, 1.0, 0.0)
            mine = (z - mean) * rstd
            norm = norm + here * mine
            act = act + here * (zgain_ref[level : level + 1, :] * mine + zbias_ref[level : level + 1, :])
        norm_ref[rows] = norm
        act_ref[rows] = act
        value = act * jax.nn.sigmoid(act)
        y_ref[rows] = value.astype(BF16)
        for level in range(4):
            mine = jnp.where(table_at(4) == level, value, 0.0)
            ye[rows, level * bw : (level + 1) * bw] = mine.astype(BF16)
    features_part(1)
    features_part(2)

    for t in range(3):
        loads[canv + 4 + t].wait()
        for dy in range(3):
            term = dot(ye[...], wbuf[t, dy]).astype(BF16)
            at = (dy * 3 + t) * CELLS
            for n in range(canv):
                terms[n, at : at + CELLS] = term[n * CELLS : (n + 1) * CELLS]
    for n in range(canv):
        fjoin[n] += dot(lifts[n], terms[n])
        fsend[n * PX : (n + 1) * PX] = fjoin[n, :, away].astype(BF16)
    swap_f = core_copy(fsend, got, core_send.at[1], core_recv.at[1])
    swap_f.start()
    dw[...] = jnp.zeros_like(dw)
    area = 0
    for n in range(canv):
        for box in range(box_count):
            side = box_at(boxes_ref, n, box, box_count)
            area = area + side[2] * side[3]
    part[1, 2:3, :] = jnp.full((1, half), area.astype(F32), F32)
    swap_f.wait()
    for n in range(canv):
        rows = slice(n * PX, (n + 1) * PX)
        value = fjoin[n, :, own] + got[rows].astype(F32)
        f[rows] = value
        part[1, 0:1, :] += jnp.sum(value, 0, keepdims=True)
        part[1, 1:2, :] += jnp.sum(value * value, 0, keepdims=True)
    first = Exchange(total, part.at[1], slots.at[1], send_sem.at[1], recv_sem.at[1])
    first.start()
    f_total = first.finish()
    count = f_total[2:3, :]
    mean = f_total[0:1, :] / count
    rstd = lax.rsqrt(f_total[1:2, :] / count - mean * mean + EPS)
    gain, bias, w = gain_ref[:, own], bias_ref[:, own], w_ref[own, :]
    valid = [wide(pixel_gates(boxes_ref, n, box_count, (PX, CELLS), 0)(0, 0), half // CELLS) for n in range(canv)]
    for n in range(canv):
        rows = slice(n * PX, (n + 1) * PX)
        norm = (f[rows] - mean) * rstd
        f[rows] = norm
        act = gain * norm + bias
        sig = jax.nn.sigmoid(act)
        hidden = (act * sig * valid[n]).astype(BF16)
        g = g_ref[rows]
        score[rows] = dot(hidden, w).astype(BF16)
        value = dot_nt(g, w) * valid[n] * sig * (1.0 + act * (1.0 - sig))
        db[rows] = value
        part[2, 0:1, :] += jnp.sum(value * norm, 0, keepdims=True)
        part[2, 1:2, :] += jnp.sum(value, 0, keepdims=True)
        part[2, 2:3, :ncls] += jnp.sum(g.astype(F32), 0, keepdims=True)
        dw[...] += dot_tn(hidden, g)
    second = Exchange(total, part.at[2], slots.at[2], send_sem.at[2], recv_sem.at[2])
    second.start()
    swap_score = core_copy(score, score_got, core_send.at[2], core_recv.at[2])
    swap_score.start()
    sums = second.finish()
    sums_ref[...] = sums
    scale = gain * rstd
    for n in range(canv):
        rows = slice(n * PX, (n + 1) * PX)
        df = scale * (db[rows] - sums[1:2, :] / count - f[rows] * (sums[0:1, :] / count)) * valid[n]
        df_ref[rows] = df.astype(BF16)
        flip[...] = pltranspose(df)
        span = pl.ds(n * PX, PX)
        pack_ref[0:half, span] = flip[...].astype(BF16)
        views = [pack_ref.at[half : half + half // 2, span], send_a.at[:, span]]
        views += [pack_ref.at[half + half // 2 : 2 * half, span], send_b.at[:, span], send_d.at[:, span]]
        split_rows(flip, half // (4 * each), each, *views)
    strip = dw_ref.shape[1]
    for device in range(total):
        dw_ref[device] = dw[device * strip : (device + 1) * strip]
    swap_score.wait()
    for n in range(canv):
        rows = slice(n * PX, (n + 1) * PX)
        both = score[rows].astype(F32) + score_got[rows].astype(F32)
        logits_ref[rows] = (both + bcls_ref[...]).astype(BF16)
    for copy in near:
        copy.wait()


def split_rows(rows, groups, each, own_a, send_a, own_b, send_b, send_d=None):
    me = lax.axis_index("dp")
    x_bit = me % 2
    y_bit = (me // 2) % 2

    def piece(group, y, x):
        return rows[pl.ds(pl.multiple_of(((group * 2 + y) * 2 + x) * each, each), each), :].astype(BF16)

    for group in range(groups):
        for bit in range(2):
            at = (bit * groups + group) * each
            own_a[at : at + each] = piece(group, bit, x_bit)
            send_a[at : at + each] = piece(group, bit, 1 - x_bit)
            own_b[at : at + each] = piece(group, y_bit, bit)
            send_b[at : at + each] = piece(group, 1 - y_bit, bit)
        if send_d is not None:
            send_d[group * each : (group + 1) * each] = piece(group, 1 - y_bit, 1 - x_bit)


def put_rows(out, index, own_ref, other_ref):
    chan = lax.axis_index("chan")
    size = own_ref.shape[0]
    width = own_ref.shape[1]
    for ref, which in ((own_ref, chan), (other_ref, 1 - chan)):
        into = pl.ds(pl.multiple_of(which * size, size), size)
        if index is None:
            out[into, :width] = ref[...]
        else:
            out[index, into, :width] = ref[...]


def cols_across(boxes_ref, canvas, at, box_count, own_ref, other_ref, lhs):
    chan = lax.axis_index("chan")
    size = own_ref.shape[0]
    span = slice(at * PX, (at + 1) * PX)
    gate = pixel_gates(boxes_ref, canvas, box_count, (8, PX), 1)
    for ref, which in ((own_ref, chan), (other_ref, 1 - chan)):
        into = pl.ds(pl.multiple_of(which * size, size), size)
        value = ref[:, span].astype(F32)
        lhs[0, into, span] = (pltpu.roll(value, PX - 1, 1) * gate(0, 1)[0:1]).astype(BF16)
        lhs[1, into, span] = ref[:, span]
        lhs[2, into, span] = (pltpu.roll(value, 1, 1) * gate(0, -1)[0:1]).astype(BF16)


def reversed_bits(number, bits):
    return sum(((number >> bit) & 1) << (bits - 1 - bit) for bit in range(bits))


def split_out(count, bit, acc, keep, send):
    parts, _, each, _ = keep.shape
    groups = parts // 2
    block = groups * each

    def one(d, carry):
        for half in range(2):
            for ref, which in ((keep, bit), (send, 1 - bit)):
                for group in range(groups):
                    at = (half * 2 + which) * block + group * each
                    ref[reversed_bits(half * groups + group, parts.bit_length() - 1), d] = acc[d, pl.ds(pl.multiple_of(at, each), each), :].astype(BF16)
        return carry

    lax.fori_loop(0, count, one, 0)


def tail_kernel(
    canv, box_count,
    total_dp, rows_all,
    boxes_ref, lanes_ref, cells_ref, pack0, sa, sb, sd, df0, y0, norm_ref, act_ref, ztotal_ref, zgain_ref, dw_ref,
    pooled_any, x_any, xm_any, ym_any, wfx_any, wfb_any, wbr_any,
    gx_ref, out_fx, out_fb, out_br, sums_ref, dw_own, dw_other,
    dw_slots, dw_sum, dw_send, dw_recv, pack1, df1, ga0, ga1, gb0, gb1, gd0, gd1, y_all, zpack0, zpack1, zsa, zsb, zga0, zga1, zgb0, zgb1, dz0, dz1, da,
    part, slots, sum_send, sum_recv, core_send, core_recv, near_send, near_recv,
    lift, grads, xbuf, wbuf, xd, lhs, acc, pool_mate,
    fb_send, fb_recv, keep_a, send_a, recv_a, zrecv_a, keep_b, send_b, recv_b, zrecv_b,
    bkeep_a, bsend_a, brecv_a, bzrecv_a, bkeep_b, bsend_b, brecv_b, bzrecv_b,
    load_sem, store_sem, w_sem, fb_sem, mate_send, mate_recv, part_send, part_recv,
):
    me = lax.axis_index("dp")
    chan = lax.axis_index("chan")
    parts = fb_send.shape[0]
    pixels = df0.shape[0]
    half = df0.shape[1]
    span = xbuf.shape[2]
    group, place = me // PLANE, me % PLANE
    x_bit, y_bit = me % 2, (me // 2) % 2
    x_mate = me + 1 - 2 * x_bit
    y_mate = me + 2 - 4 * y_bit

    stages = parts.bit_length() - 1

    def group_bit(stage):
        return (group // 2**stage) % 2

    def group_mate(stage):
        return (group + 2**stage * (1 - 2 * group_bit(stage))) * PLANE + place

    d_mate = x_mate + y_mate - me
    expected = signal_all(total_dp, True)

    def load(source, slot, which):
        return pltpu.make_async_copy(source, xbuf.at[slot], load_sem.at[which])

    loads = [
        load(x_any.at[:, pl.ds(0, span)], 0, 0),
        load(xm_any, 1, 1),
        load(x_any.at[:, pl.ds(span, span)], 0, 2),
        load(ym_any, 1, 3),
    ]
    loads[0].start()
    loads[1].start()

    def tile_load(tile):
        width = wbuf.shape[1]
        return pltpu.make_async_copy(
            wfx_any.at[:, pl.ds(pl.multiple_of(tile * width, width), width), :],
            wbuf.at[pl.ds(pl.multiple_of(lax.rem(tile, 2) * 9, 9), 9)],
            w_sem.at[lax.rem(tile, 2)],
        )

    levels_at_once = wfb_any.shape[1]

    def fb_load(d):
        at = lax.rem(d, 4) * levels_at_once
        return pltpu.make_async_copy(wfb_any.at[d], wbuf.at[pl.ds(at, levels_at_once)], fb_sem.at[lax.rem(d, 4)])

    for d in range(3):
        fb_load(d).start()

    def mate_copy(number, source, target, mate):
        return pltpu.make_async_remote_copy(
            src_ref=source, dst_ref=target, send_sem=mate_send.at[number], recv_sem=mate_recv.at[number],
            device_id=(mate, chan), device_id_type=MESH,
        )

    class Halving:
        def __init__(self, number, keep, recv):
            self.number, self.keep, self.recv = number, keep, recv
            self.copies = []

        def kept(self, stage):
            at = 0
            for bit in range(stage):
                at = at + group_bit(bit) * (parts >> (bit + 1))
            return at

        def send(self):
            stage = len(self.copies)
            count = parts >> (stage + 1)
            from_at = self.kept(stage) + (1 - group_bit(stage)) * count
            number = self.number * stages + stage
            copy = pltpu.make_async_remote_copy(
                src_ref=self.keep.at[pl.ds(from_at, count)],
                dst_ref=self.recv.at[pl.ds(parts - 2 * count, count)],
                send_sem=part_send.at[number],
                recv_sem=part_recv.at[number],
                device_id=(group_mate(stage), chan),
                device_id_type=MESH,
            )
            copy.start()
            self.copies.append(copy)

        def receive(self):
            stage = len(self.copies)
            self.copies[-1].wait_recv()
            if stage == stages:
                return
            count = parts >> stage
            at = self.kept(stage)

            def add(d, carry):
                for part in range(count):
                    got = self.recv[parts - 2 * count + part, d].astype(F32)
                    self.keep[at + part, d] = (self.keep[at + part, d].astype(F32) + got).astype(BF16)
                return carry

            lax.fori_loop(0, self.keep.shape[1], add, 0)
            self.send()

    def near_copy(number, source, target, mate):
        return pltpu.make_async_remote_copy(
            src_ref=source, dst_ref=target, send_sem=near_send.at[number], recv_sem=near_recv.at[number],
            device_id=(mate, chan), device_id_type=MESH,
        )

    def swap_copy(number, source, target):
        return core_copy(source, target, core_send.at[number], core_recv.at[number])

    pl.semaphore_wait(pltpu.get_barrier_semaphore(), expected)
    swaps = [swap_copy(0, pack0, pack1), swap_copy(1, df0, df1)]
    near = [near_copy(0, sa, ga0, x_mate), near_copy(1, sb, gb0, y_mate), near_copy(2, sd, gd0, d_mate)]
    y_near = [near_copy(5 + number, y0, y_all.at[number], mate) for number, mate in enumerate((x_mate, y_mate, d_mate))]
    for copy in swaps + near + y_near:
        copy.start()
    dw_parts = Exchange(total_dp, dw_ref, dw_slots, dw_send.at[0], dw_recv.at[0], True)
    dw_parts.start()

    def lift_of(n):
        def store(d, y, block):
            lift[y * CW : (y + 1) * CW, d * CELLS : (d + 1) * CELLS] = block

        gated_lifts(boxes_ref, n, box_count, lanes_ref, store)

    rows = canv * CELLS
    for n in range(canv):
        lift_of(n)
        for ref, which in ((pack0, chan), (pack1, 1 - chan)):
            if n == 0 and ref is pack1:
                swaps[0].wait_recv()
            found = dot(ref[:half, n * PX : (n + 1) * PX], lift[...]).astype(BF16)
            into = pl.ds(pl.multiple_of(which * half, half), half)
            for e in range(9):
                xd[e, into, n * CELLS : (n + 1) * CELLS] = found[:, e * CELLS : (e + 1) * CELLS]

    def back(d, carry):
        fb_load(d).wait()

        @pl.when(d + 3 < 9)
        def _():
            fb_load(d + 3).start()

        for level in range(4):
            found = dot(wbuf[lax.rem(d, 4) * levels_at_once + level], xd[d, :, :rows])

            @pl.when(d == 0)
            def _():
                acc[level, :, :rows] = found

            @pl.when(d > 0)
            def _():
                acc[level, :, :rows] += found

        return carry

    lax.fori_loop(0, 9, back, 0)
    tile_load(0).start()
    levels = jnp.concatenate([lanes_ref[4:5, :]] * canv, axis=1)
    dy = 0.0
    for level in range(4):
        dy = dy + jnp.where(levels == level, acc[level, :, :rows], 0.0)
    dy = pltranspose(dy)
    sig = jax.nn.sigmoid(act_ref[...])
    da[...] = dy * sig * (1.0 + act_ref[...] * (1.0 - sig))
    for level in range(4):
        gain = bias = 0.0
        for n in range(canv):
            at = slice(n * CELLS, (n + 1) * CELLS)
            mine = jnp.where(cells_ref[:, 4:5] == level, da[at], 0.0)
            gain = gain + jnp.sum(mine * norm_ref[at], 0, keepdims=True)
            bias = bias + jnp.sum(mine, 0, keepdims=True)
        part[0, level : level + 1, :] = gain
        part[0, 4 + level : 5 + level, :] = bias
    exchange = Exchange(total_dp, part.at[0], slots.at[0], sum_send.at[0], sum_recv.at[0])
    exchange.start()
    dw_sum[...] = dw_parts.finish()
    dw_sums = Exchange(total_dp, dw_sum, dw_own, dw_send.at[1], dw_recv.at[1])
    dw_sums.start()
    for number, (source, target) in enumerate(((ga0, ga1), (gb0, gb1), (gd0, gd1))):
        near[number].wait_recv()
        swaps.append(swap_copy(2 + number, source, target))
        swaps[-1].start()
    for number in range(2, 5):
        swaps[number].wait_recv()

    half_a, half_b = half, half + half // 2
    qa0, qa1 = pack0.at[half_a:half_b], pack1.at[half_a:half_b]
    qb0, qb1 = pack0.at[half_b : 2 * half], pack1.at[half_b : 2 * half]
    ye = gx_ref
    size = gd0.shape[0]
    cols = 2 * size
    for source, (own_ref, oth_ref, bit) in enumerate(((qa0, qa1, y_bit), (ga0, ga1, y_bit), (gb0, gb1, x_bit), (gd0, gd1, 0))):
        mine = pl.ds(pl.multiple_of(bit * size, size), size)
        put_rows(lhs.at[source // 2, source % 2 * cols : (source % 2 + 1) * cols], None, own_ref.at[mine], oth_ref.at[mine])

    def canvas(n, carry):
        lift_of(n)
        source = n // canv
        at = pl.ds(pl.multiple_of(lax.rem(source, 2) * cols, cols), cols)
        found = dot(lhs[source // 2, at, pl.ds(pl.multiple_of((n % canv) * PX, PX), PX)], lift[...]).astype(BF16)
        for d in range(9):
            grads[d, :, pl.ds(pl.multiple_of(n * CELLS, CELLS), CELLS)] = found[:, d * CELLS : (d + 1) * CELLS]
        return carry

    lax.fori_loop(0, PLANE * canv, canvas, 0)
    each = fb_send.shape[2]
    expand(y0[...], cells_ref, ye, 0)
    for number, copy in enumerate(y_near):
        copy.wait_recv()
        expand(y_all[number], cells_ref, ye, (number + 1) * rows)
    for d in range(9):
        result = dot(grads[d], ye[...])
        for part in range(parts):
            fb_send[reversed_bits(part, stages), d] = result[part * each : (part + 1) * each].astype(BF16)
    fb_way = Halving(0, fb_send, fb_recv)
    fb_way.send()

    sums = exchange.finish()
    sums_ref[...] = sums
    dw_sums.arrive()
    zflip = acc.at[4, :, 0:rows]
    for n in range(canv):
        at = slice(n * CELLS, (n + 1) * CELLS)
        dz = 0.0
        for level in range(4):
            _, rstd = branch_stat(ztotal_ref, level, rows_all[level])
            here = jnp.where(cells_ref[:, 4:5] == level, 1.0, 0.0)
            mean_gain = sums[level : level + 1, :] / rows_all[level]
            mean_bias = sums[4 + level : 5 + level, :] / rows_all[level]
            mine = zgain_ref[level : level + 1, :] * rstd * (da[at] - mean_bias - norm_ref[at] * mean_gain)
            dz = dz + here * mine
        dz0[at] = dz.astype(BF16)
        zflip[:, at] = pltranspose(dz)
    quarter = half // 2
    split_rows(zflip, half // (4 * each), each, zpack0.at[0:quarter], zsa, zpack0.at[quarter:half], zsb)
    swaps += [swap_copy(5, zpack0, zpack1), swap_copy(6, dz0, dz1)]
    dw_swap = swap_copy(9, dw_own, dw_other)
    dw_swap.start()
    near += [near_copy(3, zsa, zga0, x_mate), near_copy(4, zsb, zgb0, y_mate)]
    for copy in swaps[5:] + near[3:]:
        copy.start()

    mate_copies = []
    sides = (
        (0, ((0, qa0, qa1, 0), (1, ga0, ga1, 1)), y_bit, keep_a, send_a, recv_a, y_mate),
        (1, ((0, qb0, qb1, 0), (2, gb0, gb1, 1)), x_bit, keep_b, send_b, recv_b, x_mate),
    )
    for side, sources, bit, keep, send, recv, mate in sides:
        for number, (device, own_ref, oth_ref, slot) in enumerate(sources):
            loads[2 * side + slot].wait()
            for n in range(canv):
                rows_down(boxes_ref, device * canv + n, box_count, xbuf.at[slot, pl.ds(n * PX, PX)], xd, n, 2 * canv)
                xd[canv + n] = xbuf[slot, n * PX : (n + 1) * PX]
                cols_across(boxes_ref, device * canv + n, n, box_count, own_ref, oth_ref, lhs)
                if number:
                    select, count = members(
                        boxes_ref, device * canv + n, box_count, lambda row: cells_ref[:, row : row + 1], (CELLS, PX), 1
                    )
                    sums = dot(select.astype(BF16), xbuf[slot, n * PX : (n + 1) * PX])
                    pool_mate[side, n * CELLS : (n + 1) * CELLS] = (sums / count).astype(BF16)
            if side == 0:
                loads[2 + slot].start()
            for d in range(9):
                across = xd[d // 3 * canv : (d // 3 + 1) * canv].reshape(pixels, span)
                found = dot(lhs[d % 3], across)
                acc[d] = found if number == 0 else acc[d] + found
        split_out(9, bit, acc, keep, send)
        mate_copies.append(mate_copy(side, send, recv, mate))
        mate_copies[-1].start()
        if side == 0:
            for number, (source, target) in enumerate(((zga0, zga1), (zgb0, zgb1))):
                near[3 + number].wait_recv()
                swaps.append(swap_copy(7 + number, source, target))
                swaps[-1].start()

    for side in range(2):
        source = pooled_any.at[:, pl.ds(side * span, span)]
        loads.append(pltpu.make_async_copy(source, xd.at[side, pl.ds(0, rows)], load_sem.at[4 + side]))
        loads[-1].start()
    for number in (5, 7, 8):
        swaps[number].wait_recv()
    za0, za1 = zpack0.at[0:quarter], zpack1.at[0:quarter]
    zb0, zb1 = zpack0.at[quarter:half], zpack1.at[quarter:half]
    sides = (
        (0, za0, za1, zga0, zga1, y_bit, bkeep_a, bsend_a, brecv_a, y_mate),
        (1, zb0, zb1, zgb0, zgb1, x_bit, bkeep_b, bsend_b, brecv_b, x_mate),
    )
    for side, own0, oth0, own1, oth1, bit, keep, send, recv, mate in sides:
        put_rows(lhs, 0, own0, oth0)
        put_rows(lhs, 1, own1, oth1)
        loads[4 + side].wait()
        for level in range(4):
            left = [jnp.where(levels == level, lhs[k, :, :rows].astype(F32), 0.0).astype(BF16) for k in range(2)]
            acc[level] = dot(left[0], xd[side, :rows]) + dot(left[1], pool_mate[side])
        split_out(4, bit, acc, keep, send)
        mate_copies.append(mate_copy(2 + side, send, recv, mate))
        mate_copies[-1].start()

    ways = [fb_way]

    def pass_on(number, keep, recv, target):
        mate_copies[number].wait_recv()

        def add(d, carry):
            for part in range(parts):
                keep[part, d] = (keep[part, d].astype(F32) + recv[part, d].astype(F32)).astype(BF16)
            return carry

        lax.fori_loop(0, keep.shape[1], add, 0)
        ways.append(Halving(1 + number, keep, target))
        ways[-1].send()

    fb_way.receive()

    swaps[1].wait_recv()
    swaps[6].wait_recv()
    for n in range(canv):
        gate = pixel_gates(boxes_ref, n, box_count, (PX, CELLS), 0)
        at = slice(n * PX, (n + 1) * PX)
        for which, ref in ((chan, df0), (1 - chan, df1)):
            into = pl.ds(pl.multiple_of(which * half, half), half)
            df = ref[at].astype(F32)
            xd[canv + n, :, into] = ref[at]
            xd[n, :, into] = (wide(gate(0, 1), half // CELLS) * pltpu.roll(df, PX - 1, 0)).astype(BF16)
            xd[2 * canv + n, :, into] = (wide(gate(0, -1), half // CELLS) * pltpu.roll(df, 1, 0)).astype(BF16)

    width = wbuf.shape[1]
    tiles = wfx_any.shape[1] // width

    def tile(t, carry):
        tile_load(t).wait()

        @pl.when(t + 1 < tiles)
        def _():
            tile_load(t + 1).start()

        first = lax.rem(t, 2) * 9
        for n in range(canv):
            at = slice(n * PX, (n + 1) * PX)
            gate = pixel_gates(boxes_ref, n, box_count, (PX, CELLS), 0)
            total = None
            for dy in range(3):
                found = dot_nt(xd[n], wbuf[first + dy * 3])
                for dx in range(1, 3):
                    found = found + dot_nt(xd[dx * canv + n], wbuf[first + dy * 3 + dx])
                if dy != 1:
                    found = wide(gate(1 - dy, 0), width // CELLS) * pltpu.roll(found, ((dy - 1) * CW) % PX, 0)
                total = found if total is None else total + found
            gx_ref[at, pl.ds(pl.multiple_of(t * width, width), width)] = total.astype(BF16)
        return carry

    lax.fori_loop(0, 2, tile, 0)
    pass_on(0, keep_a, recv_a, zrecv_a)
    lax.fori_loop(2, tiles, tile, 0)
    pass_on(1, keep_b, recv_b, zrecv_b)

    wbr_load = pltpu.make_async_copy(wbr_any, wbuf.at[pl.ds(0, wbr_any.shape[0])], load_sem.at[6])
    wbr_load.start()
    wbr_load.wait()
    per_level = wbr_any.shape[0] // 4
    for level in range(4):
        for which, ref in ((chan, dz0), (1 - chan, dz1)):
            into = pl.ds(pl.multiple_of(which * half, half), half)
            for m in range(canv):
                at = slice(m * CELLS, (m + 1) * CELLS)
                mine = jnp.where(cells_ref[:, 4:5] == level, ref[at].astype(F32), 0.0)
                xd[level, at, into] = mine.astype(BF16)
    for side in range(2):
        total = 0.0
        for level in range(4):
            first = level * per_level + side * per_level // 2
            w = wbuf[first : first + per_level // 2].reshape(span, 2 * half)
            total = total + dot_nt(xd[level, :rows], w)
        for m in range(canv):
            _, _, high, across = by_box(boxes_ref, m, cells_ref[:, 0:1], box_count)
            r0, r1, c0, c1 = member_bounds(lambda row: cells_ref[:, row : row + 1], high, across)
            at = slice(m * CELLS, (m + 1) * CELLS)
            pool_mate[side, at] = (total[at] / ((r1 - r0) * (c1 - c0))).astype(BF16)
    for n in range(canv):
        at = slice(n * PX, (n + 1) * PX)
        select, _ = members(boxes_ref, n, box_count, lambda row: lanes_ref[row : row + 1, :], (PX, CELLS), 0)
        for side in range(2):
            into = slice(side * span, (side + 1) * span)
            pooled = dot(select.astype(BF16), pool_mate[side, n * CELLS : (n + 1) * CELLS])
            gx_ref[at, into] = (gx_ref[at, into].astype(F32) + pooled).astype(BF16)

    pass_on(2, bkeep_a, brecv_a, bzrecv_a)
    pass_on(3, bkeep_b, brecv_b, bzrecv_b)
    for stage in range(1, stages):
        for way in ways:
            if len(way.copies) == stage:
                way.receive()

    stores = []

    def finish(way, out, at, sides):
        way.receive()
        keep, recv = way.keep, way.recv
        count = keep.shape[1]
        lanes_of = keep.shape[3] // len(sides)

        def add(d, carry):
            total = keep[way.kept(stages), d].astype(F32) + recv[parts - 2, d].astype(F32)
            for place_at, _ in enumerate(sides):
                row = at + place_at * each
                acc[d, row : row + each] = total[:, place_at * lanes_of : (place_at + 1) * lanes_of]
            return carry

        lax.fori_loop(0, count, add, 0)
        for place_at, side in enumerate(sides):
            source = acc.at[pl.ds(0, count), pl.ds(at + place_at * each, each), :]
            target = out.at[:, :, pl.ds(side * lanes_of, lanes_of)]
            stores.append(pltpu.make_async_copy(source, target, store_sem.at[len(stores)]))
            stores[-1].start()

    finish(ways[0], out_fb, 0, (0, 1))
    finish(ways[1], out_fx, 2 * each, (0,))
    finish(ways[2], out_fx, 3 * each, (1,))
    finish(ways[3], out_br, 4 * each, (0,))
    finish(ways[4], out_br, 5 * each, (1,))
    for copy in stores:
        copy.wait()
    dw_swap.wait()
    for copy in mate_copies + swaps + near + y_near + [copy for way in ways for copy in way.copies]:
        copy.wait_send()


def launch(kernel, **rest):
    return pl.pallas_call(kernel, **rest)


def whole(shape):
    return pl.BlockSpec(shape, lambda i: (0,) * len(shape))


def shaped(shape, kind):
    return jax.ShapeDtypeStruct(shape, kind)


def per_device(features, boxes, w_branch, gain_branch, bias_branch, w_fx, w_fb, gain_join, bias_join, w_cls, b_cls, grad_logits):
    canv, box_count = boxes.shape[:2]
    pixels, cin = features.shape
    mid = gain_join.shape[0]
    half = mid // lax.axis_size("chan")
    bw = gain_branch.shape[1]
    br = w_branch.shape[2]
    ncls = w_cls.shape[1]
    dp = lax.axis_size("dp")
    parts = dp // PLANE
    each = mid // dp
    cols = parts * each
    rows = canv * CELLS
    chan = lax.axis_index("chan")
    me = lax.axis_index("dp")
    rows_all = [float(canv * dp * box_count * s * s) for s in BINS]
    lanes_np = cell_table(box_count)
    lanes = jnp.asarray(lanes_np)
    cells = jnp.asarray(np.concatenate([lanes_np.T, np.zeros((CELLS, CELLS - 8), np.float32)], 1))

    span = cin // 2
    tile = cin // 4
    stages = parts.bit_length() - 1
    quarter = half // 2
    bundle = quarter // 2

    def swap(array):
        return lax.ppermute(array, "chan", [(0, 1), (1, 0)])

    def sems(*counts):
        return [pltpu.SemaphoreType.DMA((count,)) for count in counts]

    flat = boxes.reshape(-1)
    box_tile = jnp.zeros((8 * CELLS,), jnp.int32).at[: flat.shape[0]].set(flat).reshape(8, CELLS)
    (
        pooled, y, z_norm, z_act, z_total, boxes_all, logits, df, pack, send_a, send_b, send_d, dw_cls, db_total, x_mate, y_mate,
    ) = launch(
        functools.partial(front_kernel, canv, box_count, dp, each, rows_all),
        in_specs=[SMEM_SPEC] + [VMEM_SPEC] * 10 + [ANY_SPEC] * 4,
        out_specs=[VMEM_SPEC] * 14 + [ANY_SPEC] * 2,
        out_shape=[
            shaped((rows, cin), BF16),
            shaped((rows, bw), BF16),
            shaped((rows, bw), F32),
            shaped((rows, bw), F32),
            shaped((8, bw), F32),
            shaped((PLANE, 8, CELLS), jnp.int32),
            shaped((pixels, ncls), BF16),
            shaped((pixels, half), BF16),
            shaped((2 * half, pixels), BF16),
            shaped((quarter, pixels), BF16),
            shaped((quarter, pixels), BF16),
            shaped((bundle, pixels), BF16),
            shaped((dp, half // dp, ncls), F32),
            shaped((8, half), F32),
            shaped((pixels, span), BF16),
            shaped((pixels, span), BF16),
        ],
        scratch_shapes=[
            pltpu.VMEM((canv, PX, cin), BF16),
            pltpu.VMEM((2 * canv, PX, cin), BF16),
            pltpu.VMEM((4, cin, br), BF16),
            pltpu.VMEM((3, 3, cin, mid), BF16),
            pltpu.VMEM((canv, PX, 9 * CELLS), BF16),
            pltpu.VMEM((canv, 9 * CELLS, mid), BF16),
            pltpu.VMEM((canv, PX, mid), F32),
            pltpu.VMEM((rows, 4 * bw), BF16),
            pltpu.VMEM((rows, br), F32),
            pltpu.VMEM((rows, bw), BF16),
            pltpu.VMEM((rows, bw), BF16),
            pltpu.VMEM((half, ncls), F32),
            pltpu.VMEM((pixels, half), BF16),
            pltpu.VMEM((pixels, half), BF16),
            pltpu.VMEM((pixels, half), F32),
            pltpu.VMEM((pixels, half), F32),
            pltpu.VMEM((pixels, ncls), BF16),
            pltpu.VMEM((pixels, ncls), BF16),
            pltpu.VMEM((half, PX), F32),
        ]
        + exchange_scratch(dp, half, 3)
        + sems(3, 3, 7, 7, canv + 7),
        compiler_params=pltpu.CompilerParams(vmem_limit_bytes=63 * 2**20, collective_id=1, has_side_effects=True),
        name="front",
    )(
        flat, box_tile, lanes, cells, gain_branch, bias_branch, gain_join.reshape(1, mid), bias_join.reshape(1, mid),
        w_cls, b_cls.reshape(1, ncls), grad_logits, features, w_branch, w_fx.reshape(3, 3, cin, mid),
        w_fb.reshape(3, 3, 4 * bw, mid),
    )
    flat_all = boxes_all.reshape(PLANE, -1)[:, : flat.shape[0]].reshape(-1)

    def buffers(count, width):
        return [
            pltpu.VMEM((parts, count, each, width), BF16),
            pltpu.VMEM((parts, count, each, width), BF16),
            pltpu.VMEM((parts, count, each, width), BF16),
            pltpu.VMEM((parts - 1, count, each, width), BF16),
        ]

    near_rows = [pltpu.VMEM((quarter, pixels), BF16)] * 4 + [pltpu.VMEM((bundle, pixels), BF16)] * 2
    near_rows.append(pltpu.VMEM((PLANE - 1, rows, bw), BF16))
    near_cells = [pltpu.VMEM((quarter, rows), BF16)] * 6
    grad_features, sum_fx, sum_fb, sum_br, da_total, dw_own, dw_other = launch(
        functools.partial(tail_kernel, canv, box_count, dp, rows_all),
        in_specs=[SMEM_SPEC] + [VMEM_SPEC] * 3 + [ANY_SPEC] * 3 + [VMEM_SPEC] * 6 + [ANY_SPEC] * 8,
        out_specs=[VMEM_SPEC] + [ANY_SPEC] * 3 + [VMEM_SPEC] * 2 + [ANY_SPEC],
        out_shape=[
            shaped((pixels, cin), BF16),
            shaped((9, each, cin), F32),
            shaped((9, each, 4 * bw), F32),
            shaped((4, each, cin), F32),
            shaped((8, bw), F32),
            shaped((dp, half // dp, ncls), F32),
            shaped((dp, half // dp, ncls), F32),
        ],
        scratch_shapes=[
            pltpu.VMEM((dp, half // dp, ncls), F32),
            pltpu.VMEM((half // dp, ncls), F32),
            pltpu.SemaphoreType.DMA((2, dp)),
            pltpu.SemaphoreType.DMA((2, dp)),
            pltpu.VMEM((2 * half, pixels), BF16),
            pltpu.VMEM((pixels, half), BF16),
        ]
        + near_rows
        + [pltpu.VMEM((bw, rows), BF16), pltpu.VMEM((bw, rows), BF16)]
        + near_cells
        + [pltpu.VMEM((rows, bw), BF16), pltpu.VMEM((rows, bw), BF16), pltpu.VMEM((rows, bw), F32)]
        + exchange_scratch(dp, bw, 1)
        + sems(10, 10, 8, 8)
        + [
            pltpu.VMEM((PX, 9 * CELLS), BF16),
            pltpu.VMEM((9, cols, PLANE * rows), BF16),
            pltpu.VMEM((2, pixels, span), BF16),
            pltpu.VMEM((18, tile, mid), BF16),
            pltpu.VMEM((3 * canv, PX, mid), BF16),
            pltpu.VMEM((3, half, pixels), BF16),
            pltpu.VMEM((9, half, span), F32),
            pltpu.VMEM((2, rows, span), BF16),
            pltpu.VMEM((parts, 9, each, 4 * bw), BF16),
            pltpu.VMEM((parts - 1, 9, each, 4 * bw), BF16),
        ]
        + buffers(9, span)
        + buffers(9, span)
        + buffers(4, span)
        + buffers(4, span)
        + sems(7, 6, 2, 4, 4, 4, 5 * stages, 5 * stages),
        compiler_params=pltpu.CompilerParams(vmem_limit_bytes=63 * 2**20, collective_id=4, has_side_effects=True),
        name="tail",
    )(
        flat_all, lanes, cells, pack, send_a, send_b, send_d, df, y, z_norm, z_act, z_total, gain_branch, dw_cls, pooled,
        features, x_mate, y_mate, w_fx, w_fb, w_branch.reshape(16, tile, br),
    )
    out_fx = jnp.transpose(sum_fx, (0, 2, 1))
    out_fb = jnp.transpose(sum_fb.reshape(9, each, 4, bw), (0, 2, 3, 1))
    out_br = jnp.transpose(sum_br, (0, 2, 1))

    small = db_total[:2]
    small_got = swap(small)
    small_all = jnp.concatenate([jnp.where(chan == 0, small, small_got), jnp.where(chan == 0, small_got, small)], 1)
    dw_halves = [jnp.where(chan == 0, dw_own, dw_other), jnp.where(chan == 0, dw_other, dw_own)]
    grad_w_cls = jnp.concatenate([a.reshape(half, ncls) for a in dw_halves], 0)
    return (
        logits,
        grad_features,
        out_br,
        da_total[:4],
        da_total[4:],
        out_fx,
        out_fb,
        small_all[0],
        small_all[1],
        grad_w_cls,
        db_total[2, :ncls],
    )


def solution(mesh):
    return jax.shard_map(
        per_device,
        mesh=mesh,
        in_specs=(
            P("dp", "chan"),
            P("dp", None, None),
            P(None, "chan", None),
            P(None, "chan"),
            P(None, "chan"),
            P(None, "chan", None),
            P(None, None, "chan", None),
            P(),
            P(),
            P(),
            P(),
            P("dp", None),
        ),
        out_specs=(
            P("dp", None),
            P("dp", "chan"),
            P(None, "chan", "dp"),
            P(None, "chan"),
            P(None, "chan"),
            P(None, "chan", "dp"),
            P(None, None, "chan", "dp"),
            P(),
            P(),
            P(),
            P(),
        ),
        check_vma=False,
    )
```

```python
import functools

import jax
import jax.numpy as jnp
import numpy as np
from jax import lax
from jax.experimental import pallas as pl
from jax.experimental.pallas import tpu as pltpu
from jax.sharding import PartitionSpec as P

CH = 16
CW = 32
PX = CH * CW
EPS = 1e-05
BINS = (1, 2, 3, 6)
CELLS = 128
PLANE = 4
F32 = jnp.float32
BF16 = jnp.bfloat16
MESH = pl.DeviceIdType.MESH
VMEM_SPEC = pl.BlockSpec(memory_space=pltpu.VMEM)
SMEM_SPEC = pl.BlockSpec(memory_space=pltpu.SMEM)
ANY_SPEC = pl.BlockSpec(memory_space=pl.ANY)
NT = (((1,), (1,)), ((), ()))
TN = (((0,), (0,)), ((), ()))


def dot(a, b):
    return jnp.dot(a, b, preferred_element_type=F32)


def dot_nt(a, b):
    return lax.dot_general(a, b, NT, preferred_element_type=F32)


def dot_tt(a, b):
    return lax.dot_general(a, b, (((0,), (1,)), ((), ())), preferred_element_type=F32)


def dot_tn(a, b):
    return lax.dot_general(a, b, TN, preferred_element_type=F32)


def cell_table(box_count):
    table = np.zeros((8, CELLS), np.float32)
    table[1] = 1.0
    table[4] = 9.0
    at = 0
    for level, bins in enumerate(BINS):
        for box in range(box_count):
            for i in range(bins):
                for j in range(bins):
                    table[:6, at] = (box, bins, i, j, level, 1.0)
                    at += 1
    return table


def box_at(boxes_ref, canvas, box, box_count):
    base = (canvas * box_count + box) * 4
    return [boxes_ref[base + part] for part in range(4)]


def by_box(boxes_ref, canvas, which, box_count):
    sides = None
    for box in range(box_count):
        mine = [side.astype(F32) for side in box_at(boxes_ref, canvas, box, box_count)]
        if sides is None:
            sides = [jnp.full(which.shape, side, F32) for side in mine]
        else:
            sides = [jnp.where(which == box, new, old) for new, old in zip(mine, sides)]
    return sides


def within(relative, extent):
    return (relative >= 0) & (relative < extent)


def pixel_gates(boxes_ref, canvas, box_count, shape, axis):
    place = lax.broadcasted_iota(jnp.int32, shape, axis)
    row = place >> 5
    col = place & (CW - 1)
    rel = []
    for box in range(box_count):
        top, left, height, width = box_at(boxes_ref, canvas, box, box_count)
        rel.append((row - top, col - left, height, width))

    def gate(dy, dx):
        total = None
        for y, x, height, width in rel:
            hit = within(y, height) & within(x, width)
            if not isinstance(dy, int) or dy:
                hit = hit & within(y + dy, height)
            if not isinstance(dx, int) or dx:
                hit = hit & within(x + dx, width)
            value = jnp.where(hit, 1.0, 0.0)
            total = value if total is None else total + value
        return total

    return gate


def wide(column_block, times):
    return jnp.concatenate([column_block] * times, axis=1)


def rows_down(boxes_ref, canvas, box_count, x, xs, n, below):
    gate = pixel_gates(boxes_ref, canvas, box_count, (PX, CELLS), 0)
    reps = xs.shape[2] // CELLS
    blank = jnp.zeros((CW, xs.shape[2]), BF16)
    xs[n, 0:CW] = blank
    xs[n, CW:PX] = x[0 : PX - CW] * wide(gate(-1, 0).astype(BF16), reps)[CW:]
    xs[below + n, 0 : PX - CW] = x[CW:PX] * wide(gate(1, 0).astype(BF16), reps)[: PX - CW]
    xs[below + n, PX - CW : PX] = blank


def member_bounds(table_at, height, width):
    bins, i, j = table_at(1), table_at(2), table_at(3)

    def start(at, extent):
        return jnp.floor((at * extent + 0.5) / bins)

    def stop(at, extent):
        return jnp.floor(((at + 1) * extent + bins - 0.5) / bins)

    return start(i, height), stop(i, height), start(j, width), stop(j, width)


def members(boxes_ref, canvas, box_count, table_at, shape, axis):
    top, left, height, width = by_box(boxes_ref, canvas, table_at(0), box_count)
    r0, r1, c0, c1 = member_bounds(table_at, height, width)
    place = lax.broadcasted_iota(jnp.int32, shape, axis)
    row = (place >> 5).astype(F32) - top
    col = (place & (CW - 1)).astype(F32) - left
    hit = (row >= r0) & (row < r1) & (col >= c0) & (col < c1) & (table_at(5) > 0)
    return jnp.where(hit, 1.0, 0.0), (r1 - r0) * (c1 - c0)


def gated_lifts(boxes_ref, canvas, box_count, lanes_ref, store):
    def table_at(row):
        return lanes_ref[row : row + 1, :]

    top, left, height, width = by_box(boxes_ref, canvas, table_at(0), box_count)

    def side(size, edge, extent, cell):
        relative = lax.broadcasted_iota(jnp.int32, (size, CELLS), 0).astype(F32) - edge
        scale = (table_at(1) - 1.0) / (extent - 1.0)
        own = within(relative, extent)
        found = []
        for step in (-1, 0, 1):
            moved = relative + step
            weight = jnp.maximum(0.0, 1.0 - jnp.abs(moved * scale - cell))
            found.append(jnp.where(own & within(moved, extent), weight, 0.0))
        return found

    rows = [found * table_at(5) for found in side(CH, top, height, table_at(2))]
    cols = side(CW, left, width, table_at(3))
    for d in range(9):
        for y in range(CH):
            store(d, y, (rows[d // 3][y : y + 1] * cols[d % 3]).astype(BF16))


def pltranspose(block):
    return jnp.transpose(block, (1, 0))


def signal_all(total, chan_too=False):
    me = lax.axis_index("dp")
    chan = lax.axis_index("chan")
    barrier = pltpu.get_barrier_semaphore()

    def signal(step, carry):
        pl.semaphore_signal(barrier, inc=1, device_id=(lax.rem(me + step, total), chan), device_id_type=MESH)
        return carry

    lax.fori_loop(1, total, signal, 0)
    if chan_too:
        pl.semaphore_signal(barrier, inc=1, device_id=(me, 1 - chan), device_id_type=MESH)
    return total if chan_too else total - 1


class Exchange:
    def __init__(self, total, own, slots, send_sem, recv_sem, parted=False):
        self.total, self.own, self.slots, self.send_sem, self.recv_sem = total, own, slots, send_sem, recv_sem
        self.me = lax.axis_index("dp")
        self.parted = parted

    def block(self, device):
        return self.own.at[device] if self.parted else self.own

    def copy_to(self, step):
        return pltpu.make_async_remote_copy(
            src_ref=self.block(lax.rem(self.me + step, self.total)),
            dst_ref=self.slots.at[self.me],
            send_sem=self.send_sem.at[step],
            recv_sem=self.recv_sem.at[self.me],
            device_id=(lax.rem(self.me + step, self.total), lax.axis_index("chan")),
            device_id_type=MESH,
        )

    def copy_from(self, step):
        other = lax.rem(self.me + self.total - step, self.total)
        return pltpu.make_async_remote_copy(
            src_ref=self.block(other),
            dst_ref=self.slots.at[other],
            send_sem=self.send_sem.at[step],
            recv_sem=self.recv_sem.at[other],
            device_id=(other, lax.axis_index("chan")),
            device_id_type=MESH,
        )

    def start(self):
        if self.parted:
            keep = pltpu.make_async_copy(self.block(self.me), self.slots.at[self.me], self.recv_sem.at[self.me])
            keep.start()
            keep.wait()
        else:
            self.slots[self.me] = self.own[...]

        def one(step, carry):
            self.copy_to(step).start()
            return carry

        lax.fori_loop(1, self.total, one, 0)

    def arrive(self):
        def one(step, carry):
            self.copy_from(step).wait_recv()
            return carry

        def sent(step, carry):
            self.copy_to(step).wait_send()
            return carry

        lax.fori_loop(1, self.total, one, 0)
        lax.fori_loop(1, self.total, sent, 0)

    def finish(self):
        self.arrive()
        value = self.slots[0]
        for other in range(1, self.total):
            value = value + self.slots[other]
        return value


def exchange_scratch(total, width, times):
    return [
        pltpu.VMEM((times, 8, width), F32),
        pltpu.VMEM((times, total, 8, width), F32),
        pltpu.SemaphoreType.DMA((times, total)),
        pltpu.SemaphoreType.DMA((times, total)),
    ]


def core_copy(source, target, send_sem, recv_sem):
    return pltpu.make_async_remote_copy(
        src_ref=source,
        dst_ref=target,
        send_sem=send_sem,
        recv_sem=recv_sem,
        device_id=(lax.axis_index("dp"), 1 - lax.axis_index("chan")),
        device_id_type=MESH,
    )


def branch_stat(total_ref, level, rows_all):
    mean = total_ref[level : level + 1, :] / rows_all
    var = total_ref[4 + level : 5 + level, :] / rows_all - mean * mean
    return mean, lax.rsqrt(var + EPS)


def expand(y, cells_ref, keep, at):
    width = y.shape[1]
    for n in range(y.shape[0] // CELLS):
        rows = slice(n * CELLS, (n + 1) * CELLS)
        block = y[rows].astype(F32)
        for level in range(4):
            mine = jnp.where(cells_ref[:, 4:5] == level, block, 0.0)
            keep[at + n * CELLS : at + (n + 1) * CELLS, level * width : (level + 1) * width] = mine.astype(BF16)


def front_kernel(
    canv, box_count, total, each, rows_all,
    boxes_ref, box_ref, lanes_ref, cells_ref, zgain_ref, zbias_ref, gain_ref, bias_ref, w_ref, bcls_ref, g_ref,
    x_any, wbr_any, wfx_any, wfb_any,
    pooled_ref, y_ref, norm_ref, act_ref, ztotal_ref, boxes_all, logits_ref, df_ref, pack_ref, send_a, send_b, send_d,
    dw_ref, sums_ref, xm_any, ym_any,
    x, xs, wbr, wbuf, lifts, terms, fjoin, ye, zs, zsend, zgot, dw, fsend, got, f, db, score, score_got, flip,
    part, slots, send_sem, recv_sem, core_send, core_recv, near_send, near_recv, load_sem,
):
    me = lax.axis_index("dp")
    chan = lax.axis_index("chan")
    x_mate = me + 1 - 2 * (me % 2)
    y_mate = me + 2 - 4 * ((me // 2) % 2)
    span = xm_any.shape[1]
    half = df_ref.shape[1]
    mid = 2 * half
    ncls = g_ref.shape[0]
    own = pl.ds(pl.multiple_of(chan * half, half), half)
    away = pl.ds(pl.multiple_of((1 - chan) * half, half), half)
    expected = signal_all(total, True)
    loads = [pltpu.make_async_copy(x_any.at[pl.ds(n * PX, PX)], x.at[n], load_sem.at[n]) for n in range(canv)]
    loads.append(pltpu.make_async_copy(wbr_any, wbr, load_sem.at[canv]))
    loads += [pltpu.make_async_copy(wfx_any.at[:, t], wbuf.at[t], load_sem.at[canv + 1 + t]) for t in range(3)]
    for copy in loads:
        copy.start()

    def near_copy(number, source, target, mate):
        return pltpu.make_async_remote_copy(
            src_ref=source, dst_ref=target, send_sem=near_send.at[number], recv_sem=near_recv.at[number],
            device_id=(mate, chan), device_id_type=MESH,
        )

    def share(number, first, last):
        at = pl.ds(first * PX, (last - first) * PX)
        copies = [
            near_copy(number, x_any.at[at, pl.ds(0, span)], xm_any.at[at], x_mate),
            near_copy(number + 1, x_any.at[at, pl.ds(span, span)], ym_any.at[at], y_mate),
        ]
        for copy in copies:
            copy.start()
        return copies

    def table_at(row):
        return cells_ref[:, row : row + 1]

    part[...] = jnp.zeros_like(part)
    near = []
    for n in range(canv):
        loads[n].wait()
        select, count = members(boxes_ref, n, box_count, table_at, (CELLS, PX), 1)
        pooled_ref[n * CELLS : (n + 1) * CELLS] = (dot(select.astype(BF16), x[n]) / count).astype(BF16)
        if n == 0:
            pl.semaphore_wait(pltpu.get_barrier_semaphore(), expected)
            near += share(0, 0, 1)
            boxes_all[0] = box_ref[...]
            for number, mate in ((1, x_mate), (2, y_mate), (3, x_mate + y_mate - me)):
                near.append(near_copy(3 + number, box_ref, boxes_all.at[number], mate))
                near[-1].start()
    loads[canv].wait()
    for level in range(4):
        found = dot(pooled_ref[...], wbr[level])
        for n in range(canv):
            rows = slice(n * CELLS, (n + 1) * CELLS)
            mine = jnp.where(table_at(4) == level, found[rows], 0.0)
            zs[rows, :] = mine if level == 0 else zs[rows, :] + mine
    zsend[...] = zs[:, away].astype(BF16)
    swap_z = core_copy(zsend, zgot, core_send.at[0], core_recv.at[0])
    swap_z.start()
    for n in range(canv):
        rows_down(boxes_ref, n, box_count, x.at[n], xs, n, canv)

        def store(d, y, block, n=n):
            lifts[n, y * CW : (y + 1) * CW, d * CELLS : (d + 1) * CELLS] = block

        gated_lifts(boxes_ref, n, box_count, lanes_ref, store)
    swap_z.wait()
    bw = y_ref.shape[1]
    for n in range(canv):
        rows = slice(n * CELLS, (n + 1) * CELLS)
        z = zs[rows, own] + zgot[rows].astype(F32)
        norm_ref[rows] = z
        for level in range(4):
            mine = jnp.where(table_at(4) == level, z, 0.0)
            part[0, level : level + 1, :] += jnp.sum(mine, 0, keepdims=True)
            part[0, 4 + level : 5 + level, :] += jnp.sum(mine * mine, 0, keepdims=True)
    z_sums = Exchange(total, part.at[0], slots.at[0], send_sem.at[0], recv_sem.at[0])
    z_sums.start()

    def features_part(t):
        loads[canv + 1 + t].wait()
        for n in range(canv):
            q = dot(xs[n], wbuf[t, 0]) + dot(x[n], wbuf[t, 1]) + dot(xs[canv + n], wbuf[t, 2])
            gate = pixel_gates(boxes_ref, n, box_count, (PX, CELLS), 0)
            if t == 0:
                fjoin[n] = wide(gate(0, -1), mid // CELLS) * pltpu.roll(q, 1, 0)
            elif t == 1:
                fjoin[n] += wide(gate(0, 0), mid // CELLS) * q
            else:
                fjoin[n] += wide(gate(0, 1), mid // CELLS) * pltpu.roll(q, PX - 1, 0)
        loads.append(pltpu.make_async_copy(wfb_any.at[:, t], wbuf.at[t], load_sem.at[canv + 4 + t]))
        loads[-1].start()

    features_part(0)
    z_total = z_sums.finish()
    ztotal_ref[...] = z_total
    near += share(2, 1, canv)
    for n in range(canv):
        rows = slice(n * CELLS, (n + 1) * CELLS)
        z = norm_ref[rows]
        norm = act = 0.0
        for level in range(4):
            mean, rstd = branch_stat(ztotal_ref, level, rows_all[level])
            here = jnp.where(table_at(4) == level, 1.0, 0.0)
            mine = (z - mean) * rstd
            norm = norm + here * mine
            act = act + here * (zgain_ref[level : level + 1, :] * mine + zbias_ref[level : level + 1, :])
        norm_ref[rows] = norm
        act_ref[rows] = act
        value = act * jax.nn.sigmoid(act)
        y_ref[rows] = value.astype(BF16)
        for level in range(4):
            mine = jnp.where(table_at(4) == level, value, 0.0)
            ye[rows, level * bw : (level + 1) * bw] = mine.astype(BF16)
    features_part(1)
    features_part(2)

    for t in range(3):
        loads[canv + 4 + t].wait()
        for dy in range(3):
            term = dot(ye[...], wbuf[t, dy]).astype(BF16)
            at = (dy * 3 + t) * CELLS
            for n in range(canv):
                terms[n, at : at + CELLS] = term[n * CELLS : (n + 1) * CELLS]
    for n in range(canv):
        fjoin[n] += dot(lifts[n], terms[n])
        fsend[n * PX : (n + 1) * PX] = fjoin[n, :, away].astype(BF16)
    swap_f = core_copy(fsend, got, core_send.at[1], core_recv.at[1])
    swap_f.start()
    dw[...] = jnp.zeros_like(dw)
    area = 0
    for n in range(canv):
        for box in range(box_count):
            side = box_at(boxes_ref, n, box, box_count)
            area = area + side[2] * side[3]
    part[1, 2:3, :] = jnp.full((1, half), area.astype(F32), F32)
    swap_f.wait()
    for n in range(canv):
        rows = slice(n * PX, (n + 1) * PX)
        value = fjoin[n, :, own] + got[rows].astype(F32)
        f[rows] = value
        part[1, 0:1, :] += jnp.sum(value, 0, keepdims=True)
        part[1, 1:2, :] += jnp.sum(value * value, 0, keepdims=True)
    first = Exchange(total, part.at[1], slots.at[1], send_sem.at[1], recv_sem.at[1])
    first.start()
    f_total = first.finish()
    count = f_total[2:3, :]
    mean = f_total[0:1, :] / count
    rstd = lax.rsqrt(f_total[1:2, :] / count - mean * mean + EPS)
    gain, bias, w = gain_ref[:, own], bias_ref[:, own], w_ref[:, own]
    ones = jnp.ones((8, PX), BF16)
    valid = [wide(pixel_gates(boxes_ref, n, box_count, (PX, CELLS), 0)(0, 0), half // CELLS) for n in range(canv)]
    for n in range(canv):
        rows = slice(n * PX, (n + 1) * PX)
        norm = (f[rows] - mean) * rstd
        f[rows] = norm
        act = gain * norm + bias
        sig = jax.nn.sigmoid(act)
        hidden = (act * sig * valid[n]).astype(BF16)
        g = g_ref[:, rows]
        score[:, rows] = dot_nt(w, hidden).astype(BF16)
        value = dot_tn(g, w) * valid[n] * sig * (1.0 + act * (1.0 - sig))
        db[rows] = value
        part[2, 0:1, :] += jnp.sum(value * norm, 0, keepdims=True)
        part[2, 1:2, :] += jnp.sum(value, 0, keepdims=True)
        part[2, 2:3, :ncls] += dot_nt(ones, g)[0:1]
        dw[...] += dot_tt(hidden, g)
    second = Exchange(total, part.at[2], slots.at[2], send_sem.at[2], recv_sem.at[2])
    second.start()
    swap_score = core_copy(score, score_got, core_send.at[2], core_recv.at[2])
    swap_score.start()
    sums = second.finish()
    sums_ref[...] = sums
    scale = gain * rstd
    for n in range(canv):
        rows = slice(n * PX, (n + 1) * PX)
        df = scale * (db[rows] - sums[1:2, :] / count - f[rows] * (sums[0:1, :] / count)) * valid[n]
        df_ref[rows] = df.astype(BF16)
        flip[...] = pltranspose(df)
        span = pl.ds(n * PX, PX)
        pack_ref[0:half, span] = flip[...].astype(BF16)
        views = [pack_ref.at[half : half + half // 2, span], send_a.at[:, span]]
        views += [pack_ref.at[half + half // 2 : 2 * half, span], send_b.at[:, span], send_d.at[:, span]]
        split_rows(flip, half // (4 * each), each, *views)
    strip = dw_ref.shape[1]
    for device in range(total):
        dw_ref[device] = dw[device * strip : (device + 1) * strip]
    swap_score.wait()
    for n in range(canv):
        rows = slice(n * PX, (n + 1) * PX)
        both = score[:, rows].astype(F32) + score_got[:, rows].astype(F32)
        logits_ref[:, rows] = (both + bcls_ref[...]).astype(BF16)
    for copy in near:
        copy.wait()


def split_rows(rows, groups, each, own_a, send_a, own_b, send_b, send_d=None):
    me = lax.axis_index("dp")
    x_bit = me % 2
    y_bit = (me // 2) % 2

    def piece(group, y, x):
        return rows[pl.ds(pl.multiple_of(((group * 2 + y) * 2 + x) * each, each), each), :].astype(BF16)

    for group in range(groups):
        for bit in range(2):
            at = (bit * groups + group) * each
            own_a[at : at + each] = piece(group, bit, x_bit)
            send_a[at : at + each] = piece(group, bit, 1 - x_bit)
            own_b[at : at + each] = piece(group, y_bit, bit)
            send_b[at : at + each] = piece(group, 1 - y_bit, bit)
        if send_d is not None:
            send_d[group * each : (group + 1) * each] = piece(group, 1 - y_bit, 1 - x_bit)


def put_rows(out, index, own_ref, other_ref):
    chan = lax.axis_index("chan")
    size = own_ref.shape[0]
    width = own_ref.shape[1]
    for ref, which in ((own_ref, chan), (other_ref, 1 - chan)):
        into = pl.ds(pl.multiple_of(which * size, size), size)
        if index is None:
            out[into, :width] = ref[...]
        else:
            out[index, into, :width] = ref[...]


def cols_across(boxes_ref, canvas, at, box_count, own_ref, other_ref, lhs):
    chan = lax.axis_index("chan")
    size = own_ref.shape[0]
    span = slice(at * PX, (at + 1) * PX)
    gate = pixel_gates(boxes_ref, canvas, box_count, (8, PX), 1)
    for ref, which in ((own_ref, chan), (other_ref, 1 - chan)):
        into = pl.ds(pl.multiple_of(which * size, size), size)
        value = ref[:, span].astype(F32)
        lhs[0, into, span] = (pltpu.roll(value, PX - 1, 1) * gate(0, 1)[0:1]).astype(BF16)
        lhs[1, into, span] = ref[:, span]
        lhs[2, into, span] = (pltpu.roll(value, 1, 1) * gate(0, -1)[0:1]).astype(BF16)


def reversed_bits(number, bits):
    return sum(((number >> bit) & 1) << (bits - 1 - bit) for bit in range(bits))


def split_out(offsets, bit, acc, keep, send):
    parts, _, each, _ = keep.shape
    groups = parts // 2
    block = groups * each

    def one(d, carry):
        for half in range(2):
            for ref, which in ((keep, bit), (send, 1 - bit)):
                for group in range(groups):
                    at = (half * 2 + which) * block + group * each
                    ref[reversed_bits(half * groups + group, parts.bit_length() - 1), d] = acc[d, pl.ds(pl.multiple_of(at, each), each), :].astype(BF16)
        return carry

    lax.fori_loop(offsets[0], offsets[1], one, 0)


def tail_kernel(
    canv, box_count,
    total_dp, rows_all,
    boxes_ref, lanes_ref, cells_ref, pack0, sa, sb, sd, df0, y0, norm_ref, act_ref, ztotal_ref, zgain_ref, dw_ref,
    pooled_any, x_any, xm_any, ym_any, wfx_any, wfb_any, wbr_any,
    gx_ref, out_fx, out_fb, out_br, sums_ref, dw_own, dw_other,
    dw_slots, dw_sum, dw_send, dw_recv, pack1, df1, ga0, ga1, gb0, gb1, gd0, gd1, y_all, zpack0, zpack1, zsa, zsb, zga0, zga1, zgb0, zgb1, dz0, dz1, da,
    part, slots, sum_send, sum_recv, core_send, core_recv, near_send, near_recv,
    lift, grads, xbuf, wbuf, xd, lhs, acc, pool_mate,
    fb_send, fb_recv, keep_a, send_a, recv_a, zrecv_a, keep_b, send_b, recv_b, zrecv_b,
    bkeep_a, bsend_a, brecv_a, bzrecv_a, bkeep_b, bsend_b, brecv_b, bzrecv_b,
    load_sem, store_sem, w_sem, fb_sem, mate_send, mate_recv, part_send, part_recv,
):
    me = lax.axis_index("dp")
    chan = lax.axis_index("chan")
    parts = fb_send.shape[0]
    pixels = df0.shape[0]
    half = df0.shape[1]
    span = xbuf.shape[2]
    group, place = me // PLANE, me % PLANE
    x_bit, y_bit = me % 2, (me // 2) % 2
    x_mate = me + 1 - 2 * x_bit
    y_mate = me + 2 - 4 * y_bit

    stages = parts.bit_length() - 1

    def group_bit(stage):
        return (group // 2**stage) % 2

    def group_mate(stage):
        return (group + 2**stage * (1 - 2 * group_bit(stage))) * PLANE + place

    d_mate = x_mate + y_mate - me
    expected = signal_all(total_dp, True)

    def load(source, slot, which):
        return pltpu.make_async_copy(source, xbuf.at[slot], load_sem.at[which])

    loads = [
        load(x_any.at[:, pl.ds(0, span)], 0, 0),
        load(xm_any, 1, 1),
        load(x_any.at[:, pl.ds(span, span)], 0, 2),
        load(ym_any, 1, 3),
    ]
    loads[0].start()
    loads[1].start()

    def tile_load(tile):
        width = wbuf.shape[1]
        return pltpu.make_async_copy(
            wfx_any.at[:, pl.ds(pl.multiple_of(tile * width, width), width), :],
            wbuf.at[pl.ds(pl.multiple_of(lax.rem(tile, 2) * 9, 9), 9)],
            w_sem.at[lax.rem(tile, 2)],
        )

    levels_at_once = wfb_any.shape[1]

    def fb_load(d):
        at = d % 4 * levels_at_once
        return pltpu.make_async_copy(wfb_any.at[d], wbuf.at[pl.ds(at, levels_at_once)], fb_sem.at[d % 4])

    for d in range(3):
        fb_load(d).start()

    def mate_copy(number, source, target, mate):
        return pltpu.make_async_remote_copy(
            src_ref=source, dst_ref=target, send_sem=mate_send.at[number], recv_sem=mate_recv.at[number],
            device_id=(mate, chan), device_id_type=MESH,
        )

    class Halving:
        def __init__(self, number, keep, recv, offsets):
            self.number, self.keep, self.recv, self.offsets = number, keep, recv, offsets
            self.copies = []

        def kept(self, stage):
            at = 0
            for bit in range(stage):
                at = at + group_bit(bit) * (parts >> (bit + 1))
            return at

        def send(self):
            stage = len(self.copies)
            count = parts >> (stage + 1)
            from_at = self.kept(stage) + (1 - group_bit(stage)) * count
            number = self.number * stages + stage
            some = pl.ds(self.offsets[0], self.offsets[1] - self.offsets[0])
            copy = pltpu.make_async_remote_copy(
                src_ref=self.keep.at[pl.ds(from_at, count), some],
                dst_ref=self.recv.at[pl.ds(parts - 2 * count, count), some],
                send_sem=part_send.at[number],
                recv_sem=part_recv.at[number],
                device_id=(group_mate(stage), chan),
                device_id_type=MESH,
            )
            copy.start()
            self.copies.append(copy)

        def receive(self):
            stage = len(self.copies)
            self.copies[-1].wait_recv()
            if stage == stages:
                return
            count = parts >> stage
            at = self.kept(stage)

            def add(d, carry):
                for part in range(count):
                    got = self.recv[parts - 2 * count + part, d].astype(F32)
                    self.keep[at + part, d] = (self.keep[at + part, d].astype(F32) + got).astype(BF16)
                return carry

            lax.fori_loop(*self.offsets, add, 0)
            self.send()

    def near_copy(number, source, target, mate):
        return pltpu.make_async_remote_copy(
            src_ref=source, dst_ref=target, send_sem=near_send.at[number], recv_sem=near_recv.at[number],
            device_id=(mate, chan), device_id_type=MESH,
        )

    def swap_copy(number, source, target):
        return core_copy(source, target, core_send.at[number], core_recv.at[number])

    pl.semaphore_wait(pltpu.get_barrier_semaphore(), expected)
    swaps = [swap_copy(0, pack0, pack1), swap_copy(1, df0, df1)]
    near = [near_copy(0, sa, ga0, x_mate), near_copy(1, sb, gb0, y_mate), near_copy(2, sd, gd0, d_mate)]
    y_near = [near_copy(5 + number, y0, y_all.at[number], mate) for number, mate in enumerate((x_mate, y_mate, d_mate))]
    for copy in swaps + near + y_near:
        copy.start()
    dw_parts = Exchange(total_dp, dw_ref, dw_slots, dw_send.at[0], dw_recv.at[0], True)
    dw_parts.start()

    def lift_of(n):
        def store(d, y, block):
            lift[y * CW : (y + 1) * CW, d * CELLS : (d + 1) * CELLS] = block

        gated_lifts(boxes_ref, n, box_count, lanes_ref, store)

    rows = canv * CELLS
    for n in range(canv):
        lift_of(n)
        for ref, which in ((pack0, chan), (pack1, 1 - chan)):
            if n == 0 and ref is pack1:
                swaps[0].wait_recv()
            found = dot(ref[:half, n * PX : (n + 1) * PX], lift[...]).astype(BF16)
            into = pl.ds(pl.multiple_of(which * half, half), half)
            for e in range(9):
                xd[e, into, n * CELLS : (n + 1) * CELLS] = found[:, e * CELLS : (e + 1) * CELLS]

    for d in range(9):
        fb_load(d).wait()
        if d + 3 < 9:
            fb_load(d + 3).start()
        for level in range(4):
            found = dot(wbuf[d % 4 * levels_at_once + level], xd[d, :, :rows])
            acc[level, :, :rows] = found if d == 0 else acc[level, :, :rows] + found
    tile_load(0).start()
    levels = jnp.concatenate([lanes_ref[4:5, :]] * canv, axis=1)
    dy = 0.0
    for level in range(4):
        dy = dy + jnp.where(levels == level, acc[level, :, :rows], 0.0)
    dy = pltranspose(dy)
    sig = jax.nn.sigmoid(act_ref[...])
    da[...] = dy * sig * (1.0 + act_ref[...] * (1.0 - sig))
    for level in range(4):
        gain = bias = 0.0
        for n in range(canv):
            at = slice(n * CELLS, (n + 1) * CELLS)
            mine = jnp.where(cells_ref[:, 4:5] == level, da[at], 0.0)
            gain = gain + jnp.sum(mine * norm_ref[at], 0, keepdims=True)
            bias = bias + jnp.sum(mine, 0, keepdims=True)
        part[0, level : level + 1, :] = gain
        part[0, 4 + level : 5 + level, :] = bias
    exchange = Exchange(total_dp, part.at[0], slots.at[0], sum_send.at[0], sum_recv.at[0])
    exchange.start()
    dw_sum[...] = dw_parts.finish()
    dw_sums = Exchange(total_dp, dw_sum, dw_own, dw_send.at[1], dw_recv.at[1])
    dw_sums.start()
    for number, (source, target) in enumerate(((ga0, ga1), (gb0, gb1), (gd0, gd1))):
        near[number].wait_recv()
        swaps.append(swap_copy(2 + number, source, target))
        swaps[-1].start()
    for number in range(2, 5):
        swaps[number].wait_recv()

    half_a, half_b = half, half + half // 2
    qa0, qa1 = pack0.at[half_a:half_b], pack1.at[half_a:half_b]
    qb0, qb1 = pack0.at[half_b : 2 * half], pack1.at[half_b : 2 * half]
    ye = gx_ref
    size = gd0.shape[0]
    cols = 2 * size
    for source, (own_ref, oth_ref, bit) in enumerate(((qa0, qa1, y_bit), (ga0, ga1, y_bit), (gb0, gb1, x_bit), (gd0, gd1, 0))):
        mine = pl.ds(pl.multiple_of(bit * size, size), size)
        put_rows(lhs.at[source // 2, source % 2 * cols : (source % 2 + 1) * cols], None, own_ref.at[mine], oth_ref.at[mine])

    def canvas(n, carry):
        lift_of(n)
        source = n // canv
        at = pl.ds(pl.multiple_of(lax.rem(source, 2) * cols, cols), cols)
        found = dot(lhs[source // 2, at, pl.ds(pl.multiple_of((n % canv) * PX, PX), PX)], lift[...]).astype(BF16)
        for d in range(9):
            grads[d, :, pl.ds(pl.multiple_of(n * CELLS, CELLS), CELLS)] = found[:, d * CELLS : (d + 1) * CELLS]
        return carry

    lax.fori_loop(0, PLANE * canv, canvas, 0)
    each = fb_send.shape[2]
    expand(y0[...], cells_ref, ye, 0)
    for number, copy in enumerate(y_near):
        copy.wait_recv()
        expand(y_all[number], cells_ref, ye, (number + 1) * rows)
    for d in range(9):
        result = dot(grads[d], ye[...])
        for part in range(parts):
            fb_send[reversed_bits(part, stages), d] = result[part * each : (part + 1) * each].astype(BF16)
    fb_way = Halving(0, fb_send, fb_recv, (0, 9))
    fb_way.send()

    sums = exchange.finish()
    sums_ref[...] = sums
    dw_sums.arrive()
    zflip = acc.at[4, :, 0:rows]
    for n in range(canv):
        at = slice(n * CELLS, (n + 1) * CELLS)
        dz = 0.0
        for level in range(4):
            _, rstd = branch_stat(ztotal_ref, level, rows_all[level])
            here = jnp.where(cells_ref[:, 4:5] == level, 1.0, 0.0)
            mean_gain = sums[level : level + 1, :] / rows_all[level]
            mean_bias = sums[4 + level : 5 + level, :] / rows_all[level]
            mine = zgain_ref[level : level + 1, :] * rstd * (da[at] - mean_bias - norm_ref[at] * mean_gain)
            dz = dz + here * mine
        dz0[at] = dz.astype(BF16)
        zflip[:, at] = pltranspose(dz)
    quarter = half // 2
    split_rows(zflip, half // (4 * each), each, zpack0.at[0:quarter], zsa, zpack0.at[quarter:half], zsb)
    swaps += [swap_copy(5, zpack0, zpack1), swap_copy(6, dz0, dz1)]
    dw_swap = swap_copy(9, dw_own, dw_other)
    dw_swap.start()
    near += [near_copy(3, zsa, zga0, x_mate), near_copy(4, zsb, zgb0, y_mate)]
    for copy in swaps[5:] + near[3:]:
        copy.start()

    mate_copies = []
    sides = (
        (0, ((0, qa0, qa1, 0), (1, ga0, ga1, 1)), y_bit, keep_a, send_a, recv_a, y_mate),
        (1, ((0, qb0, qb1, 0), (2, gb0, gb1, 1)), x_bit, keep_b, send_b, recv_b, x_mate),
    )
    for side, sources, bit, keep, send, recv, mate in sides:
        for number, (device, own_ref, oth_ref, slot) in enumerate(sources):
            loads[2 * side + slot].wait()
            for n in range(canv):
                rows_down(boxes_ref, device * canv + n, box_count, xbuf.at[slot, pl.ds(n * PX, PX)], xd, n, 2 * canv)
                xd[canv + n] = xbuf[slot, n * PX : (n + 1) * PX]
                cols_across(boxes_ref, device * canv + n, n, box_count, own_ref, oth_ref, lhs)
                if number:
                    select, count = members(
                        boxes_ref, device * canv + n, box_count, lambda row: cells_ref[:, row : row + 1], (CELLS, PX), 1
                    )
                    sums = dot(select.astype(BF16), xbuf[slot, n * PX : (n + 1) * PX])
                    pool_mate[side, n * CELLS : (n + 1) * CELLS] = (sums / count).astype(BF16)
            if side == 0:
                loads[2 + slot].start()
            for d in range(9):
                across = xd[d // 3 * canv : (d // 3 + 1) * canv].reshape(pixels, span)
                found = dot(lhs[d % 3], across)
                acc[d] = found if number == 0 else acc[d] + found
                if number and d % 3 == 2:
                    split_out((d - 2, d + 1), bit, acc, keep, send)
                    some = pl.ds(d - 2, 3)
                    mate_copies.append(mate_copy(len(mate_copies), send.at[:, some], recv.at[:, some], mate))
                    mate_copies[-1].start()
        if side == 0:
            for number, (source, target) in enumerate(((zga0, zga1), (zgb0, zgb1))):
                near[3 + number].wait_recv()
                swaps.append(swap_copy(7 + number, source, target))
                swaps[-1].start()

    for side in range(2):
        source = pooled_any.at[:, pl.ds(side * span, span)]
        loads.append(pltpu.make_async_copy(source, xd.at[side, pl.ds(0, rows)], load_sem.at[4 + side]))
        loads[-1].start()
    for number in (5, 7, 8):
        swaps[number].wait_recv()
    za0, za1 = zpack0.at[0:quarter], zpack1.at[0:quarter]
    zb0, zb1 = zpack0.at[quarter:half], zpack1.at[quarter:half]
    sides = (
        (0, za0, za1, zga0, zga1, y_bit, bkeep_a, bsend_a, brecv_a, y_mate),
        (1, zb0, zb1, zgb0, zgb1, x_bit, bkeep_b, bsend_b, brecv_b, x_mate),
    )
    for side, own0, oth0, own1, oth1, bit, keep, send, recv, mate in sides:
        put_rows(lhs, 0, own0, oth0)
        put_rows(lhs, 1, own1, oth1)
        loads[4 + side].wait()
        for level in range(4):
            left = [jnp.where(levels == level, lhs[k, :, :rows].astype(F32), 0.0).astype(BF16) for k in range(2)]
            acc[level] = dot(left[0], xd[side, :rows]) + dot(left[1], pool_mate[side])
        split_out((0, 4), bit, acc, keep, send)
        mate_copies.append(mate_copy(len(mate_copies), send, recv, mate))
        mate_copies[-1].start()

    ways = {}

    def pass_on(number):
        mate_copies[number].wait_recv()
        if number < 6:
            keep, recv, target = (keep_a, recv_a, zrecv_a) if number < 3 else (keep_b, recv_b, zrecv_b)
            offsets = (number % 3 * 3, number % 3 * 3 + 3)
        else:
            keep, recv, target = (bkeep_a, brecv_a, bzrecv_a) if number == 6 else (bkeep_b, brecv_b, bzrecv_b)
            offsets = (0, 4)

        def add(d, carry):
            for part in range(parts):
                keep[part, d] = (keep[part, d].astype(F32) + recv[part, d].astype(F32)).astype(BF16)
            return carry

        lax.fori_loop(*offsets, add, 0)
        ways[number] = Halving(1 + number, keep, target, offsets)
        ways[number].send()

    pass_on(0)
    fb_way.receive()

    swaps[1].wait_recv()
    swaps[6].wait_recv()
    for n in range(canv):
        gate = pixel_gates(boxes_ref, n, box_count, (PX, CELLS), 0)
        at = slice(n * PX, (n + 1) * PX)
        for which, ref in ((chan, df0), (1 - chan, df1)):
            into = pl.ds(pl.multiple_of(which * half, half), half)
            df = ref[at].astype(F32)
            xd[canv + n, :, into] = ref[at]
            xd[n, :, into] = (wide(gate(0, 1), half // CELLS) * pltpu.roll(df, PX - 1, 0)).astype(BF16)
            xd[2 * canv + n, :, into] = (wide(gate(0, -1), half // CELLS) * pltpu.roll(df, 1, 0)).astype(BF16)

    width = wbuf.shape[1]
    tiles = wfx_any.shape[1] // width

    def tile(t, carry):
        tile_load(t).wait()

        @pl.when(t + 1 < tiles)
        def _():
            tile_load(t + 1).start()

        first = lax.rem(t, 2) * 9
        for n in range(canv):
            at = slice(n * PX, (n + 1) * PX)
            gate = pixel_gates(boxes_ref, n, box_count, (PX, CELLS), 0)
            total = None
            for dy in range(3):
                found = dot_nt(xd[n], wbuf[first + dy * 3])
                for dx in range(1, 3):
                    found = found + dot_nt(xd[dx * canv + n], wbuf[first + dy * 3 + dx])
                if dy != 1:
                    found = wide(gate(1 - dy, 0), width // CELLS) * pltpu.roll(found, ((dy - 1) * CW) % PX, 0)
                total = found if total is None else total + found
            gx_ref[at, pl.ds(pl.multiple_of(t * width, width), width)] = total.astype(BF16)
        return carry

    lax.fori_loop(0, 1, tile, 0)
    pass_on(1)
    lax.fori_loop(1, 2, tile, 0)
    pass_on(3)
    lax.fori_loop(2, 3, tile, 0)
    pass_on(2)
    pass_on(4)
    lax.fori_loop(3, tiles, tile, 0)

    wbr_load = pltpu.make_async_copy(wbr_any, wbuf.at[pl.ds(0, wbr_any.shape[0])], load_sem.at[6])
    wbr_load.start()
    wbr_load.wait()
    per_level = wbr_any.shape[0] // 4
    for level in range(4):
        for which, ref in ((chan, dz0), (1 - chan, dz1)):
            into = pl.ds(pl.multiple_of(which * half, half), half)
            for m in range(canv):
                at = slice(m * CELLS, (m + 1) * CELLS)
                mine = jnp.where(cells_ref[:, 4:5] == level, ref[at].astype(F32), 0.0)
                xd[level, at, into] = mine.astype(BF16)
    for side in range(2):
        total = 0.0
        for level in range(4):
            first = level * per_level + side * per_level // 2
            w = wbuf[first : first + per_level // 2].reshape(span, 2 * half)
            total = total + dot_nt(xd[level, :rows], w)
        for m in range(canv):
            _, _, high, across = by_box(boxes_ref, m, cells_ref[:, 0:1], box_count)
            r0, r1, c0, c1 = member_bounds(lambda row: cells_ref[:, row : row + 1], high, across)
            at = slice(m * CELLS, (m + 1) * CELLS)
            pool_mate[side, at] = (total[at] / ((r1 - r0) * (c1 - c0))).astype(BF16)
    for n in range(canv):
        at = slice(n * PX, (n + 1) * PX)
        select, _ = members(boxes_ref, n, box_count, lambda row: lanes_ref[row : row + 1, :], (PX, CELLS), 0)
        for side in range(2):
            into = slice(side * span, (side + 1) * span)
            pooled = dot(select.astype(BF16), pool_mate[side, n * CELLS : (n + 1) * CELLS])
            gx_ref[at, into] = (gx_ref[at, into].astype(F32) + pooled).astype(BF16)

    pass_on(5)
    ways[0].receive()
    ways[1].receive()
    ways[3].receive()
    pass_on(6)
    pass_on(7)
    for number in (2, 4, 5, 6, 7):
        ways[number].receive()
    in_order = [fb_way] + [ways[number] for number in (0, 1, 3, 2, 4, 5, 6, 7)]
    for stage in range(2, stages):
        for way in in_order:
            way.receive()

    stores = []

    def finish(way, out, at, sides):
        way.receive()
        keep, recv = way.keep, way.recv
        width_of = keep.shape[3] // len(sides)

        def add(d, carry):
            total = keep[way.kept(stages), d].astype(F32) + recv[parts - 2, d].astype(F32)
            for spot in range(len(sides)):
                row = (at + spot) * each
                acc[d, row : row + each, :width_of] = total[:, spot * width_of : (spot + 1) * width_of]
            return carry

        lax.fori_loop(*way.offsets, add, 0)
        some = pl.ds(way.offsets[0], way.offsets[1] - way.offsets[0])
        for spot, side in enumerate(sides):
            source = acc.at[some, pl.ds((at + spot) * each, each), pl.ds(0, width_of)]
            target = out.at[some, side] if len(out.shape) == 4 else out.at[some, :, pl.ds(side * width_of, width_of)]
            stores.append(pltpu.make_async_copy(source, target, store_sem.at[len(stores)]))
            stores[-1].start()

    finish(fb_way, out_fb, 0, (0, 1, 2, 3))
    for number in (0, 1, 3, 2, 4, 5):
        finish(ways[number], out_fx, 4 + number // 3, (number // 3,))
    finish(ways[6], out_br, 6, (0,))
    finish(ways[7], out_br, 7, (1,))
    for copy in stores:
        copy.wait()
    dw_swap.wait()
    for copy in mate_copies + swaps + near + y_near + [copy for way in in_order for copy in way.copies]:
        copy.wait_send()


def launch(kernel, **rest):
    return pl.pallas_call(kernel, **rest)


def whole(shape):
    return pl.BlockSpec(shape, lambda i: (0,) * len(shape))


def shaped(shape, kind):
    return jax.ShapeDtypeStruct(shape, kind)


def per_device(features, boxes, w_branch, gain_branch, bias_branch, w_fx, w_fb, gain_join, bias_join, w_cls, b_cls, grad_logits):
    canv, box_count = boxes.shape[:2]
    pixels, cin = features.shape
    mid = gain_join.shape[0]
    half = mid // lax.axis_size("chan")
    bw = gain_branch.shape[1]
    br = w_branch.shape[2]
    ncls = w_cls.shape[1]
    dp = lax.axis_size("dp")
    parts = dp // PLANE
    each = mid // dp
    cols = parts * each
    rows = canv * CELLS
    chan = lax.axis_index("chan")
    me = lax.axis_index("dp")
    rows_all = [float(canv * dp * box_count * s * s) for s in BINS]
    lanes_np = cell_table(box_count)
    lanes = jnp.asarray(lanes_np)
    cells = jnp.asarray(np.concatenate([lanes_np.T, np.zeros((CELLS, CELLS - 8), np.float32)], 1))

    span = cin // 2
    tile = cin // 4
    stages = parts.bit_length() - 1
    quarter = half // 2
    bundle = quarter // 2

    def swap(array):
        return lax.ppermute(array, "chan", [(0, 1), (1, 0)])

    def sems(*counts):
        return [pltpu.SemaphoreType.DMA((count,)) for count in counts]

    flat = boxes.reshape(-1)
    box_tile = jnp.zeros((8 * CELLS,), jnp.int32).at[: flat.shape[0]].set(flat).reshape(8, CELLS)
    (
        pooled, y, z_norm, z_act, z_total, boxes_all, logits, df, pack, send_a, send_b, send_d, dw_cls, db_total, x_mate, y_mate,
    ) = launch(
        functools.partial(front_kernel, canv, box_count, dp, each, rows_all),
        in_specs=[SMEM_SPEC] + [VMEM_SPEC] * 10 + [ANY_SPEC] * 4,
        out_specs=[VMEM_SPEC] * 14 + [ANY_SPEC] * 2,
        out_shape=[
            shaped((rows, cin), BF16),
            shaped((rows, bw), BF16),
            shaped((rows, bw), F32),
            shaped((rows, bw), F32),
            shaped((8, bw), F32),
            shaped((PLANE, 8, CELLS), jnp.int32),
            shaped((ncls, pixels), BF16),
            shaped((pixels, half), BF16),
            shaped((2 * half, pixels), BF16),
            shaped((quarter, pixels), BF16),
            shaped((quarter, pixels), BF16),
            shaped((bundle, pixels), BF16),
            shaped((dp, half // dp, ncls), F32),
            shaped((8, half), F32),
            shaped((pixels, span), BF16),
            shaped((pixels, span), BF16),
        ],
        scratch_shapes=[
            pltpu.VMEM((canv, PX, cin), BF16),
            pltpu.VMEM((2 * canv, PX, cin), BF16),
            pltpu.VMEM((4, cin, br), BF16),
            pltpu.VMEM((3, 3, cin, mid), BF16),
            pltpu.VMEM((canv, PX, 9 * CELLS), BF16),
            pltpu.VMEM((canv, 9 * CELLS, mid), BF16),
            pltpu.VMEM((canv, PX, mid), F32),
            pltpu.VMEM((rows, 4 * bw), BF16),
            pltpu.VMEM((rows, br), F32),
            pltpu.VMEM((rows, bw), BF16),
            pltpu.VMEM((rows, bw), BF16),
            pltpu.VMEM((half, ncls), F32),
            pltpu.VMEM((pixels, half), BF16),
            pltpu.VMEM((pixels, half), BF16),
            pltpu.VMEM((pixels, half), F32),
            pltpu.VMEM((pixels, half), F32),
            pltpu.VMEM((ncls, pixels), BF16),
            pltpu.VMEM((ncls, pixels), BF16),
            pltpu.VMEM((half, PX), F32),
        ]
        + exchange_scratch(dp, half, 3)
        + sems(3, 3, 7, 7, canv + 7),
        compiler_params=pltpu.CompilerParams(vmem_limit_bytes=63 * 2**20, collective_id=1, has_side_effects=True),
        name="front",
    )(
        flat, box_tile, lanes, cells, gain_branch, bias_branch, gain_join.reshape(1, mid), bias_join.reshape(1, mid),
        w_cls.T, b_cls.reshape(ncls, 1), grad_logits.T, features, w_branch, w_fx.reshape(3, 3, cin, mid),
        w_fb.reshape(3, 3, 4 * bw, mid),
    )
    flat_all = boxes_all.reshape(PLANE, -1)[:, : flat.shape[0]].reshape(-1)

    def buffers(count, width):
        return [
            pltpu.VMEM((parts, count, each, width), BF16),
            pltpu.VMEM((parts, count, each, width), BF16),
            pltpu.VMEM((parts, count, each, width), BF16),
            pltpu.VMEM((parts - 1, count, each, width), BF16),
        ]

    near_rows = [pltpu.VMEM((quarter, pixels), BF16)] * 4 + [pltpu.VMEM((bundle, pixels), BF16)] * 2
    near_rows.append(pltpu.VMEM((PLANE - 1, rows, bw), BF16))
    near_cells = [pltpu.VMEM((quarter, rows), BF16)] * 6
    grad_features, sum_fx, sum_fb, sum_br, da_total, dw_own, dw_other = launch(
        functools.partial(tail_kernel, canv, box_count, dp, rows_all),
        in_specs=[SMEM_SPEC] + [VMEM_SPEC] * 3 + [ANY_SPEC] * 3 + [VMEM_SPEC] * 6 + [ANY_SPEC] * 8,
        out_specs=[VMEM_SPEC] + [ANY_SPEC] * 3 + [VMEM_SPEC] * 2 + [ANY_SPEC],
        out_shape=[
            shaped((pixels, cin), BF16),
            shaped((9, each, cin), F32),
            shaped((9, 4, each, bw), F32),
            shaped((4, each, cin), F32),
            shaped((8, bw), F32),
            shaped((dp, half // dp, ncls), F32),
            shaped((dp, half // dp, ncls), F32),
        ],
        scratch_shapes=[
            pltpu.VMEM((dp, half // dp, ncls), F32),
            pltpu.VMEM((half // dp, ncls), F32),
            pltpu.SemaphoreType.DMA((2, dp)),
            pltpu.SemaphoreType.DMA((2, dp)),
            pltpu.VMEM((2 * half, pixels), BF16),
            pltpu.VMEM((pixels, half), BF16),
        ]
        + near_rows
        + [pltpu.VMEM((bw, rows), BF16), pltpu.VMEM((bw, rows), BF16)]
        + near_cells
        + [pltpu.VMEM((rows, bw), BF16), pltpu.VMEM((rows, bw), BF16), pltpu.VMEM((rows, bw), F32)]
        + exchange_scratch(dp, bw, 1)
        + sems(10, 10, 8, 8)
        + [
            pltpu.VMEM((PX, 9 * CELLS), BF16),
            pltpu.VMEM((9, cols, PLANE * rows), BF16),
            pltpu.VMEM((2, pixels, span), BF16),
            pltpu.VMEM((18, tile, mid), BF16),
            pltpu.VMEM((3 * canv, PX, mid), BF16),
            pltpu.VMEM((3, half, pixels), BF16),
            pltpu.VMEM((9, half, span), F32),
            pltpu.VMEM((2, rows, span), BF16),
            pltpu.VMEM((parts, 9, each, 4 * bw), BF16),
            pltpu.VMEM((parts - 1, 9, each, 4 * bw), BF16),
        ]
        + buffers(9, span)
        + buffers(9, span)
        + buffers(4, span)
        + buffers(4, span)
        + sems(7, 12, 2, 4, 8, 8, 9 * stages, 9 * stages),
        compiler_params=pltpu.CompilerParams(vmem_limit_bytes=63 * 2**20, collective_id=4, has_side_effects=True),
        name="tail",
    )(
        flat_all, lanes, cells, pack, send_a, send_b, send_d, df, y, z_norm, z_act, z_total, gain_branch, dw_cls, pooled,
        features, x_mate, y_mate, w_fx, w_fb, w_branch.reshape(16, tile, br),
    )
    out_fx = jnp.transpose(sum_fx, (0, 2, 1))
    out_fb = jnp.transpose(sum_fb, (0, 1, 3, 2))
    out_br = jnp.transpose(sum_br, (0, 2, 1))

    small = db_total[:2]
    small_got = swap(small)
    small_all = jnp.concatenate([jnp.where(chan == 0, small, small_got), jnp.where(chan == 0, small_got, small)], 1)
    dw_halves = [jnp.where(chan == 0, dw_own, dw_other), jnp.where(chan == 0, dw_other, dw_own)]
    grad_w_cls = jnp.concatenate([a.reshape(half, ncls) for a in dw_halves], 0)
    return (
        logits.T,
        grad_features,
        out_br,
        da_total[:4],
        da_total[4:],
        out_fx,
        out_fb,
        small_all[0],
        small_all[1],
        grad_w_cls,
        db_total[2, :ncls],
    )


def solution(mesh):
    return jax.shard_map(
        per_device,
        mesh=mesh,
        in_specs=(
            P("dp", "chan"),
            P("dp", None, None),
            P(None, "chan", None),
            P(None, "chan"),
            P(None, "chan"),
            P(None, "chan", None),
            P(None, None, "chan", None),
            P(),
            P(),
            P(),
            P(),
            P("dp", None),
        ),
        out_specs=(
            P("dp", None),
            P("dp", "chan"),
            P(None, "chan", "dp"),
            P(None, "chan"),
            P(None, "chan"),
            P(None, "chan", "dp"),
            P(None, None, "chan", "dp"),
            P(),
            P(),
            P(),
            P(),
        ),
        check_vma=False,
    )
```

```python
import functools

import jax
import jax.numpy as jnp
import numpy as np
from jax import lax
from jax.experimental import pallas as pl
from jax.experimental.pallas import tpu as pltpu
from jax.sharding import PartitionSpec as P

CH = 16
CW = 32
PX = CH * CW
EPS = 1e-05
BINS = (1, 2, 3, 6)
CELLS = 128
PLANE = 4
F32 = jnp.float32
BF16 = jnp.bfloat16
MESH = pl.DeviceIdType.MESH
VMEM_SPEC = pl.BlockSpec(memory_space=pltpu.VMEM)
SMEM_SPEC = pl.BlockSpec(memory_space=pltpu.SMEM)
ANY_SPEC = pl.BlockSpec(memory_space=pl.ANY)
NT = (((1,), (1,)), ((), ()))
TN = (((0,), (0,)), ((), ()))


def dot(a, b):
    return jnp.dot(a, b, preferred_element_type=F32)


def dot_nt(a, b):
    return lax.dot_general(a, b, NT, preferred_element_type=F32)


def dot_tt(a, b):
    return lax.dot_general(a, b, (((0,), (1,)), ((), ())), preferred_element_type=F32)


def dot_tn(a, b):
    return lax.dot_general(a, b, TN, preferred_element_type=F32)


def cell_table(box_count):
    table = np.zeros((8, CELLS), np.float32)
    table[1] = 1.0
    table[4] = 9.0
    at = 0
    for level, bins in enumerate(BINS):
        for box in range(box_count):
            for i in range(bins):
                for j in range(bins):
                    table[:6, at] = (box, bins, i, j, level, 1.0)
                    at += 1
    return table


def box_at(boxes_ref, canvas, box, box_count):
    base = (canvas * box_count + box) * 4
    return [boxes_ref[base + part] for part in range(4)]


def by_box(boxes_ref, canvas, which, box_count):
    sides = None
    for box in range(box_count):
        mine = [side.astype(F32) for side in box_at(boxes_ref, canvas, box, box_count)]
        if sides is None:
            sides = [jnp.full(which.shape, side, F32) for side in mine]
        else:
            sides = [jnp.where(which == box, new, old) for new, old in zip(mine, sides)]
    return sides


def within(relative, extent):
    return (relative >= 0) & (relative < extent)


def pixel_gates(boxes_ref, canvas, box_count, shape, axis):
    place = lax.broadcasted_iota(jnp.int32, shape, axis)
    row = place >> 5
    col = place & (CW - 1)
    rel = []
    for box in range(box_count):
        top, left, height, width = box_at(boxes_ref, canvas, box, box_count)
        rel.append((row - top, col - left, height, width))

    def gate(dy, dx):
        total = None
        for y, x, height, width in rel:
            hit = within(y, height) & within(x, width)
            if not isinstance(dy, int) or dy:
                hit = hit & within(y + dy, height)
            if not isinstance(dx, int) or dx:
                hit = hit & within(x + dx, width)
            value = jnp.where(hit, 1.0, 0.0)
            total = value if total is None else total + value
        return total

    return gate


def wide(column_block, times):
    return jnp.concatenate([column_block] * times, axis=1)


def rows_down(boxes_ref, canvas, box_count, x, xs, n, below):
    gate = pixel_gates(boxes_ref, canvas, box_count, (PX, CELLS), 0)
    reps = xs.shape[2] // CELLS
    blank = jnp.zeros((CW, xs.shape[2]), BF16)
    xs[n, 0:CW] = blank
    xs[n, CW:PX] = x[0 : PX - CW] * wide(gate(-1, 0).astype(BF16), reps)[CW:]
    xs[below + n, 0 : PX - CW] = x[CW:PX] * wide(gate(1, 0).astype(BF16), reps)[: PX - CW]
    xs[below + n, PX - CW : PX] = blank


def member_bounds(table_at, height, width):
    bins, i, j = table_at(1), table_at(2), table_at(3)

    def start(at, extent):
        return jnp.floor((at * extent + 0.5) / bins)

    def stop(at, extent):
        return jnp.floor(((at + 1) * extent + bins - 0.5) / bins)

    return start(i, height), stop(i, height), start(j, width), stop(j, width)


def members(boxes_ref, canvas, box_count, table_at, shape, axis):
    top, left, height, width = by_box(boxes_ref, canvas, table_at(0), box_count)
    r0, r1, c0, c1 = member_bounds(table_at, height, width)
    place = lax.broadcasted_iota(jnp.int32, shape, axis)
    row = (place >> 5).astype(F32) - top
    col = (place & (CW - 1)).astype(F32) - left
    hit = (row >= r0) & (row < r1) & (col >= c0) & (col < c1) & (table_at(5) > 0)
    return jnp.where(hit, 1.0, 0.0), (r1 - r0) * (c1 - c0)


def gated_lifts(boxes_ref, canvas, box_count, lanes_ref, store):
    def table_at(row):
        return lanes_ref[row : row + 1, :]

    top, left, height, width = by_box(boxes_ref, canvas, table_at(0), box_count)

    def side(size, edge, extent, cell):
        relative = lax.broadcasted_iota(jnp.int32, (size, CELLS), 0).astype(F32) - edge
        scale = (table_at(1) - 1.0) / (extent - 1.0)
        own = within(relative, extent)
        found = []
        for step in (-1, 0, 1):
            moved = relative + step
            weight = jnp.maximum(0.0, 1.0 - jnp.abs(moved * scale - cell))
            found.append(jnp.where(own & within(moved, extent), weight, 0.0))
        return found

    rows = [found * table_at(5) for found in side(CH, top, height, table_at(2))]
    cols = side(CW, left, width, table_at(3))
    for d in range(9):
        for y in range(CH):
            store(d, y, (rows[d // 3][y : y + 1] * cols[d % 3]).astype(BF16))


def pltranspose(block):
    return jnp.transpose(block, (1, 0))


def signal_all(total, chan_too=False):
    me = lax.axis_index("dp")
    chan = lax.axis_index("chan")
    barrier = pltpu.get_barrier_semaphore()

    def signal(step, carry):
        pl.semaphore_signal(barrier, inc=1, device_id=(lax.rem(me + step, total), chan), device_id_type=MESH)
        return carry

    lax.fori_loop(1, total, signal, 0)
    if chan_too:
        pl.semaphore_signal(barrier, inc=1, device_id=(me, 1 - chan), device_id_type=MESH)
    return total if chan_too else total - 1


class Exchange:
    def __init__(self, total, own, slots, send_sem, recv_sem, parted=False):
        self.total, self.own, self.slots, self.send_sem, self.recv_sem = total, own, slots, send_sem, recv_sem
        self.me = lax.axis_index("dp")
        self.parted = parted

    def block(self, device):
        return self.own.at[device] if self.parted else self.own

    def copy_to(self, step):
        return pltpu.make_async_remote_copy(
            src_ref=self.block(lax.rem(self.me + step, self.total)),
            dst_ref=self.slots.at[self.me],
            send_sem=self.send_sem.at[step],
            recv_sem=self.recv_sem.at[self.me],
            device_id=(lax.rem(self.me + step, self.total), lax.axis_index("chan")),
            device_id_type=MESH,
        )

    def copy_from(self, step):
        other = lax.rem(self.me + self.total - step, self.total)
        return pltpu.make_async_remote_copy(
            src_ref=self.block(other),
            dst_ref=self.slots.at[other],
            send_sem=self.send_sem.at[step],
            recv_sem=self.recv_sem.at[other],
            device_id=(other, lax.axis_index("chan")),
            device_id_type=MESH,
        )

    def start(self):
        if self.parted:
            keep = pltpu.make_async_copy(self.block(self.me), self.slots.at[self.me], self.recv_sem.at[self.me])
            keep.start()
            keep.wait()
        else:
            self.slots[self.me] = self.own[...]

        def one(step, carry):
            self.copy_to(step).start()
            return carry

        lax.fori_loop(1, self.total, one, 0)

    def arrive(self):
        def one(step, carry):
            self.copy_from(step).wait_recv()
            return carry

        def sent(step, carry):
            self.copy_to(step).wait_send()
            return carry

        lax.fori_loop(1, self.total, one, 0)
        lax.fori_loop(1, self.total, sent, 0)

    def finish(self):
        self.arrive()
        value = self.slots[0]
        for other in range(1, self.total):
            value = value + self.slots[other]
        return value


def exchange_scratch(total, width, times):
    return [
        pltpu.VMEM((times, 8, width), F32),
        pltpu.VMEM((times, total, 8, width), F32),
        pltpu.SemaphoreType.DMA((times, total)),
        pltpu.SemaphoreType.DMA((times, total)),
    ]


def core_copy(source, target, send_sem, recv_sem):
    return pltpu.make_async_remote_copy(
        src_ref=source,
        dst_ref=target,
        send_sem=send_sem,
        recv_sem=recv_sem,
        device_id=(lax.axis_index("dp"), 1 - lax.axis_index("chan")),
        device_id_type=MESH,
    )


def branch_stat(total_ref, level, rows_all):
    mean = total_ref[level : level + 1, :] / rows_all
    var = total_ref[4 + level : 5 + level, :] / rows_all - mean * mean
    return mean, lax.rsqrt(var + EPS)


def expand(y, cells_ref, keep, at):
    width = y.shape[1]
    for n in range(y.shape[0] // CELLS):
        rows = slice(n * CELLS, (n + 1) * CELLS)
        block = y[rows].astype(F32)
        for level in range(4):
            mine = jnp.where(cells_ref[:, 4:5] == level, block, 0.0)
            keep[at + n * CELLS : at + (n + 1) * CELLS, level * width : (level + 1) * width] = mine.astype(BF16)


def front_kernel(
    canv, box_count, total, each, rows_all,
    boxes_ref, box_ref, lanes_ref, cells_ref, zgain_ref, zbias_ref, gain_ref, bias_ref, w_ref, bcls_ref, g_ref,
    x_any, wbr_any, wfx_any, wfb_any,
    pooled_ref, y_ref, norm_ref, act_ref, ztotal_ref, boxes_all, logits_ref, df_ref, pack_ref, send_a, send_b, send_d,
    dw_ref, sums_ref, xm_any, ym_any,
    x, xs, wbr, wbuf, lifts, terms, fjoin, ye, zs, zsend, zgot, dw, fsend, got, f, db, score, score_got, flip,
    part, slots, send_sem, recv_sem, core_send, core_recv, near_send, near_recv, load_sem,
):
    me = lax.axis_index("dp")
    chan = lax.axis_index("chan")
    x_mate = me + 1 - 2 * (me % 2)
    y_mate = me + 2 - 4 * ((me // 2) % 2)
    span = xm_any.shape[1]
    half = df_ref.shape[1]
    mid = 2 * half
    ncls = g_ref.shape[0]
    own = pl.ds(pl.multiple_of(chan * half, half), half)
    away = pl.ds(pl.multiple_of((1 - chan) * half, half), half)
    expected = signal_all(total, True)
    loads = [pltpu.make_async_copy(x_any.at[pl.ds(n * PX, PX)], x.at[n], load_sem.at[n]) for n in range(canv)]
    loads.append(pltpu.make_async_copy(wbr_any, wbr, load_sem.at[canv]))
    loads += [pltpu.make_async_copy(wfx_any.at[:, t], wbuf.at[t], load_sem.at[canv + 1 + t]) for t in range(3)]
    for copy in loads:
        copy.start()

    def near_copy(number, source, target, mate):
        return pltpu.make_async_remote_copy(
            src_ref=source, dst_ref=target, send_sem=near_send.at[number], recv_sem=near_recv.at[number],
            device_id=(mate, chan), device_id_type=MESH,
        )

    def share(number, first, last):
        at = pl.ds(first * PX, (last - first) * PX)
        copies = [
            near_copy(number, x_any.at[at, pl.ds(0, span)], xm_any.at[at], x_mate),
            near_copy(number + 1, x_any.at[at, pl.ds(span, span)], ym_any.at[at], y_mate),
        ]
        for copy in copies:
            copy.start()
        return copies

    def table_at(row):
        return cells_ref[:, row : row + 1]

    part[...] = jnp.zeros_like(part)
    near = []
    for n in range(canv):
        loads[n].wait()
        select, count = members(boxes_ref, n, box_count, table_at, (CELLS, PX), 1)
        pooled_ref[n * CELLS : (n + 1) * CELLS] = (dot(select.astype(BF16), x[n]) / count).astype(BF16)
        if n == 0:
            pl.semaphore_wait(pltpu.get_barrier_semaphore(), expected)
            near += share(0, 0, 1)
            boxes_all[0] = box_ref[...]
            for number, mate in ((1, x_mate), (2, y_mate), (3, x_mate + y_mate - me)):
                near.append(near_copy(3 + number, box_ref, boxes_all.at[number], mate))
                near[-1].start()
    loads[canv].wait()
    for level in range(4):
        found = dot(pooled_ref[...], wbr[level])
        for n in range(canv):
            rows = slice(n * CELLS, (n + 1) * CELLS)
            mine = jnp.where(table_at(4) == level, found[rows], 0.0)
            zs[rows, :] = mine if level == 0 else zs[rows, :] + mine
    zsend[...] = zs[:, away].astype(BF16)
    swap_z = core_copy(zsend, zgot, core_send.at[0], core_recv.at[0])
    swap_z.start()
    for n in range(canv):
        rows_down(boxes_ref, n, box_count, x.at[n], xs, n, canv)

        def store(d, y, block, n=n):
            lifts[n, y * CW : (y + 1) * CW, d * CELLS : (d + 1) * CELLS] = block

        gated_lifts(boxes_ref, n, box_count, lanes_ref, store)
    swap_z.wait()
    bw = y_ref.shape[1]
    for n in range(canv):
        rows = slice(n * CELLS, (n + 1) * CELLS)
        z = zs[rows, own] + zgot[rows].astype(F32)
        norm_ref[rows] = z
        for level in range(4):
            mine = jnp.where(table_at(4) == level, z, 0.0)
            part[0, level : level + 1, :] += jnp.sum(mine, 0, keepdims=True)
            part[0, 4 + level : 5 + level, :] += jnp.sum(mine * mine, 0, keepdims=True)
    z_sums = Exchange(total, part.at[0], slots.at[0], send_sem.at[0], recv_sem.at[0])
    z_sums.start()

    def features_part(t):
        loads[canv + 1 + t].wait()
        for n in range(canv):
            q = dot(xs[n], wbuf[t, 0]) + dot(x[n], wbuf[t, 1]) + dot(xs[canv + n], wbuf[t, 2])
            gate = pixel_gates(boxes_ref, n, box_count, (PX, CELLS), 0)
            if t == 0:
                fjoin[n] = wide(gate(0, -1), mid // CELLS) * pltpu.roll(q, 1, 0)
            elif t == 1:
                fjoin[n] += wide(gate(0, 0), mid // CELLS) * q
            else:
                fjoin[n] += wide(gate(0, 1), mid // CELLS) * pltpu.roll(q, PX - 1, 0)
        loads.append(pltpu.make_async_copy(wfb_any.at[:, t], wbuf.at[t], load_sem.at[canv + 4 + t]))
        loads[-1].start()

    features_part(0)
    z_total = z_sums.finish()
    ztotal_ref[...] = z_total
    near += share(2, 1, canv)
    for n in range(canv):
        rows = slice(n * CELLS, (n + 1) * CELLS)
        z = norm_ref[rows]
        norm = act = 0.0
        for level in range(4):
            mean, rstd = branch_stat(ztotal_ref, level, rows_all[level])
            here = jnp.where(table_at(4) == level, 1.0, 0.0)
            mine = (z - mean) * rstd
            norm = norm + here * mine
            act = act + here * (zgain_ref[level : level + 1, :] * mine + zbias_ref[level : level + 1, :])
        norm_ref[rows] = norm
        act_ref[rows] = act
        value = act * jax.nn.sigmoid(act)
        y_ref[rows] = value.astype(BF16)
        for level in range(4):
            mine = jnp.where(table_at(4) == level, value, 0.0)
            ye[rows, level * bw : (level + 1) * bw] = mine.astype(BF16)
    features_part(1)
    features_part(2)

    for t in range(3):
        loads[canv + 4 + t].wait()
        for dy in range(3):
            term = dot(ye[...], wbuf[t, dy]).astype(BF16)
            at = (dy * 3 + t) * CELLS
            for n in range(canv):
                terms[n, at : at + CELLS] = term[n * CELLS : (n + 1) * CELLS]
    for n in range(canv):
        fjoin[n] += dot(lifts[n], terms[n])
        fsend[n * PX : (n + 1) * PX] = fjoin[n, :, away].astype(BF16)
    swap_f = core_copy(fsend, got, core_send.at[1], core_recv.at[1])
    swap_f.start()
    dw[...] = jnp.zeros_like(dw)
    area = 0
    for n in range(canv):
        for box in range(box_count):
            side = box_at(boxes_ref, n, box, box_count)
            area = area + side[2] * side[3]
    part[1, 2:3, :] = jnp.full((1, half), area.astype(F32), F32)
    swap_f.wait()
    for n in range(canv):
        rows = slice(n * PX, (n + 1) * PX)
        value = fjoin[n, :, own] + got[rows].astype(F32)
        f[rows] = value
        part[1, 0:1, :] += jnp.sum(value, 0, keepdims=True)
        part[1, 1:2, :] += jnp.sum(value * value, 0, keepdims=True)
    first = Exchange(total, part.at[1], slots.at[1], send_sem.at[1], recv_sem.at[1])
    first.start()
    f_total = first.finish()
    count = f_total[2:3, :]
    mean = f_total[0:1, :] / count
    rstd = lax.rsqrt(f_total[1:2, :] / count - mean * mean + EPS)
    gain, bias, w = gain_ref[:, own], bias_ref[:, own], w_ref[:, own]
    ones = jnp.ones((8, PX), BF16)
    valid = [wide(pixel_gates(boxes_ref, n, box_count, (PX, CELLS), 0)(0, 0), half // CELLS) for n in range(canv)]
    for n in range(canv):
        rows = slice(n * PX, (n + 1) * PX)
        norm = (f[rows] - mean) * rstd
        f[rows] = norm
        act = gain * norm + bias
        sig = jax.nn.sigmoid(act)
        hidden = (act * sig * valid[n]).astype(BF16)
        g = g_ref[:, rows]
        score[:, rows] = dot_nt(w, hidden).astype(BF16)
        value = dot_tn(g, w) * valid[n] * sig * (1.0 + act * (1.0 - sig))
        db[rows] = value
        part[2, 0:1, :] += jnp.sum(value * norm, 0, keepdims=True)
        part[2, 1:2, :] += jnp.sum(value, 0, keepdims=True)
        part[2, 2:3, :ncls] += dot_nt(ones, g)[0:1]
        dw[...] += dot_tt(hidden, g)
    second = Exchange(total, part.at[2], slots.at[2], send_sem.at[2], recv_sem.at[2])
    second.start()
    swap_score = core_copy(score, score_got, core_send.at[2], core_recv.at[2])
    swap_score.start()
    sums = second.finish()
    sums_ref[...] = sums
    scale = gain * rstd
    for n in range(canv):
        rows = slice(n * PX, (n + 1) * PX)
        df = scale * (db[rows] - sums[1:2, :] / count - f[rows] * (sums[0:1, :] / count)) * valid[n]
        df_ref[rows] = df.astype(BF16)
        flip[...] = pltranspose(df)
        span = pl.ds(n * PX, PX)
        pack_ref[0:half, span] = flip[...].astype(BF16)
        views = [pack_ref.at[half : half + half // 2, span], send_a.at[:, span]]
        views += [pack_ref.at[half + half // 2 : 2 * half, span], send_b.at[:, span], send_d.at[:, span]]
        split_rows(flip, half // (4 * each), each, *views)
    strip = dw_ref.shape[1]
    for device in range(total):
        dw_ref[device] = dw[device * strip : (device + 1) * strip]
    swap_score.wait()
    square = (ncls, ncls)
    same = lax.broadcasted_iota(jnp.int32, square, 0) == lax.broadcasted_iota(jnp.int32, square, 1)
    bias_cls = jnp.sum(jnp.where(same, bcls_ref[...], 0.0), 1, keepdims=True)
    for n in range(canv):
        rows = slice(n * PX, (n + 1) * PX)
        both = score[:, rows].astype(F32) + score_got[:, rows].astype(F32)
        logits_ref[:, rows] = (both + bias_cls).astype(BF16)
    for copy in near:
        copy.wait()


def split_rows(rows, groups, each, own_a, send_a, own_b, send_b, send_d=None):
    me = lax.axis_index("dp")
    x_bit = me % 2
    y_bit = (me // 2) % 2

    def piece(group, y, x):
        return rows[pl.ds(pl.multiple_of(((group * 2 + y) * 2 + x) * each, each), each), :].astype(BF16)

    for group in range(groups):
        for bit in range(2):
            at = (bit * groups + group) * each
            own_a[at : at + each] = piece(group, bit, x_bit)
            send_a[at : at + each] = piece(group, bit, 1 - x_bit)
            own_b[at : at + each] = piece(group, y_bit, bit)
            send_b[at : at + each] = piece(group, 1 - y_bit, bit)
        if send_d is not None:
            send_d[group * each : (group + 1) * each] = piece(group, 1 - y_bit, 1 - x_bit)


def put_rows(out, index, own_ref, other_ref):
    chan = lax.axis_index("chan")
    size = own_ref.shape[0]
    width = own_ref.shape[1]
    for ref, which in ((own_ref, chan), (other_ref, 1 - chan)):
        into = pl.ds(pl.multiple_of(which * size, size), size)
        if index is None:
            out[into, :width] = ref[...]
        else:
            out[index, into, :width] = ref[...]


def cols_across(boxes_ref, canvas, at, box_count, own_ref, other_ref, lhs):
    chan = lax.axis_index("chan")
    size = own_ref.shape[0]
    span = slice(at * PX, (at + 1) * PX)
    gate = pixel_gates(boxes_ref, canvas, box_count, (8, PX), 1)
    for ref, which in ((own_ref, chan), (other_ref, 1 - chan)):
        into = pl.ds(pl.multiple_of(which * size, size), size)
        value = ref[:, span].astype(F32)
        lhs[0, into, span] = (pltpu.roll(value, PX - 1, 1) * gate(0, 1)[0:1]).astype(BF16)
        lhs[1, into, span] = ref[:, span]
        lhs[2, into, span] = (pltpu.roll(value, 1, 1) * gate(0, -1)[0:1]).astype(BF16)


def reversed_bits(number, bits):
    return sum(((number >> bit) & 1) << (bits - 1 - bit) for bit in range(bits))


def split_out(offsets, bit, acc, keep, send):
    parts, _, each, _ = keep.shape
    groups = parts // 2
    block = groups * each

    def one(d, carry):
        for half in range(2):
            for ref, which in ((keep, bit), (send, 1 - bit)):
                for group in range(groups):
                    at = (half * 2 + which) * block + group * each
                    ref[reversed_bits(half * groups + group, parts.bit_length() - 1), d] = acc[d, pl.ds(pl.multiple_of(at, each), each), :].astype(BF16)
        return carry

    lax.fori_loop(offsets[0], offsets[1], one, 0)


def tail_kernel(
    canv, box_count,
    total_dp, rows_all,
    boxes_ref, lanes_ref, cells_ref, pack0, sa, sb, sd, df0, y0, norm_ref, act_ref, ztotal_ref, zgain_ref, dw_ref,
    pooled_any, x_any, xm_any, ym_any, wfx_any, wfb_any, wbr_any,
    gx_ref, out_fx, out_fb, out_br, sums_ref, out_dw,
    dw_own, dw_other, dw_slots, dw_sum, dw_send, dw_recv, pack1, df1, ga0, ga1, gb0, gb1, gd0, gd1, y_all, zpack0, zpack1, zsa, zsb, zga0, zga1, zgb0, zgb1, dz0, dz1, da,
    part, slots, sum_send, sum_recv, core_send, core_recv, near_send, near_recv,
    lift, grads, xbuf, wbuf, xd, lhs, acc, pool_mate,
    fb_send, fb_recv, keep_a, send_a, recv_a, zrecv_a, keep_b, send_b, recv_b, zrecv_b,
    bkeep_a, bsend_a, brecv_a, bzrecv_a, bkeep_b, bsend_b, brecv_b, bzrecv_b,
    load_sem, store_sem, w_sem, fb_sem, mate_send, mate_recv, part_send, part_recv,
):
    me = lax.axis_index("dp")
    chan = lax.axis_index("chan")
    parts = fb_send.shape[0]
    pixels = df0.shape[0]
    half = df0.shape[1]
    span = xbuf.shape[2]
    group, place = me // PLANE, me % PLANE
    x_bit, y_bit = me % 2, (me // 2) % 2
    x_mate = me + 1 - 2 * x_bit
    y_mate = me + 2 - 4 * y_bit

    stages = parts.bit_length() - 1

    def group_bit(stage):
        return (group // 2**stage) % 2

    def group_mate(stage):
        return (group + 2**stage * (1 - 2 * group_bit(stage))) * PLANE + place

    d_mate = x_mate + y_mate - me
    expected = signal_all(total_dp, True)

    def load(source, slot, which):
        return pltpu.make_async_copy(source, xbuf.at[slot], load_sem.at[which])

    loads = [
        load(x_any.at[:, pl.ds(0, span)], 0, 0),
        load(xm_any, 1, 1),
        load(x_any.at[:, pl.ds(span, span)], 0, 2),
        load(ym_any, 1, 3),
    ]
    loads[0].start()
    loads[1].start()

    def tile_load(tile):
        width = wbuf.shape[1]
        return pltpu.make_async_copy(
            wfx_any.at[:, pl.ds(pl.multiple_of(tile * width, width), width), :],
            wbuf.at[pl.ds(pl.multiple_of(lax.rem(tile, 2) * 9, 9), 9)],
            w_sem.at[lax.rem(tile, 2)],
        )

    levels_at_once = wfb_any.shape[1]

    def fb_load(d):
        at = d % 4 * levels_at_once
        return pltpu.make_async_copy(wfb_any.at[d], wbuf.at[pl.ds(at, levels_at_once)], fb_sem.at[d % 4])

    for d in range(3):
        fb_load(d).start()

    def mate_copy(number, source, target, mate):
        return pltpu.make_async_remote_copy(
            src_ref=source, dst_ref=target, send_sem=mate_send.at[number], recv_sem=mate_recv.at[number],
            device_id=(mate, chan), device_id_type=MESH,
        )

    class Halving:
        def __init__(self, number, keep, recv, offsets):
            self.number, self.keep, self.recv, self.offsets = number, keep, recv, offsets
            self.copies = []

        def kept(self, stage):
            at = 0
            for bit in range(stage):
                at = at + group_bit(bit) * (parts >> (bit + 1))
            return at

        def send(self):
            stage = len(self.copies)
            count = parts >> (stage + 1)
            from_at = self.kept(stage) + (1 - group_bit(stage)) * count
            number = self.number * stages + stage
            some = pl.ds(self.offsets[0], self.offsets[1] - self.offsets[0])
            copy = pltpu.make_async_remote_copy(
                src_ref=self.keep.at[pl.ds(from_at, count), some],
                dst_ref=self.recv.at[pl.ds(parts - 2 * count, count), some],
                send_sem=part_send.at[number],
                recv_sem=part_recv.at[number],
                device_id=(group_mate(stage), chan),
                device_id_type=MESH,
            )
            copy.start()
            self.copies.append(copy)

        def receive(self):
            stage = len(self.copies)
            self.copies[-1].wait_recv()
            if stage == stages:
                return
            count = parts >> stage
            at = self.kept(stage)

            def add(d, carry):
                for part in range(count):
                    got = self.recv[parts - 2 * count + part, d].astype(F32)
                    self.keep[at + part, d] = (self.keep[at + part, d].astype(F32) + got).astype(BF16)
                return carry

            lax.fori_loop(*self.offsets, add, 0)
            self.send()

    def near_copy(number, source, target, mate):
        return pltpu.make_async_remote_copy(
            src_ref=source, dst_ref=target, send_sem=near_send.at[number], recv_sem=near_recv.at[number],
            device_id=(mate, chan), device_id_type=MESH,
        )

    def swap_copy(number, source, target):
        return core_copy(source, target, core_send.at[number], core_recv.at[number])

    pl.semaphore_wait(pltpu.get_barrier_semaphore(), expected)
    swaps = [swap_copy(0, pack0, pack1), swap_copy(1, df0, df1)]
    near = [near_copy(0, sa, ga0, x_mate), near_copy(1, sb, gb0, y_mate), near_copy(2, sd, gd0, d_mate)]
    y_near = [near_copy(5 + number, y0, y_all.at[number], mate) for number, mate in enumerate((x_mate, y_mate, d_mate))]
    for copy in swaps + near + y_near:
        copy.start()
    dw_parts = Exchange(total_dp, dw_ref, dw_slots, dw_send.at[0], dw_recv.at[0], True)
    dw_parts.start()

    def lift_of(n):
        def store(d, y, block):
            lift[y * CW : (y + 1) * CW, d * CELLS : (d + 1) * CELLS] = block

        gated_lifts(boxes_ref, n, box_count, lanes_ref, store)

    rows = canv * CELLS
    for n in range(canv):
        lift_of(n)
        for ref, which in ((pack0, chan), (pack1, 1 - chan)):
            if n == 0 and ref is pack1:
                swaps[0].wait_recv()
            found = dot(ref[:half, n * PX : (n + 1) * PX], lift[...]).astype(BF16)
            into = pl.ds(pl.multiple_of(which * half, half), half)
            for e in range(9):
                xd[e, into, n * CELLS : (n + 1) * CELLS] = found[:, e * CELLS : (e + 1) * CELLS]

    for d in range(9):
        fb_load(d).wait()
        if d + 3 < 9:
            fb_load(d + 3).start()
        for level in range(4):
            found = dot(wbuf[d % 4 * levels_at_once + level], xd[d, :, :rows])
            acc[level, :, :rows] = found if d == 0 else acc[level, :, :rows] + found
    tile_load(0).start()
    levels = jnp.concatenate([lanes_ref[4:5, :]] * canv, axis=1)
    dy = 0.0
    for level in range(4):
        dy = dy + jnp.where(levels == level, acc[level, :, :rows], 0.0)
    dy = pltranspose(dy)
    sig = jax.nn.sigmoid(act_ref[...])
    da[...] = dy * sig * (1.0 + act_ref[...] * (1.0 - sig))
    for level in range(4):
        gain = bias = 0.0
        for n in range(canv):
            at = slice(n * CELLS, (n + 1) * CELLS)
            mine = jnp.where(cells_ref[:, 4:5] == level, da[at], 0.0)
            gain = gain + jnp.sum(mine * norm_ref[at], 0, keepdims=True)
            bias = bias + jnp.sum(mine, 0, keepdims=True)
        part[0, level : level + 1, :] = gain
        part[0, 4 + level : 5 + level, :] = bias
    exchange = Exchange(total_dp, part.at[0], slots.at[0], sum_send.at[0], sum_recv.at[0])
    exchange.start()
    dw_sum[...] = dw_parts.finish()
    dw_sums = Exchange(total_dp, dw_sum, dw_own, dw_send.at[1], dw_recv.at[1])
    dw_sums.start()
    for number, (source, target) in enumerate(((ga0, ga1), (gb0, gb1), (gd0, gd1))):
        near[number].wait_recv()
        swaps.append(swap_copy(2 + number, source, target))
        swaps[-1].start()
    for number in range(2, 5):
        swaps[number].wait_recv()

    half_a, half_b = half, half + half // 2
    qa0, qa1 = pack0.at[half_a:half_b], pack1.at[half_a:half_b]
    qb0, qb1 = pack0.at[half_b : 2 * half], pack1.at[half_b : 2 * half]
    ye = gx_ref
    size = gd0.shape[0]
    cols = 2 * size
    for source, (own_ref, oth_ref, bit) in enumerate(((qa0, qa1, y_bit), (ga0, ga1, y_bit), (gb0, gb1, x_bit), (gd0, gd1, 0))):
        mine = pl.ds(pl.multiple_of(bit * size, size), size)
        put_rows(lhs.at[source // 2, source % 2 * cols : (source % 2 + 1) * cols], None, own_ref.at[mine], oth_ref.at[mine])

    def canvas(n, carry):
        lift_of(n)
        source = n // canv
        at = pl.ds(pl.multiple_of(lax.rem(source, 2) * cols, cols), cols)
        found = dot(lhs[source // 2, at, pl.ds(pl.multiple_of((n % canv) * PX, PX), PX)], lift[...]).astype(BF16)
        for d in range(9):
            grads[d, :, pl.ds(pl.multiple_of(n * CELLS, CELLS), CELLS)] = found[:, d * CELLS : (d + 1) * CELLS]
        return carry

    lax.fori_loop(0, PLANE * canv, canvas, 0)
    each = fb_send.shape[2]
    fb_ways = []
    expand(y0[...], cells_ref, ye, 0)
    for number, copy in enumerate(y_near):
        copy.wait_recv()
        expand(y_all[number], cells_ref, ye, (number + 1) * rows)
    for d in range(9):
        result = dot(grads[d], ye[...])
        for part in range(parts):
            fb_send[reversed_bits(part, stages), d] = result[part * each : (part + 1) * each].astype(BF16)
        if d % 3 == 2:
            fb_ways.append(Halving(8 + d // 3, fb_send, fb_recv, (d - 2, d + 1)))
            fb_ways[-1].send()

    sums = exchange.finish()
    sums_ref[...] = sums
    dw_sums.arrive()
    zflip = acc.at[4, :, 0:rows]
    for n in range(canv):
        at = slice(n * CELLS, (n + 1) * CELLS)
        dz = 0.0
        for level in range(4):
            _, rstd = branch_stat(ztotal_ref, level, rows_all[level])
            here = jnp.where(cells_ref[:, 4:5] == level, 1.0, 0.0)
            mean_gain = sums[level : level + 1, :] / rows_all[level]
            mean_bias = sums[4 + level : 5 + level, :] / rows_all[level]
            mine = zgain_ref[level : level + 1, :] * rstd * (da[at] - mean_bias - norm_ref[at] * mean_gain)
            dz = dz + here * mine
        dz0[at] = dz.astype(BF16)
        zflip[:, at] = pltranspose(dz)
    quarter = half // 2
    split_rows(zflip, half // (4 * each), each, zpack0.at[0:quarter], zsa, zpack0.at[quarter:half], zsb)
    swaps += [swap_copy(5, zpack0, zpack1), swap_copy(6, dz0, dz1)]
    dw_swap = swap_copy(9, dw_own, dw_other)
    dw_swap.start()
    near += [near_copy(3, zsa, zga0, x_mate), near_copy(4, zsb, zgb0, y_mate)]
    for copy in swaps[5:] + near[3:]:
        copy.start()

    mate_copies = []
    sides = (
        (0, ((0, qa0, qa1, 0), (1, ga0, ga1, 1)), y_bit, keep_a, send_a, recv_a, y_mate),
        (1, ((0, qb0, qb1, 0), (2, gb0, gb1, 1)), x_bit, keep_b, send_b, recv_b, x_mate),
    )
    for side, sources, bit, keep, send, recv, mate in sides:
        for number, (device, own_ref, oth_ref, slot) in enumerate(sources):
            loads[2 * side + slot].wait()
            for n in range(canv):
                rows_down(boxes_ref, device * canv + n, box_count, xbuf.at[slot, pl.ds(n * PX, PX)], xd, n, 2 * canv)
                xd[canv + n] = xbuf[slot, n * PX : (n + 1) * PX]
                cols_across(boxes_ref, device * canv + n, n, box_count, own_ref, oth_ref, lhs)
                if number:
                    select, count = members(
                        boxes_ref, device * canv + n, box_count, lambda row: cells_ref[:, row : row + 1], (CELLS, PX), 1
                    )
                    sums = dot(select.astype(BF16), xbuf[slot, n * PX : (n + 1) * PX])
                    pool_mate[side, n * CELLS : (n + 1) * CELLS] = (sums / count).astype(BF16)
            if side == 0:
                loads[2 + slot].start()
            for d in range(9):
                across = xd[d // 3 * canv : (d // 3 + 1) * canv].reshape(pixels, span)
                found = dot(lhs[d % 3], across)
                acc[d] = found if number == 0 else acc[d] + found
                if number and d % 3 == 2:
                    split_out((d - 2, d + 1), bit, acc, keep, send)
                    some = pl.ds(d - 2, 3)
                    mate_copies.append(mate_copy(len(mate_copies), send.at[:, some], recv.at[:, some], mate))
                    mate_copies[-1].start()
        fb_ways[side].receive()
        if side == 0:
            for number, (source, target) in enumerate(((zga0, zga1), (zgb0, zgb1))):
                near[3 + number].wait_recv()
                swaps.append(swap_copy(7 + number, source, target))
                swaps[-1].start()

    for side in range(2):
        source = pooled_any.at[:, pl.ds(side * span, span)]
        loads.append(pltpu.make_async_copy(source, xd.at[side, pl.ds(0, rows)], load_sem.at[4 + side]))
        loads[-1].start()
    for number in (5, 7, 8):
        swaps[number].wait_recv()
    za0, za1 = zpack0.at[0:quarter], zpack1.at[0:quarter]
    zb0, zb1 = zpack0.at[quarter:half], zpack1.at[quarter:half]
    sides = (
        (0, za0, za1, zga0, zga1, y_bit, bkeep_a, bsend_a, brecv_a, y_mate),
        (1, zb0, zb1, zgb0, zgb1, x_bit, bkeep_b, bsend_b, brecv_b, x_mate),
    )
    for side, own0, oth0, own1, oth1, bit, keep, send, recv, mate in sides:
        put_rows(lhs, 0, own0, oth0)
        put_rows(lhs, 1, own1, oth1)
        loads[4 + side].wait()
        for level in range(4):
            left = [jnp.where(levels == level, lhs[k, :, :rows].astype(F32), 0.0).astype(BF16) for k in range(2)]
            acc[level] = dot(left[0], xd[side, :rows]) + dot(left[1], pool_mate[side])
        split_out((0, 4), bit, acc, keep, send)
        mate_copies.append(mate_copy(len(mate_copies), send, recv, mate))
        mate_copies[-1].start()

    ways = {}

    def pass_on(number):
        mate_copies[number].wait_recv()
        if number < 6:
            keep, recv, target = (keep_a, recv_a, zrecv_a) if number < 3 else (keep_b, recv_b, zrecv_b)
            offsets = (number % 3 * 3, number % 3 * 3 + 3)
        else:
            keep, recv, target = (bkeep_a, brecv_a, bzrecv_a) if number == 6 else (bkeep_b, brecv_b, bzrecv_b)
            offsets = (0, 4)

        def add(d, carry):
            for part in range(parts):
                keep[part, d] = (keep[part, d].astype(F32) + recv[part, d].astype(F32)).astype(BF16)
            return carry

        lax.fori_loop(*offsets, add, 0)
        ways[number] = Halving(number, keep, target, offsets)
        ways[number].send()

    pass_on(0)
    fb_ways[2].receive()

    swaps[1].wait_recv()
    swaps[6].wait_recv()
    for n in range(canv):
        gate = pixel_gates(boxes_ref, n, box_count, (PX, CELLS), 0)
        at = slice(n * PX, (n + 1) * PX)
        for which, ref in ((chan, df0), (1 - chan, df1)):
            into = pl.ds(pl.multiple_of(which * half, half), half)
            df = ref[at].astype(F32)
            xd[canv + n, :, into] = ref[at]
            xd[n, :, into] = (wide(gate(0, 1), half // CELLS) * pltpu.roll(df, PX - 1, 0)).astype(BF16)
            xd[2 * canv + n, :, into] = (wide(gate(0, -1), half // CELLS) * pltpu.roll(df, 1, 0)).astype(BF16)

    width = wbuf.shape[1]
    tiles = wfx_any.shape[1] // width

    def tile(t, carry):
        tile_load(t).wait()

        @pl.when(t + 1 < tiles)
        def _():
            tile_load(t + 1).start()

        first = lax.rem(t, 2) * 9
        for n in range(canv):
            at = slice(n * PX, (n + 1) * PX)
            gate = pixel_gates(boxes_ref, n, box_count, (PX, CELLS), 0)
            total = None
            for dy in range(3):
                found = dot_nt(xd[n], wbuf[first + dy * 3])
                for dx in range(1, 3):
                    found = found + dot_nt(xd[dx * canv + n], wbuf[first + dy * 3 + dx])
                if dy != 1:
                    found = wide(gate(1 - dy, 0), width // CELLS) * pltpu.roll(found, ((dy - 1) * CW) % PX, 0)
                total = found if total is None else total + found
            gx_ref[at, pl.ds(pl.multiple_of(t * width, width), width)] = total.astype(BF16)
        return carry

    lax.fori_loop(0, 1, tile, 0)
    pass_on(1)
    lax.fori_loop(1, 2, tile, 0)
    pass_on(3)
    lax.fori_loop(2, 3, tile, 0)
    pass_on(2)
    pass_on(4)
    lax.fori_loop(3, tiles, tile, 0)

    wbr_load = pltpu.make_async_copy(wbr_any, wbuf.at[pl.ds(0, wbr_any.shape[0])], load_sem.at[6])
    wbr_load.start()
    wbr_load.wait()
    per_level = wbr_any.shape[0] // 4
    for level in range(4):
        for which, ref in ((chan, dz0), (1 - chan, dz1)):
            into = pl.ds(pl.multiple_of(which * half, half), half)
            for m in range(canv):
                at = slice(m * CELLS, (m + 1) * CELLS)
                mine = jnp.where(cells_ref[:, 4:5] == level, ref[at].astype(F32), 0.0)
                xd[level, at, into] = mine.astype(BF16)
    for side in range(2):
        total = 0.0
        for level in range(4):
            first = level * per_level + side * per_level // 2
            w = wbuf[first : first + per_level // 2].reshape(span, 2 * half)
            total = total + dot_nt(xd[level, :rows], w)
        for m in range(canv):
            _, _, high, across = by_box(boxes_ref, m, cells_ref[:, 0:1], box_count)
            r0, r1, c0, c1 = member_bounds(lambda row: cells_ref[:, row : row + 1], high, across)
            at = slice(m * CELLS, (m + 1) * CELLS)
            pool_mate[side, at] = (total[at] / ((r1 - r0) * (c1 - c0))).astype(BF16)
    for n in range(canv):
        at = slice(n * PX, (n + 1) * PX)
        select, _ = members(boxes_ref, n, box_count, lambda row: lanes_ref[row : row + 1, :], (PX, CELLS), 0)
        for side in range(2):
            into = slice(side * span, (side + 1) * span)
            pooled = dot(select.astype(BF16), pool_mate[side, n * CELLS : (n + 1) * CELLS])
            gx_ref[at, into] = (gx_ref[at, into].astype(F32) + pooled).astype(BF16)

    pass_on(5)
    ways[0].receive()
    ways[1].receive()
    ways[3].receive()
    pass_on(6)
    pass_on(7)
    for number in (2, 4, 5, 6, 7):
        ways[number].receive()
    in_order = fb_ways + [ways[number] for number in (0, 1, 3, 2, 4, 5, 6, 7)]
    for stage in range(2, stages):
        for way in in_order:
            way.receive()

    stores = []

    def finish(way, out, at, sides):
        way.receive()
        keep, recv = way.keep, way.recv
        width_of = keep.shape[3] // len(sides)

        def add(d, carry):
            total = keep[way.kept(stages), d].astype(F32) + recv[parts - 2, d].astype(F32)
            for spot in range(len(sides)):
                row = (at + spot) * each
                acc[d, row : row + each, :width_of] = total[:, spot * width_of : (spot + 1) * width_of]
            return carry

        lax.fori_loop(*way.offsets, add, 0)
        some = pl.ds(way.offsets[0], way.offsets[1] - way.offsets[0])
        for spot, side in enumerate(sides):
            source = acc.at[some, pl.ds((at + spot) * each, each), pl.ds(0, width_of)]
            target = out.at[some, side] if len(out.shape) == 4 else out.at[some, :, pl.ds(side * width_of, width_of)]
            stores.append(pltpu.make_async_copy(source, target, store_sem.at[len(stores)]))
            stores[-1].start()

    for way in fb_ways:
        finish(way, out_fb, 0, (0, 1, 2, 3))
    for number in (0, 1, 3, 2, 4, 5):
        finish(ways[number], out_fx, 4 + number // 3, (number // 3,))
    finish(ways[6], out_br, 6, (0,))
    finish(ways[7], out_br, 7, (1,))
    for copy in stores:
        copy.wait()
    dw_swap.wait()
    ncls = dw_sum.shape[1]
    for source, which in ((dw_own, chan), (dw_other, 1 - chan)):
        strip = source.shape[1]
        da[0:half] = jnp.zeros((half, half), F32)
        for device in range(total_dp):
            da[device * strip : (device + 1) * strip, :ncls] = source[device]
        into = pl.ds(pl.multiple_of(which * half, half), half)
        out_dw[:, into] = pltranspose(da[0:half])[:ncls]
    for copy in mate_copies + swaps + near + y_near + [copy for way in in_order for copy in way.copies]:
        copy.wait_send()


def launch(kernel, **rest):
    return pl.pallas_call(kernel, **rest)


def whole(shape):
    return pl.BlockSpec(shape, lambda i: (0,) * len(shape))


def shaped(shape, kind):
    return jax.ShapeDtypeStruct(shape, kind)


def per_device(features, boxes, w_branch, gain_branch, bias_branch, w_fx, w_fb, gain_join, bias_join, w_cls, b_cls, grad_logits):
    canv, box_count = boxes.shape[:2]
    pixels, cin = features.shape
    mid = gain_join.shape[0]
    half = mid // lax.axis_size("chan")
    bw = gain_branch.shape[1]
    br = w_branch.shape[2]
    ncls = w_cls.shape[1]
    dp = lax.axis_size("dp")
    parts = dp // PLANE
    each = mid // dp
    cols = parts * each
    rows = canv * CELLS
    chan = lax.axis_index("chan")
    me = lax.axis_index("dp")
    rows_all = [float(canv * dp * box_count * s * s) for s in BINS]
    lanes_np = cell_table(box_count)
    lanes = jnp.asarray(lanes_np)
    cells = jnp.asarray(np.concatenate([lanes_np.T, np.zeros((CELLS, CELLS - 8), np.float32)], 1))

    span = cin // 2
    tile = cin // 4
    stages = parts.bit_length() - 1
    quarter = half // 2
    bundle = quarter // 2

    def swap(array):
        return lax.ppermute(array, "chan", [(0, 1), (1, 0)])

    def sems(*counts):
        return [pltpu.SemaphoreType.DMA((count,)) for count in counts]

    flat = boxes.reshape(-1)
    box_tile = jnp.zeros((8 * CELLS,), jnp.int32).at[: flat.shape[0]].set(flat).reshape(8, CELLS)
    (
        pooled, y, z_norm, z_act, z_total, boxes_all, logits, df, pack, send_a, send_b, send_d, dw_cls, db_total, x_mate, y_mate,
    ) = launch(
        functools.partial(front_kernel, canv, box_count, dp, each, rows_all),
        in_specs=[SMEM_SPEC] + [VMEM_SPEC] * 10 + [ANY_SPEC] * 4,
        out_specs=[VMEM_SPEC] * 14 + [ANY_SPEC] * 2,
        out_shape=[
            shaped((rows, cin), BF16),
            shaped((rows, bw), BF16),
            shaped((rows, bw), F32),
            shaped((rows, bw), F32),
            shaped((8, bw), F32),
            shaped((PLANE, 8, CELLS), jnp.int32),
            shaped((ncls, pixels), BF16),
            shaped((pixels, half), BF16),
            shaped((2 * half, pixels), BF16),
            shaped((quarter, pixels), BF16),
            shaped((quarter, pixels), BF16),
            shaped((bundle, pixels), BF16),
            shaped((dp, half // dp, ncls), F32),
            shaped((8, half), F32),
            shaped((pixels, span), BF16),
            shaped((pixels, span), BF16),
        ],
        scratch_shapes=[
            pltpu.VMEM((canv, PX, cin), BF16),
            pltpu.VMEM((2 * canv, PX, cin), BF16),
            pltpu.VMEM((4, cin, br), BF16),
            pltpu.VMEM((3, 3, cin, mid), BF16),
            pltpu.VMEM((canv, PX, 9 * CELLS), BF16),
            pltpu.VMEM((canv, 9 * CELLS, mid), BF16),
            pltpu.VMEM((canv, PX, mid), F32),
            pltpu.VMEM((rows, 4 * bw), BF16),
            pltpu.VMEM((rows, br), F32),
            pltpu.VMEM((rows, bw), BF16),
            pltpu.VMEM((rows, bw), BF16),
            pltpu.VMEM((half, ncls), F32),
            pltpu.VMEM((pixels, half), BF16),
            pltpu.VMEM((pixels, half), BF16),
            pltpu.VMEM((pixels, half), F32),
            pltpu.VMEM((pixels, half), F32),
            pltpu.VMEM((ncls, pixels), BF16),
            pltpu.VMEM((ncls, pixels), BF16),
            pltpu.VMEM((half, PX), F32),
        ]
        + exchange_scratch(dp, half, 3)
        + sems(3, 3, 7, 7, canv + 7),
        compiler_params=pltpu.CompilerParams(vmem_limit_bytes=63 * 2**20, collective_id=1, has_side_effects=True),
        name="front",
    )(
        flat, box_tile, lanes, cells, gain_branch, bias_branch, gain_join.reshape(1, mid), bias_join.reshape(1, mid),
        w_cls.T, b_cls.reshape(1, ncls), grad_logits.T, features, w_branch, w_fx.reshape(3, 3, cin, mid),
        w_fb.reshape(3, 3, 4 * bw, mid),
    )
    flat_all = boxes_all.reshape(PLANE, -1)[:, : flat.shape[0]].reshape(-1)

    def buffers(count, width):
        return [
            pltpu.VMEM((parts, count, each, width), BF16),
            pltpu.VMEM((parts, count, each, width), BF16),
            pltpu.VMEM((parts, count, each, width), BF16),
            pltpu.VMEM((parts - 1, count, each, width), BF16),
        ]

    near_rows = [pltpu.VMEM((quarter, pixels), BF16)] * 4 + [pltpu.VMEM((bundle, pixels), BF16)] * 2
    near_rows.append(pltpu.VMEM((PLANE - 1, rows, bw), BF16))
    near_cells = [pltpu.VMEM((quarter, rows), BF16)] * 6
    grad_features, sum_fx, sum_fb, sum_br, da_total, grad_w_cls = launch(
        functools.partial(tail_kernel, canv, box_count, dp, rows_all),
        in_specs=[SMEM_SPEC] + [VMEM_SPEC] * 3 + [ANY_SPEC] * 3 + [VMEM_SPEC] * 6 + [ANY_SPEC] * 8,
        out_specs=[VMEM_SPEC] + [ANY_SPEC] * 3 + [VMEM_SPEC] * 2,
        out_shape=[
            shaped((pixels, cin), BF16),
            shaped((9, each, cin), F32),
            shaped((9, 4, each, bw), F32),
            shaped((4, each, cin), F32),
            shaped((8, bw), F32),
            shaped((ncls, mid), F32),
        ],
        scratch_shapes=[
            pltpu.VMEM((dp, half // dp, ncls), F32),
            pltpu.VMEM((dp, half // dp, ncls), F32),
            pltpu.VMEM((dp, half // dp, ncls), F32),
            pltpu.VMEM((half // dp, ncls), F32),
            pltpu.SemaphoreType.DMA((2, dp)),
            pltpu.SemaphoreType.DMA((2, dp)),
            pltpu.VMEM((2 * half, pixels), BF16),
            pltpu.VMEM((pixels, half), BF16),
        ]
        + near_rows
        + [pltpu.VMEM((bw, rows), BF16), pltpu.VMEM((bw, rows), BF16)]
        + near_cells
        + [pltpu.VMEM((rows, bw), BF16), pltpu.VMEM((rows, bw), BF16), pltpu.VMEM((rows, bw), F32)]
        + exchange_scratch(dp, bw, 1)
        + sems(10, 10, 8, 8)
        + [
            pltpu.VMEM((PX, 9 * CELLS), BF16),
            pltpu.VMEM((9, cols, PLANE * rows), BF16),
            pltpu.VMEM((2, pixels, span), BF16),
            pltpu.VMEM((18, tile, mid), BF16),
            pltpu.VMEM((3 * canv, PX, mid), BF16),
            pltpu.VMEM((3, half, pixels), BF16),
            pltpu.VMEM((9, half, span), F32),
            pltpu.VMEM((2, rows, span), BF16),
            pltpu.VMEM((parts, 9, each, 4 * bw), BF16),
            pltpu.VMEM((parts - 1, 9, each, 4 * bw), BF16),
        ]
        + buffers(9, span)
        + buffers(9, span)
        + buffers(4, span)
        + buffers(4, span)
        + sems(7, 20, 2, 4, 8, 8, 11 * stages, 11 * stages),
        compiler_params=pltpu.CompilerParams(vmem_limit_bytes=63 * 2**20, collective_id=4, has_side_effects=True),
        name="tail",
    )(
        flat_all, lanes, cells, pack, send_a, send_b, send_d, df, y, z_norm, z_act, z_total, gain_branch, dw_cls, pooled,
        features, x_mate, y_mate, w_fx, w_fb, w_branch.reshape(16, tile, br),
    )
    out_fx = jnp.transpose(sum_fx, (0, 2, 1))
    out_fb = jnp.transpose(sum_fb, (0, 1, 3, 2))
    out_br = jnp.transpose(sum_br, (0, 2, 1))

    small = db_total[:2]
    small_got = swap(small)
    small_all = jnp.concatenate([jnp.where(chan == 0, small, small_got), jnp.where(chan == 0, small_got, small)], 1)
    return (
        logits.T,
        grad_features,
        out_br,
        da_total[:4],
        da_total[4:],
        out_fx,
        out_fb,
        small_all[0],
        small_all[1],
        grad_w_cls.T,
        db_total[2, :ncls],
    )


def solution(mesh):
    return jax.shard_map(
        per_device,
        mesh=mesh,
        in_specs=(
            P("dp", "chan"),
            P("dp", None, None),
            P(None, "chan", None),
            P(None, "chan"),
            P(None, "chan"),
            P(None, "chan", None),
            P(None, None, "chan", None),
            P(),
            P(),
            P(),
            P(),
            P("dp", None),
        ),
        out_specs=(
            P("dp", None),
            P("dp", "chan"),
            P(None, "chan", "dp"),
            P(None, "chan"),
            P(None, "chan"),
            P(None, "chan", "dp"),
            P(None, None, "chan", "dp"),
            P(),
            P(),
            P(),
            P(),
        ),
        check_vma=False,
    )
```

```python
import functools

import jax
import jax.numpy as jnp
import numpy as np
from jax import lax
from jax.experimental import pallas as pl
from jax.experimental.pallas import tpu as pltpu
from jax.sharding import PartitionSpec as P

CH = 16
CW = 32
PX = CH * CW
EPS = 1e-05
BINS = (1, 2, 3, 6)
CELLS = 128
PLANE = 4
F32 = jnp.float32
BF16 = jnp.bfloat16
MESH = pl.DeviceIdType.MESH
VMEM_SPEC = pl.BlockSpec(memory_space=pltpu.VMEM)
SMEM_SPEC = pl.BlockSpec(memory_space=pltpu.SMEM)
ANY_SPEC = pl.BlockSpec(memory_space=pl.ANY)
NT = (((1,), (1,)), ((), ()))
TN = (((0,), (0,)), ((), ()))


def dot(a, b):
    return jnp.dot(a, b, preferred_element_type=F32)


def dot_nt(a, b):
    return lax.dot_general(a, b, NT, preferred_element_type=F32)


def dot_tt(a, b):
    return lax.dot_general(a, b, (((0,), (1,)), ((), ())), preferred_element_type=F32)


def dot_tn(a, b):
    return lax.dot_general(a, b, TN, preferred_element_type=F32)


def cell_table(box_count):
    table = np.zeros((8, CELLS), np.float32)
    table[1] = 1.0
    table[4] = 9.0
    at = 0
    for level, bins in enumerate(BINS):
        for box in range(box_count):
            for i in range(bins):
                for j in range(bins):
                    table[:6, at] = (box, bins, i, j, level, 1.0)
                    at += 1
    return table


def box_at(boxes_ref, canvas, box, box_count):
    base = (canvas * box_count + box) * 4
    return [boxes_ref[base + part] for part in range(4)]


def by_box(boxes_ref, canvas, which, box_count):
    sides = None
    for box in range(box_count):
        mine = [side.astype(F32) for side in box_at(boxes_ref, canvas, box, box_count)]
        if sides is None:
            sides = [jnp.full(which.shape, side, F32) for side in mine]
        else:
            sides = [jnp.where(which == box, new, old) for new, old in zip(mine, sides)]
    return sides


def within(relative, extent):
    return (relative >= 0) & (relative < extent)


def pixel_gates(boxes_ref, canvas, box_count, shape, axis):
    place = lax.broadcasted_iota(jnp.int32, shape, axis)
    row = place >> 5
    col = place & (CW - 1)
    rel = []
    for box in range(box_count):
        top, left, height, width = box_at(boxes_ref, canvas, box, box_count)
        rel.append((row - top, col - left, height, width))

    def gate(dy, dx):
        total = None
        for y, x, height, width in rel:
            hit = within(y, height) & within(x, width)
            if not isinstance(dy, int) or dy:
                hit = hit & within(y + dy, height)
            if not isinstance(dx, int) or dx:
                hit = hit & within(x + dx, width)
            value = jnp.where(hit, 1.0, 0.0)
            total = value if total is None else total + value
        return total

    return gate


def wide(column_block, times):
    return jnp.concatenate([column_block] * times, axis=1)


def rows_down(boxes_ref, canvas, box_count, x, xs, n, below):
    gate = pixel_gates(boxes_ref, canvas, box_count, (PX, CELLS), 0)
    reps = xs.shape[2] // CELLS
    blank = jnp.zeros((CW, xs.shape[2]), BF16)
    xs[n, 0:CW] = blank
    xs[n, CW:PX] = x[0 : PX - CW] * wide(gate(-1, 0).astype(BF16), reps)[CW:]
    xs[below + n, 0 : PX - CW] = x[CW:PX] * wide(gate(1, 0).astype(BF16), reps)[: PX - CW]
    xs[below + n, PX - CW : PX] = blank


def member_bounds(table_at, height, width):
    bins, i, j = table_at(1), table_at(2), table_at(3)

    def start(at, extent):
        return jnp.floor((at * extent + 0.5) / bins)

    def stop(at, extent):
        return jnp.floor(((at + 1) * extent + bins - 0.5) / bins)

    return start(i, height), stop(i, height), start(j, width), stop(j, width)


def members(boxes_ref, canvas, box_count, table_at, shape, axis):
    top, left, height, width = by_box(boxes_ref, canvas, table_at(0), box_count)
    r0, r1, c0, c1 = member_bounds(table_at, height, width)
    place = lax.broadcasted_iota(jnp.int32, shape, axis)
    row = (place >> 5).astype(F32) - top
    col = (place & (CW - 1)).astype(F32) - left
    hit = (row >= r0) & (row < r1) & (col >= c0) & (col < c1) & (table_at(5) > 0)
    return jnp.where(hit, 1.0, 0.0), (r1 - r0) * (c1 - c0)


def gated_lifts(boxes_ref, canvas, box_count, lanes_ref, store):
    def table_at(row):
        return lanes_ref[row : row + 1, :]

    top, left, height, width = by_box(boxes_ref, canvas, table_at(0), box_count)

    def side(size, edge, extent, cell):
        relative = lax.broadcasted_iota(jnp.int32, (size, CELLS), 0).astype(F32) - edge
        scale = (table_at(1) - 1.0) / (extent - 1.0)
        own = within(relative, extent)
        found = []
        for step in (-1, 0, 1):
            moved = relative + step
            weight = jnp.maximum(0.0, 1.0 - jnp.abs(moved * scale - cell))
            found.append(jnp.where(own & within(moved, extent), weight, 0.0))
        return found

    rows = [found * table_at(5) for found in side(CH, top, height, table_at(2))]
    cols = side(CW, left, width, table_at(3))
    for d in range(9):
        for y in range(CH):
            store(d, y, (rows[d // 3][y : y + 1] * cols[d % 3]).astype(BF16))


def pltranspose(block):
    return jnp.transpose(block, (1, 0))


def signal_all(total, chan_too=False):
    me = lax.axis_index("dp")
    chan = lax.axis_index("chan")
    barrier = pltpu.get_barrier_semaphore()

    def signal(step, carry):
        pl.semaphore_signal(barrier, inc=1, device_id=(lax.rem(me + step, total), chan), device_id_type=MESH)
        return carry

    lax.fori_loop(1, total, signal, 0)
    if chan_too:
        pl.semaphore_signal(barrier, inc=1, device_id=(me, 1 - chan), device_id_type=MESH)
    return total if chan_too else total - 1


class Exchange:
    def __init__(self, total, own, slots, send_sem, recv_sem, parted=False):
        self.total, self.own, self.slots, self.send_sem, self.recv_sem = total, own, slots, send_sem, recv_sem
        self.me = lax.axis_index("dp")
        self.parted = parted

    def block(self, device):
        return self.own.at[device] if self.parted else self.own

    def copy_to(self, step):
        return pltpu.make_async_remote_copy(
            src_ref=self.block(lax.rem(self.me + step, self.total)),
            dst_ref=self.slots.at[self.me],
            send_sem=self.send_sem.at[step],
            recv_sem=self.recv_sem.at[self.me],
            device_id=(lax.rem(self.me + step, self.total), lax.axis_index("chan")),
            device_id_type=MESH,
        )

    def copy_from(self, step):
        other = lax.rem(self.me + self.total - step, self.total)
        return pltpu.make_async_remote_copy(
            src_ref=self.block(other),
            dst_ref=self.slots.at[other],
            send_sem=self.send_sem.at[step],
            recv_sem=self.recv_sem.at[other],
            device_id=(other, lax.axis_index("chan")),
            device_id_type=MESH,
        )

    def start(self):
        if self.parted:
            keep = pltpu.make_async_copy(self.block(self.me), self.slots.at[self.me], self.recv_sem.at[self.me])
            keep.start()
            keep.wait()
        else:
            self.slots[self.me] = self.own[...]

        def one(step, carry):
            self.copy_to(step).start()
            return carry

        lax.fori_loop(1, self.total, one, 0)

    def arrive(self):
        def one(step, carry):
            self.copy_from(step).wait_recv()
            return carry

        def sent(step, carry):
            self.copy_to(step).wait_send()
            return carry

        lax.fori_loop(1, self.total, one, 0)
        lax.fori_loop(1, self.total, sent, 0)

    def finish(self):
        self.arrive()
        value = self.slots[0]
        for other in range(1, self.total):
            value = value + self.slots[other]
        return value


def exchange_scratch(total, width, times):
    return [
        pltpu.VMEM((times, 8, width), F32),
        pltpu.VMEM((times, total, 8, width), F32),
        pltpu.SemaphoreType.DMA((times, total)),
        pltpu.SemaphoreType.DMA((times, total)),
    ]


def core_copy(source, target, send_sem, recv_sem):
    return pltpu.make_async_remote_copy(
        src_ref=source,
        dst_ref=target,
        send_sem=send_sem,
        recv_sem=recv_sem,
        device_id=(lax.axis_index("dp"), 1 - lax.axis_index("chan")),
        device_id_type=MESH,
    )


def branch_stat(total_ref, level, rows_all):
    mean = total_ref[level : level + 1, :] / rows_all
    var = total_ref[4 + level : 5 + level, :] / rows_all - mean * mean
    return mean, lax.rsqrt(var + EPS)


def expand(y, cells_ref, keep, at):
    width = y.shape[1]
    for n in range(y.shape[0] // CELLS):
        rows = slice(n * CELLS, (n + 1) * CELLS)
        block = y[rows].astype(F32)
        for level in range(4):
            mine = jnp.where(cells_ref[:, 4:5] == level, block, 0.0)
            keep[at + n * CELLS : at + (n + 1) * CELLS, level * width : (level + 1) * width] = mine.astype(BF16)


def front_kernel(
    canv, box_count, total, each, rows_all,
    boxes_ref, box_ref, lanes_ref, cells_ref, zgain_ref, zbias_ref, gain_ref, bias_ref, w_ref, bcls_ref, g_ref,
    x_any, wbr_any, wfx_any, wfb_any,
    pooled_ref, y_ref, norm_ref, act_ref, ztotal_ref, boxes_all, logits_ref, df_ref, pack_ref, send_a, send_b, send_d,
    dw_ref, sums_ref, xm_any, ym_any,
    x, xs, wbr, wbuf, lifts, terms, fjoin, ye, zs, zsend, zgot, dw, fsend, got, f, db, score, score_got, flip,
    part, slots, send_sem, recv_sem, core_send, core_recv, near_send, near_recv, load_sem,
):
    me = lax.axis_index("dp")
    chan = lax.axis_index("chan")
    x_mate = me + 1 - 2 * (me % 2)
    y_mate = me + 2 - 4 * ((me // 2) % 2)
    span = xm_any.shape[1]
    half = df_ref.shape[1]
    mid = 2 * half
    ncls = g_ref.shape[0]
    own = pl.ds(pl.multiple_of(chan * half, half), half)
    away = pl.ds(pl.multiple_of((1 - chan) * half, half), half)
    expected = signal_all(total, True)
    loads = [pltpu.make_async_copy(x_any.at[pl.ds(n * PX, PX)], x.at[n], load_sem.at[n]) for n in range(canv)]
    loads.append(pltpu.make_async_copy(wbr_any, wbr, load_sem.at[canv]))
    loads += [pltpu.make_async_copy(wfx_any.at[:, t], wbuf.at[t], load_sem.at[canv + 1 + t]) for t in range(3)]
    for copy in loads:
        copy.start()

    def near_copy(number, source, target, mate):
        return pltpu.make_async_remote_copy(
            src_ref=source, dst_ref=target, send_sem=near_send.at[number], recv_sem=near_recv.at[number],
            device_id=(mate, chan), device_id_type=MESH,
        )

    def share(number, first, last):
        at = pl.ds(first * PX, (last - first) * PX)
        copies = [
            near_copy(number, x_any.at[at, pl.ds(0, span)], xm_any.at[at], x_mate),
            near_copy(number + 1, x_any.at[at, pl.ds(span, span)], ym_any.at[at], y_mate),
        ]
        for copy in copies:
            copy.start()
        return copies

    def table_at(row):
        return cells_ref[:, row : row + 1]

    part[...] = jnp.zeros_like(part)
    near = []
    for n in range(canv):
        loads[n].wait()
        select, count = members(boxes_ref, n, box_count, table_at, (CELLS, PX), 1)
        pooled_ref[n * CELLS : (n + 1) * CELLS] = (dot(select.astype(BF16), x[n]) / count).astype(BF16)
        if n == 0:
            pl.semaphore_wait(pltpu.get_barrier_semaphore(), expected)
            near += share(0, 0, 1)
            boxes_all[0] = box_ref[...]
            for number, mate in ((1, x_mate), (2, y_mate), (3, x_mate + y_mate - me)):
                near.append(near_copy(3 + number, box_ref, boxes_all.at[number], mate))
                near[-1].start()
    loads[canv].wait()
    for level in range(4):
        found = dot(pooled_ref[...], wbr[level])
        for n in range(canv):
            rows = slice(n * CELLS, (n + 1) * CELLS)
            mine = jnp.where(table_at(4) == level, found[rows], 0.0)
            zs[rows, :] = mine if level == 0 else zs[rows, :] + mine
    zsend[...] = zs[:, away].astype(BF16)
    swap_z = core_copy(zsend, zgot, core_send.at[0], core_recv.at[0])
    swap_z.start()
    for n in range(canv):
        rows_down(boxes_ref, n, box_count, x.at[n], xs, n, canv)

        def store(d, y, block, n=n):
            lifts[n, y * CW : (y + 1) * CW, d * CELLS : (d + 1) * CELLS] = block

        gated_lifts(boxes_ref, n, box_count, lanes_ref, store)
    swap_z.wait()
    bw = y_ref.shape[1]
    for n in range(canv):
        rows = slice(n * CELLS, (n + 1) * CELLS)
        z = zs[rows, own] + zgot[rows].astype(F32)
        norm_ref[rows] = z
        for level in range(4):
            mine = jnp.where(table_at(4) == level, z, 0.0)
            part[0, level : level + 1, :] += jnp.sum(mine, 0, keepdims=True)
            part[0, 4 + level : 5 + level, :] += jnp.sum(mine * mine, 0, keepdims=True)
    z_sums = Exchange(total, part.at[0], slots.at[0], send_sem.at[0], recv_sem.at[0])
    z_sums.start()

    def features_part(t):
        loads[canv + 1 + t].wait()
        for n in range(canv):
            q = dot(xs[n], wbuf[t, 0]) + dot(x[n], wbuf[t, 1]) + dot(xs[canv + n], wbuf[t, 2])
            gate = pixel_gates(boxes_ref, n, box_count, (PX, CELLS), 0)
            if t == 0:
                fjoin[n] = wide(gate(0, -1), mid // CELLS) * pltpu.roll(q, 1, 0)
            elif t == 1:
                fjoin[n] += wide(gate(0, 0), mid // CELLS) * q
            else:
                fjoin[n] += wide(gate(0, 1), mid // CELLS) * pltpu.roll(q, PX - 1, 0)
        loads.append(pltpu.make_async_copy(wfb_any.at[:, t], wbuf.at[t], load_sem.at[canv + 4 + t]))
        loads[-1].start()

    features_part(0)
    z_total = z_sums.finish()
    ztotal_ref[...] = z_total
    near += share(2, 1, canv)
    for n in range(canv):
        rows = slice(n * CELLS, (n + 1) * CELLS)
        z = norm_ref[rows]
        norm = act = 0.0
        for level in range(4):
            mean, rstd = branch_stat(ztotal_ref, level, rows_all[level])
            here = jnp.where(table_at(4) == level, 1.0, 0.0)
            mine = (z - mean) * rstd
            norm = norm + here * mine
            act = act + here * (zgain_ref[level : level + 1, :] * mine + zbias_ref[level : level + 1, :])
        norm_ref[rows] = norm
        act_ref[rows] = act
        value = act * jax.nn.sigmoid(act)
        y_ref[rows] = value.astype(BF16)
        for level in range(4):
            mine = jnp.where(table_at(4) == level, value, 0.0)
            ye[rows, level * bw : (level + 1) * bw] = mine.astype(BF16)
    features_part(1)
    features_part(2)

    for t in range(3):
        loads[canv + 4 + t].wait()
        for dy in range(3):
            term = dot(ye[...], wbuf[t, dy]).astype(BF16)
            at = (dy * 3 + t) * CELLS
            for n in range(canv):
                terms[n, at : at + CELLS] = term[n * CELLS : (n + 1) * CELLS]
    swap_f = []
    for n in range(canv):
        fjoin[n] += dot(lifts[n], terms[n])
        rows = pl.ds(n * PX, PX)
        fsend[rows] = fjoin[n, :, away].astype(BF16)
        swap_f.append(core_copy(fsend.at[rows], got.at[rows], core_send.at[2 + n], core_recv.at[2 + n]))
        swap_f[-1].start()
    dw[...] = jnp.zeros_like(dw)
    area = 0
    for n in range(canv):
        for box in range(box_count):
            side = box_at(boxes_ref, n, box, box_count)
            area = area + side[2] * side[3]
    part[1, 2:3, :] = jnp.full((1, half), area.astype(F32), F32)
    for n in range(canv):
        swap_f[n].wait()
        rows = slice(n * PX, (n + 1) * PX)
        value = fjoin[n, :, own] + got[rows].astype(F32)
        f[rows] = value
        part[1, 0:1, :] += jnp.sum(value, 0, keepdims=True)
        part[1, 1:2, :] += jnp.sum(value * value, 0, keepdims=True)
    first = Exchange(total, part.at[1], slots.at[1], send_sem.at[1], recv_sem.at[1])
    first.start()
    f_total = first.finish()
    count = f_total[2:3, :]
    mean = f_total[0:1, :] / count
    rstd = lax.rsqrt(f_total[1:2, :] / count - mean * mean + EPS)
    gain, bias, w = gain_ref[:, own], bias_ref[:, own], w_ref[:, own]
    ones = jnp.ones((8, PX), BF16)
    valid = [wide(pixel_gates(boxes_ref, n, box_count, (PX, CELLS), 0)(0, 0), half // CELLS) for n in range(canv)]
    for n in range(canv):
        rows = slice(n * PX, (n + 1) * PX)
        norm = (f[rows] - mean) * rstd
        f[rows] = norm
        act = gain * norm + bias
        sig = jax.nn.sigmoid(act)
        hidden = (act * sig * valid[n]).astype(BF16)
        g = g_ref[:, rows]
        score[:, rows] = dot_nt(w, hidden).astype(BF16)
        value = dot_tn(g, w) * valid[n] * sig * (1.0 + act * (1.0 - sig))
        db[rows] = value
        part[2, 0:1, :] += jnp.sum(value * norm, 0, keepdims=True)
        part[2, 1:2, :] += jnp.sum(value, 0, keepdims=True)
        part[2, 2:3, :ncls] += dot_nt(ones, g)[0:1]
        dw[...] += dot_tt(hidden, g)
    second = Exchange(total, part.at[2], slots.at[2], send_sem.at[2], recv_sem.at[2])
    second.start()
    swap_score = core_copy(score, score_got, core_send.at[1], core_recv.at[1])
    swap_score.start()
    sums = second.finish()
    sums_ref[...] = sums
    scale = gain * rstd
    for n in range(canv):
        rows = slice(n * PX, (n + 1) * PX)
        df = scale * (db[rows] - sums[1:2, :] / count - f[rows] * (sums[0:1, :] / count)) * valid[n]
        df_ref[rows] = df.astype(BF16)
        flip[...] = pltranspose(df)
        span = pl.ds(n * PX, PX)
        pack_ref[0:half, span] = flip[...].astype(BF16)
        views = [pack_ref.at[half : half + half // 2, span], send_a.at[:, span]]
        views += [pack_ref.at[half + half // 2 : 2 * half, span], send_b.at[:, span], send_d.at[:, span]]
        split_rows(flip, half // (4 * each), each, *views)
    strip = dw_ref.shape[1]
    for device in range(total):
        dw_ref[device] = dw[device * strip : (device + 1) * strip]
    swap_score.wait()
    square = (ncls, ncls)
    same = lax.broadcasted_iota(jnp.int32, square, 0) == lax.broadcasted_iota(jnp.int32, square, 1)
    bias_cls = jnp.sum(jnp.where(same, bcls_ref[...], 0.0), 1, keepdims=True)
    for n in range(canv):
        rows = slice(n * PX, (n + 1) * PX)
        both = score[:, rows].astype(F32) + score_got[:, rows].astype(F32)
        logits_ref[:, rows] = (both + bias_cls).astype(BF16)
    for copy in near:
        copy.wait()


def split_rows(rows, groups, each, own_a, send_a, own_b, send_b, send_d=None):
    me = lax.axis_index("dp")
    x_bit = me % 2
    y_bit = (me // 2) % 2

    def piece(group, y, x):
        return rows[pl.ds(pl.multiple_of(((group * 2 + y) * 2 + x) * each, each), each), :].astype(BF16)

    for group in range(groups):
        for bit in range(2):
            at = (bit * groups + group) * each
            own_a[at : at + each] = piece(group, bit, x_bit)
            send_a[at : at + each] = piece(group, bit, 1 - x_bit)
            own_b[at : at + each] = piece(group, y_bit, bit)
            send_b[at : at + each] = piece(group, 1 - y_bit, bit)
        if send_d is not None:
            send_d[group * each : (group + 1) * each] = piece(group, 1 - y_bit, 1 - x_bit)


def put_rows(out, index, own_ref, other_ref):
    chan = lax.axis_index("chan")
    size = own_ref.shape[0]
    width = own_ref.shape[1]
    for ref, which in ((own_ref, chan), (other_ref, 1 - chan)):
        into = pl.ds(pl.multiple_of(which * size, size), size)
        if index is None:
            out[into, :width] = ref[...]
        else:
            out[index, into, :width] = ref[...]


def cols_across(boxes_ref, canvas, at, box_count, own_ref, other_ref, lhs):
    chan = lax.axis_index("chan")
    size = own_ref.shape[0]
    span = slice(at * PX, (at + 1) * PX)
    gate = pixel_gates(boxes_ref, canvas, box_count, (8, PX), 1)
    for ref, which in ((own_ref, chan), (other_ref, 1 - chan)):
        into = pl.ds(pl.multiple_of(which * size, size), size)
        value = ref[:, span].astype(F32)
        lhs[0, into, span] = (pltpu.roll(value, PX - 1, 1) * gate(0, 1)[0:1]).astype(BF16)
        lhs[1, into, span] = ref[:, span]
        lhs[2, into, span] = (pltpu.roll(value, 1, 1) * gate(0, -1)[0:1]).astype(BF16)


def reversed_bits(number, bits):
    return sum(((number >> bit) & 1) << (bits - 1 - bit) for bit in range(bits))


def split_out(offsets, bit, acc, keep, send):
    parts, _, each, _ = keep.shape
    groups = parts // 2
    block = groups * each

    def one(d, carry):
        for half in range(2):
            for ref, which in ((keep, bit), (send, 1 - bit)):
                for group in range(groups):
                    at = (half * 2 + which) * block + group * each
                    ref[reversed_bits(half * groups + group, parts.bit_length() - 1), d] = acc[d, pl.ds(pl.multiple_of(at, each), each), :].astype(BF16)
        return carry

    lax.fori_loop(offsets[0], offsets[1], one, 0)


def tail_kernel(
    canv, box_count,
    total_dp, rows_all,
    boxes_ref, lanes_ref, cells_ref, pack0, sa, sb, sd, df0, y0, norm_ref, act_ref, ztotal_ref, zgain_ref, dw_ref,
    pooled_any, x_any, xm_any, ym_any, wfx_any, wfb_any, wbr_any,
    gx_ref, out_fx, out_fb, out_br, sums_ref, out_dw,
    dw_own, dw_other, dw_slots, dw_sum, dw_send, dw_recv, pack1, df1, ga0, ga1, gb0, gb1, gd0, gd1, y_all, zpack0, zpack1, zsa, zsb, zga0, zga1, zgb0, zgb1, dz0, dz1, da,
    part, slots, sum_send, sum_recv, core_send, core_recv, near_send, near_recv,
    lift, grads, xbuf, wbuf, xd, lhs, acc, pool_mate,
    fb_send, fb_recv, keep_a, send_a, recv_a, zrecv_a, keep_b, send_b, recv_b, zrecv_b,
    bkeep_a, bsend_a, brecv_a, bzrecv_a, bkeep_b, bsend_b, brecv_b, bzrecv_b,
    load_sem, store_sem, w_sem, fb_sem, mate_send, mate_recv, part_send, part_recv,
):
    me = lax.axis_index("dp")
    chan = lax.axis_index("chan")
    parts = fb_send.shape[0]
    pixels = df0.shape[0]
    half = df0.shape[1]
    span = xbuf.shape[2]
    group, place = me // PLANE, me % PLANE
    x_bit, y_bit = me % 2, (me // 2) % 2
    x_mate = me + 1 - 2 * x_bit
    y_mate = me + 2 - 4 * y_bit

    stages = parts.bit_length() - 1

    def group_bit(stage):
        return (group // 2**stage) % 2

    def group_mate(stage):
        return (group + 2**stage * (1 - 2 * group_bit(stage))) * PLANE + place

    d_mate = x_mate + y_mate - me
    expected = signal_all(total_dp, True)

    def load(source, slot, which):
        return pltpu.make_async_copy(source, xbuf.at[slot], load_sem.at[which])

    loads = [
        load(x_any.at[:, pl.ds(0, span)], 0, 0),
        load(xm_any, 1, 1),
        load(x_any.at[:, pl.ds(span, span)], 0, 2),
        load(ym_any, 1, 3),
    ]
    loads[0].start()
    loads[1].start()

    def tile_load(tile):
        width = wbuf.shape[1]
        return pltpu.make_async_copy(
            wfx_any.at[:, pl.ds(pl.multiple_of(tile * width, width), width), :],
            wbuf.at[pl.ds(pl.multiple_of(lax.rem(tile, 2) * 9, 9), 9)],
            w_sem.at[lax.rem(tile, 2)],
        )

    levels_at_once = wfb_any.shape[1]

    def fb_load(d):
        at = d % 4 * levels_at_once
        return pltpu.make_async_copy(wfb_any.at[d], wbuf.at[pl.ds(at, levels_at_once)], fb_sem.at[d % 4])

    for d in range(3):
        fb_load(d).start()

    def mate_copy(number, source, target, mate):
        return pltpu.make_async_remote_copy(
            src_ref=source, dst_ref=target, send_sem=mate_send.at[number], recv_sem=mate_recv.at[number],
            device_id=(mate, chan), device_id_type=MESH,
        )

    class Halving:
        def __init__(self, number, keep, recv, offsets):
            self.number, self.keep, self.recv, self.offsets = number, keep, recv, offsets
            self.copies = []

        def kept(self, stage):
            at = 0
            for bit in range(stage):
                at = at + group_bit(bit) * (parts >> (bit + 1))
            return at

        def send(self):
            stage = len(self.copies)
            count = parts >> (stage + 1)
            from_at = self.kept(stage) + (1 - group_bit(stage)) * count
            number = self.number * stages + stage
            some = pl.ds(self.offsets[0], self.offsets[1] - self.offsets[0])
            copy = pltpu.make_async_remote_copy(
                src_ref=self.keep.at[pl.ds(from_at, count), some],
                dst_ref=self.recv.at[pl.ds(parts - 2 * count, count), some],
                send_sem=part_send.at[number],
                recv_sem=part_recv.at[number],
                device_id=(group_mate(stage), chan),
                device_id_type=MESH,
            )
            copy.start()
            self.copies.append(copy)

        def receive(self):
            stage = len(self.copies)
            self.copies[-1].wait_recv()
            if stage == stages:
                return
            count = parts >> stage
            at = self.kept(stage)

            def add(d, carry):
                for part in range(count):
                    got = self.recv[parts - 2 * count + part, d].astype(F32)
                    self.keep[at + part, d] = (self.keep[at + part, d].astype(F32) + got).astype(BF16)
                return carry

            lax.fori_loop(*self.offsets, add, 0)
            self.send()

    def near_copy(number, source, target, mate):
        return pltpu.make_async_remote_copy(
            src_ref=source, dst_ref=target, send_sem=near_send.at[number], recv_sem=near_recv.at[number],
            device_id=(mate, chan), device_id_type=MESH,
        )

    def swap_copy(number, source, target):
        return core_copy(source, target, core_send.at[number], core_recv.at[number])

    pl.semaphore_wait(pltpu.get_barrier_semaphore(), expected)
    swaps = [swap_copy(0, pack0.at[0:half], pack1.at[0:half]), swap_copy(1, df0, df1)]
    pack_swap = swap_copy(10, pack0.at[half : 2 * half], pack1.at[half : 2 * half])
    near = [near_copy(0, sa, ga0, x_mate), near_copy(1, sb, gb0, y_mate), near_copy(2, sd, gd0, d_mate)]
    y_near = [near_copy(5 + number, y0, y_all.at[number], mate) for number, mate in enumerate((x_mate, y_mate, d_mate))]
    for copy in [swaps[0], pack_swap, swaps[1]] + near + y_near:
        copy.start()
    dw_parts = Exchange(total_dp, dw_ref, dw_slots, dw_send.at[0], dw_recv.at[0], True)
    dw_parts.start()

    def lift_of(n):
        def store(d, y, block):
            lift[y * CW : (y + 1) * CW, d * CELLS : (d + 1) * CELLS] = block

        gated_lifts(boxes_ref, n, box_count, lanes_ref, store)

    rows = canv * CELLS
    for n in range(canv):
        lift_of(n)
        for ref, which in ((pack0, chan), (pack1, 1 - chan)):
            if n == 0 and ref is pack1:
                swaps[0].wait_recv()
            found = dot(ref[:half, n * PX : (n + 1) * PX], lift[...]).astype(BF16)
            into = pl.ds(pl.multiple_of(which * half, half), half)
            for e in range(9):
                xd[e, into, n * CELLS : (n + 1) * CELLS] = found[:, e * CELLS : (e + 1) * CELLS]

    for d in range(9):
        fb_load(d).wait()
        if d + 3 < 9:
            fb_load(d + 3).start()
        for level in range(4):
            found = dot(wbuf[d % 4 * levels_at_once + level], xd[d, :, :rows])
            acc[level, :, :rows] = found if d == 0 else acc[level, :, :rows] + found
    tile_load(0).start()
    levels = jnp.concatenate([lanes_ref[4:5, :]] * canv, axis=1)
    dy = 0.0
    for level in range(4):
        dy = dy + jnp.where(levels == level, acc[level, :, :rows], 0.0)
    dy = pltranspose(dy)
    sig = jax.nn.sigmoid(act_ref[...])
    da[...] = dy * sig * (1.0 + act_ref[...] * (1.0 - sig))
    for level in range(4):
        gain = bias = 0.0
        for n in range(canv):
            at = slice(n * CELLS, (n + 1) * CELLS)
            mine = jnp.where(cells_ref[:, 4:5] == level, da[at], 0.0)
            gain = gain + jnp.sum(mine * norm_ref[at], 0, keepdims=True)
            bias = bias + jnp.sum(mine, 0, keepdims=True)
        part[0, level : level + 1, :] = gain
        part[0, 4 + level : 5 + level, :] = bias
    exchange = Exchange(total_dp, part.at[0], slots.at[0], sum_send.at[0], sum_recv.at[0])
    exchange.start()
    dw_sum[...] = dw_parts.finish()
    dw_sums = Exchange(total_dp, dw_sum, dw_own, dw_send.at[1], dw_recv.at[1])
    dw_sums.start()
    for number, (source, target) in enumerate(((ga0, ga1), (gb0, gb1), (gd0, gd1))):
        near[number].wait_recv()
        swaps.append(swap_copy(2 + number, source, target))
        swaps[-1].start()
    for number in range(2, 5):
        swaps[number].wait_recv()

    pack_swap.wait_recv()
    half_a, half_b = half, half + half // 2
    qa0, qa1 = pack0.at[half_a:half_b], pack1.at[half_a:half_b]
    qb0, qb1 = pack0.at[half_b : 2 * half], pack1.at[half_b : 2 * half]
    ye = gx_ref
    size = gd0.shape[0]
    cols = 2 * size
    for source, (own_ref, oth_ref, bit) in enumerate(((qa0, qa1, y_bit), (ga0, ga1, y_bit), (gb0, gb1, x_bit), (gd0, gd1, 0))):
        mine = pl.ds(pl.multiple_of(bit * size, size), size)
        put_rows(lhs.at[source // 2, source % 2 * cols : (source % 2 + 1) * cols], None, own_ref.at[mine], oth_ref.at[mine])

    def canvas(n, carry):
        lift_of(n)
        source = n // canv
        at = pl.ds(pl.multiple_of(lax.rem(source, 2) * cols, cols), cols)
        found = dot(lhs[source // 2, at, pl.ds(pl.multiple_of((n % canv) * PX, PX), PX)], lift[...]).astype(BF16)
        for d in range(9):
            grads[d, :, pl.ds(pl.multiple_of(n * CELLS, CELLS), CELLS)] = found[:, d * CELLS : (d + 1) * CELLS]
        return carry

    lax.fori_loop(0, PLANE * canv, canvas, 0)
    each = fb_send.shape[2]
    fb_ways = []
    expand(y0[...], cells_ref, ye, 0)
    for number, copy in enumerate(y_near):
        copy.wait_recv()
        expand(y_all[number], cells_ref, ye, (number + 1) * rows)
    for d in range(9):
        result = dot(grads[d], ye[...])
        for part in range(parts):
            fb_send[reversed_bits(part, stages), d] = result[part * each : (part + 1) * each].astype(BF16)
        if d % 3 == 2:
            fb_ways.append(Halving(8 + d // 3, fb_send, fb_recv, (d - 2, d + 1)))
            fb_ways[-1].send()

    sums = exchange.finish()
    sums_ref[...] = sums
    dw_sums.arrive()
    zflip = acc.at[4, :, 0:rows]
    for n in range(canv):
        at = slice(n * CELLS, (n + 1) * CELLS)
        dz = 0.0
        for level in range(4):
            _, rstd = branch_stat(ztotal_ref, level, rows_all[level])
            here = jnp.where(cells_ref[:, 4:5] == level, 1.0, 0.0)
            mean_gain = sums[level : level + 1, :] / rows_all[level]
            mean_bias = sums[4 + level : 5 + level, :] / rows_all[level]
            mine = zgain_ref[level : level + 1, :] * rstd * (da[at] - mean_bias - norm_ref[at] * mean_gain)
            dz = dz + here * mine
        dz0[at] = dz.astype(BF16)
        zflip[:, at] = pltranspose(dz)
    quarter = half // 2
    split_rows(zflip, half // (4 * each), each, zpack0.at[0:quarter], zsa, zpack0.at[quarter:half], zsb)
    swaps += [swap_copy(5, zpack0, zpack1), swap_copy(6, dz0, dz1)]
    dw_swap = swap_copy(9, dw_own, dw_other)
    dw_swap.start()
    near += [near_copy(3, zsa, zga0, x_mate), near_copy(4, zsb, zgb0, y_mate)]
    for copy in swaps[5:] + near[3:]:
        copy.start()

    mate_copies = []
    sides = (
        (0, ((0, qa0, qa1, 0), (1, ga0, ga1, 1)), y_bit, keep_a, send_a, recv_a, y_mate),
        (1, ((0, qb0, qb1, 0), (2, gb0, gb1, 1)), x_bit, keep_b, send_b, recv_b, x_mate),
    )
    for side, sources, bit, keep, send, recv, mate in sides:
        for number, (device, own_ref, oth_ref, slot) in enumerate(sources):
            loads[2 * side + slot].wait()
            for n in range(canv):
                rows_down(boxes_ref, device * canv + n, box_count, xbuf.at[slot, pl.ds(n * PX, PX)], xd, n, 2 * canv)
                xd[canv + n] = xbuf[slot, n * PX : (n + 1) * PX]
                cols_across(boxes_ref, device * canv + n, n, box_count, own_ref, oth_ref, lhs)
                if number:
                    select, count = members(
                        boxes_ref, device * canv + n, box_count, lambda row: cells_ref[:, row : row + 1], (CELLS, PX), 1
                    )
                    sums = dot(select.astype(BF16), xbuf[slot, n * PX : (n + 1) * PX])
                    pool_mate[side, n * CELLS : (n + 1) * CELLS] = (sums / count).astype(BF16)
            if side == 0:
                loads[2 + slot].start()
            for d in range(9):
                across = xd[d // 3 * canv : (d // 3 + 1) * canv].reshape(pixels, span)
                found = dot(lhs[d % 3], across)
                acc[d] = found if number == 0 else acc[d] + found
                if number and d % 3 == 2:
                    split_out((d - 2, d + 1), bit, acc, keep, send)
                    some = pl.ds(d - 2, 3)
                    mate_copies.append(mate_copy(len(mate_copies), send.at[:, some], recv.at[:, some], mate))
                    mate_copies[-1].start()
        fb_ways[side].receive()
        if side == 0:
            for number, (source, target) in enumerate(((zga0, zga1), (zgb0, zgb1))):
                near[3 + number].wait_recv()
                swaps.append(swap_copy(7 + number, source, target))
                swaps[-1].start()

    for side in range(2):
        source = pooled_any.at[:, pl.ds(side * span, span)]
        loads.append(pltpu.make_async_copy(source, xd.at[side, pl.ds(0, rows)], load_sem.at[4 + side]))
        loads[-1].start()
    for number in (5, 7, 8):
        swaps[number].wait_recv()
    za0, za1 = zpack0.at[0:quarter], zpack1.at[0:quarter]
    zb0, zb1 = zpack0.at[quarter:half], zpack1.at[quarter:half]
    sides = (
        (0, za0, za1, zga0, zga1, y_bit, bkeep_a, bsend_a, brecv_a, y_mate),
        (1, zb0, zb1, zgb0, zgb1, x_bit, bkeep_b, bsend_b, brecv_b, x_mate),
    )
    for side, own0, oth0, own1, oth1, bit, keep, send, recv, mate in sides:
        put_rows(lhs, 0, own0, oth0)
        put_rows(lhs, 1, own1, oth1)
        loads[4 + side].wait()
        for level in range(4):
            left = [jnp.where(levels == level, lhs[k, :, :rows].astype(F32), 0.0).astype(BF16) for k in range(2)]
            acc[level] = dot(left[0], xd[side, :rows]) + dot(left[1], pool_mate[side])
        split_out((0, 4), bit, acc, keep, send)
        mate_copies.append(mate_copy(len(mate_copies), send, recv, mate))
        mate_copies[-1].start()

    ways = {}

    def pass_on(number):
        mate_copies[number].wait_recv()
        if number < 6:
            keep, recv, target = (keep_a, recv_a, zrecv_a) if number < 3 else (keep_b, recv_b, zrecv_b)
            offsets = (number % 3 * 3, number % 3 * 3 + 3)
        else:
            keep, recv, target = (bkeep_a, brecv_a, bzrecv_a) if number == 6 else (bkeep_b, brecv_b, bzrecv_b)
            offsets = (0, 4)

        def add(d, carry):
            for part in range(parts):
                keep[part, d] = (keep[part, d].astype(F32) + recv[part, d].astype(F32)).astype(BF16)
            return carry

        lax.fori_loop(*offsets, add, 0)
        ways[number] = Halving(number, keep, target, offsets)
        ways[number].send()

    pass_on(0)
    fb_ways[2].receive()

    swaps[1].wait_recv()
    swaps[6].wait_recv()
    for n in range(canv):
        gate = pixel_gates(boxes_ref, n, box_count, (PX, CELLS), 0)
        at = slice(n * PX, (n + 1) * PX)
        for which, ref in ((chan, df0), (1 - chan, df1)):
            into = pl.ds(pl.multiple_of(which * half, half), half)
            df = ref[at].astype(F32)
            xd[canv + n, :, into] = ref[at]
            xd[n, :, into] = (wide(gate(0, 1), half // CELLS) * pltpu.roll(df, PX - 1, 0)).astype(BF16)
            xd[2 * canv + n, :, into] = (wide(gate(0, -1), half // CELLS) * pltpu.roll(df, 1, 0)).astype(BF16)

    width = wbuf.shape[1]
    tiles = wfx_any.shape[1] // width

    def tile(t, carry):
        tile_load(t).wait()

        @pl.when(t + 1 < tiles)
        def _():
            tile_load(t + 1).start()

        first = lax.rem(t, 2) * 9
        for n in range(canv):
            at = slice(n * PX, (n + 1) * PX)
            gate = pixel_gates(boxes_ref, n, box_count, (PX, CELLS), 0)
            total = None
            for dy in range(3):
                found = dot_nt(xd[n], wbuf[first + dy * 3])
                for dx in range(1, 3):
                    found = found + dot_nt(xd[dx * canv + n], wbuf[first + dy * 3 + dx])
                if dy != 1:
                    found = wide(gate(1 - dy, 0), width // CELLS) * pltpu.roll(found, ((dy - 1) * CW) % PX, 0)
                total = found if total is None else total + found
            gx_ref[at, pl.ds(pl.multiple_of(t * width, width), width)] = total.astype(BF16)
        return carry

    lax.fori_loop(0, 1, tile, 0)
    pass_on(1)
    lax.fori_loop(1, 2, tile, 0)
    pass_on(3)
    lax.fori_loop(2, 3, tile, 0)
    pass_on(2)
    pass_on(4)
    lax.fori_loop(3, tiles, tile, 0)

    wbr_load = pltpu.make_async_copy(wbr_any, wbuf.at[pl.ds(0, wbr_any.shape[0])], load_sem.at[6])
    wbr_load.start()
    wbr_load.wait()
    per_level = wbr_any.shape[0] // 4
    for level in range(4):
        for which, ref in ((chan, dz0), (1 - chan, dz1)):
            into = pl.ds(pl.multiple_of(which * half, half), half)
            for m in range(canv):
                at = slice(m * CELLS, (m + 1) * CELLS)
                mine = jnp.where(cells_ref[:, 4:5] == level, ref[at].astype(F32), 0.0)
                xd[level, at, into] = mine.astype(BF16)
    for side in range(2):
        total = 0.0
        for level in range(4):
            first = level * per_level + side * per_level // 2
            w = wbuf[first : first + per_level // 2].reshape(span, 2 * half)
            total = total + dot_nt(xd[level, :rows], w)
        for m in range(canv):
            _, _, high, across = by_box(boxes_ref, m, cells_ref[:, 0:1], box_count)
            r0, r1, c0, c1 = member_bounds(lambda row: cells_ref[:, row : row + 1], high, across)
            at = slice(m * CELLS, (m + 1) * CELLS)
            pool_mate[side, at] = (total[at] / ((r1 - r0) * (c1 - c0))).astype(BF16)
    for n in range(canv):
        at = slice(n * PX, (n + 1) * PX)
        select, _ = members(boxes_ref, n, box_count, lambda row: lanes_ref[row : row + 1, :], (PX, CELLS), 0)
        for side in range(2):
            into = slice(side * span, (side + 1) * span)
            pooled = dot(select.astype(BF16), pool_mate[side, n * CELLS : (n + 1) * CELLS])
            gx_ref[at, into] = (gx_ref[at, into].astype(F32) + pooled).astype(BF16)

    pass_on(5)
    ways[0].receive()
    ways[1].receive()
    ways[3].receive()
    pass_on(6)
    pass_on(7)
    for number in (2, 4, 5, 6, 7):
        ways[number].receive()
    in_order = fb_ways + [ways[number] for number in (0, 1, 3, 2, 4, 5, 6, 7)]
    for stage in range(2, stages):
        for way in in_order:
            way.receive()

    stores = []

    def finish(way, out, at, sides):
        way.receive()
        keep, recv = way.keep, way.recv
        width_of = keep.shape[3] // len(sides)

        def add(d, carry):
            total = keep[way.kept(stages), d].astype(F32) + recv[parts - 2, d].astype(F32)
            for spot in range(len(sides)):
                row = (at + spot) * each
                acc[d, row : row + each, :width_of] = total[:, spot * width_of : (spot + 1) * width_of]
            return carry

        lax.fori_loop(*way.offsets, add, 0)
        some = pl.ds(way.offsets[0], way.offsets[1] - way.offsets[0])
        for spot, side in enumerate(sides):
            source = acc.at[some, pl.ds((at + spot) * each, each), pl.ds(0, width_of)]
            target = out.at[some, side] if len(out.shape) == 4 else out.at[some, :, pl.ds(side * width_of, width_of)]
            stores.append(pltpu.make_async_copy(source, target, store_sem.at[len(stores)]))
            stores[-1].start()

    for way in fb_ways:
        finish(way, out_fb, 0, (0, 1, 2, 3))
    for number in (0, 1, 3, 2, 4, 5):
        finish(ways[number], out_fx, 4 + number // 3, (number // 3,))
    finish(ways[6], out_br, 6, (0,))
    finish(ways[7], out_br, 7, (1,))
    for copy in stores:
        copy.wait()
    dw_swap.wait()
    ncls = dw_sum.shape[1]
    for source, which in ((dw_own, chan), (dw_other, 1 - chan)):
        strip = source.shape[1]
        da[0:half] = jnp.zeros((half, half), F32)
        for device in range(total_dp):
            da[device * strip : (device + 1) * strip, :ncls] = source[device]
        into = pl.ds(pl.multiple_of(which * half, half), half)
        out_dw[:, into] = pltranspose(da[0:half])[:ncls]
    for copy in [pack_swap] + mate_copies + swaps + near + y_near + [copy for way in in_order for copy in way.copies]:
        copy.wait_send()


def launch(kernel, **rest):
    return pl.pallas_call(kernel, **rest)


def whole(shape):
    return pl.BlockSpec(shape, lambda i: (0,) * len(shape))


def shaped(shape, kind):
    return jax.ShapeDtypeStruct(shape, kind)


def per_device(features, boxes, w_branch, gain_branch, bias_branch, w_fx, w_fb, gain_join, bias_join, w_cls, b_cls, grad_logits):
    canv, box_count = boxes.shape[:2]
    pixels, cin = features.shape
    mid = gain_join.shape[0]
    half = mid // lax.axis_size("chan")
    bw = gain_branch.shape[1]
    br = w_branch.shape[2]
    ncls = w_cls.shape[1]
    dp = lax.axis_size("dp")
    parts = dp // PLANE
    each = mid // dp
    cols = parts * each
    rows = canv * CELLS
    chan = lax.axis_index("chan")
    me = lax.axis_index("dp")
    rows_all = [float(canv * dp * box_count * s * s) for s in BINS]
    lanes_np = cell_table(box_count)
    lanes = jnp.asarray(lanes_np)
    cells = jnp.asarray(np.concatenate([lanes_np.T, np.zeros((CELLS, CELLS - 8), np.float32)], 1))

    span = cin // 2
    tile = cin // 4
    stages = parts.bit_length() - 1
    quarter = half // 2
    bundle = quarter // 2

    def swap(array):
        return lax.ppermute(array, "chan", [(0, 1), (1, 0)])

    def sems(*counts):
        return [pltpu.SemaphoreType.DMA((count,)) for count in counts]

    flat = boxes.reshape(-1)
    box_tile = jnp.zeros((8 * CELLS,), jnp.int32).at[: flat.shape[0]].set(flat).reshape(8, CELLS)
    (
        pooled, y, z_norm, z_act, z_total, boxes_all, logits, df, pack, send_a, send_b, send_d, dw_cls, db_total, x_mate, y_mate,
    ) = launch(
        functools.partial(front_kernel, canv, box_count, dp, each, rows_all),
        in_specs=[SMEM_SPEC] + [VMEM_SPEC] * 10 + [ANY_SPEC] * 4,
        out_specs=[VMEM_SPEC] * 14 + [ANY_SPEC] * 2,
        out_shape=[
            shaped((rows, cin), BF16),
            shaped((rows, bw), BF16),
            shaped((rows, bw), F32),
            shaped((rows, bw), F32),
            shaped((8, bw), F32),
            shaped((PLANE, 8, CELLS), jnp.int32),
            shaped((ncls, pixels), BF16),
            shaped((pixels, half), BF16),
            shaped((2 * half, pixels), BF16),
            shaped((quarter, pixels), BF16),
            shaped((quarter, pixels), BF16),
            shaped((bundle, pixels), BF16),
            shaped((dp, half // dp, ncls), F32),
            shaped((8, half), F32),
            shaped((pixels, span), BF16),
            shaped((pixels, span), BF16),
        ],
        scratch_shapes=[
            pltpu.VMEM((canv, PX, cin), BF16),
            pltpu.VMEM((2 * canv, PX, cin), BF16),
            pltpu.VMEM((4, cin, br), BF16),
            pltpu.VMEM((3, 3, cin, mid), BF16),
            pltpu.VMEM((canv, PX, 9 * CELLS), BF16),
            pltpu.VMEM((canv, 9 * CELLS, mid), BF16),
            pltpu.VMEM((canv, PX, mid), F32),
            pltpu.VMEM((rows, 4 * bw), BF16),
            pltpu.VMEM((rows, br), F32),
            pltpu.VMEM((rows, bw), BF16),
            pltpu.VMEM((rows, bw), BF16),
            pltpu.VMEM((half, ncls), F32),
            pltpu.VMEM((pixels, half), BF16),
            pltpu.VMEM((pixels, half), BF16),
            pltpu.VMEM((pixels, half), F32),
            pltpu.VMEM((pixels, half), F32),
            pltpu.VMEM((ncls, pixels), BF16),
            pltpu.VMEM((ncls, pixels), BF16),
            pltpu.VMEM((half, PX), F32),
        ]
        + exchange_scratch(dp, half, 3)
        + sems(2 + canv, 2 + canv, 7, 7, canv + 7),
        compiler_params=pltpu.CompilerParams(vmem_limit_bytes=63 * 2**20, collective_id=1, has_side_effects=True),
        name="front",
    )(
        flat, box_tile, lanes, cells, gain_branch, bias_branch, gain_join.reshape(1, mid), bias_join.reshape(1, mid),
        w_cls.T, b_cls.reshape(1, ncls), grad_logits.T, features, w_branch, w_fx.reshape(3, 3, cin, mid),
        w_fb.reshape(3, 3, 4 * bw, mid),
    )
    flat_all = boxes_all.reshape(PLANE, -1)[:, : flat.shape[0]].reshape(-1)

    def buffers(count, width):
        return [
            pltpu.VMEM((parts, count, each, width), BF16),
            pltpu.VMEM((parts, count, each, width), BF16),
            pltpu.VMEM((parts, count, each, width), BF16),
            pltpu.VMEM((parts - 1, count, each, width), BF16),
        ]

    near_rows = [pltpu.VMEM((quarter, pixels), BF16)] * 4 + [pltpu.VMEM((bundle, pixels), BF16)] * 2
    near_rows.append(pltpu.VMEM((PLANE - 1, rows, bw), BF16))
    near_cells = [pltpu.VMEM((quarter, rows), BF16)] * 6
    grad_features, sum_fx, sum_fb, sum_br, da_total, grad_w_cls = launch(
        functools.partial(tail_kernel, canv, box_count, dp, rows_all),
        in_specs=[SMEM_SPEC] + [VMEM_SPEC] * 3 + [ANY_SPEC] * 3 + [VMEM_SPEC] * 6 + [ANY_SPEC] * 8,
        out_specs=[VMEM_SPEC] + [ANY_SPEC] * 3 + [VMEM_SPEC] * 2,
        out_shape=[
            shaped((pixels, cin), BF16),
            shaped((9, each, cin), F32),
            shaped((9, 4, each, bw), F32),
            shaped((4, each, cin), F32),
            shaped((8, bw), F32),
            shaped((ncls, mid), F32),
        ],
        scratch_shapes=[
            pltpu.VMEM((dp, half // dp, ncls), F32),
            pltpu.VMEM((dp, half // dp, ncls), F32),
            pltpu.VMEM((dp, half // dp, ncls), F32),
            pltpu.VMEM((half // dp, ncls), F32),
            pltpu.SemaphoreType.DMA((2, dp)),
            pltpu.SemaphoreType.DMA((2, dp)),
            pltpu.VMEM((2 * half, pixels), BF16),
            pltpu.VMEM((pixels, half), BF16),
        ]
        + near_rows
        + [pltpu.VMEM((bw, rows), BF16), pltpu.VMEM((bw, rows), BF16)]
        + near_cells
        + [pltpu.VMEM((rows, bw), BF16), pltpu.VMEM((rows, bw), BF16), pltpu.VMEM((rows, bw), F32)]
        + exchange_scratch(dp, bw, 1)
        + sems(11, 11, 8, 8)
        + [
            pltpu.VMEM((PX, 9 * CELLS), BF16),
            pltpu.VMEM((9, cols, PLANE * rows), BF16),
            pltpu.VMEM((2, pixels, span), BF16),
            pltpu.VMEM((18, tile, mid), BF16),
            pltpu.VMEM((3 * canv, PX, mid), BF16),
            pltpu.VMEM((3, half, pixels), BF16),
            pltpu.VMEM((9, half, span), F32),
            pltpu.VMEM((2, rows, span), BF16),
            pltpu.VMEM((parts, 9, each, 4 * bw), BF16),
            pltpu.VMEM((parts - 1, 9, each, 4 * bw), BF16),
        ]
        + buffers(9, span)
        + buffers(9, span)
        + buffers(4, span)
        + buffers(4, span)
        + sems(7, 20, 2, 4, 8, 8, 11 * stages, 11 * stages),
        compiler_params=pltpu.CompilerParams(vmem_limit_bytes=63 * 2**20, collective_id=4, has_side_effects=True),
        name="tail",
    )(
        flat_all, lanes, cells, pack, send_a, send_b, send_d, df, y, z_norm, z_act, z_total, gain_branch, dw_cls, pooled,
        features, x_mate, y_mate, w_fx, w_fb, w_branch.reshape(16, tile, br),
    )
    out_fx = jnp.transpose(sum_fx, (0, 2, 1))
    out_fb = jnp.transpose(sum_fb, (0, 1, 3, 2))
    out_br = jnp.transpose(sum_br, (0, 2, 1))

    small = db_total[:2]
    small_got = swap(small)
    small_all = jnp.concatenate([jnp.where(chan == 0, small, small_got), jnp.where(chan == 0, small_got, small)], 1)
    return (
        logits.T,
        grad_features,
        out_br,
        da_total[:4],
        da_total[4:],
        out_fx,
        out_fb,
        small_all[0],
        small_all[1],
        grad_w_cls.T,
        db_total[2, :ncls],
    )


def solution(mesh):
    return jax.shard_map(
        per_device,
        mesh=mesh,
        in_specs=(
            P("dp", "chan"),
            P("dp", None, None),
            P(None, "chan", None),
            P(None, "chan"),
            P(None, "chan"),
            P(None, "chan", None),
            P(None, None, "chan", None),
            P(),
            P(),
            P(),
            P(),
            P("dp", None),
        ),
        out_specs=(
            P("dp", None),
            P("dp", "chan"),
            P(None, "chan", "dp"),
            P(None, "chan"),
            P(None, "chan"),
            P(None, "chan", "dp"),
            P(None, None, "chan", "dp"),
            P(),
            P(),
            P(),
            P(),
        ),
        check_vma=False,
    )
```
